32 devices in a mesh: row: 4 (over y, core), col: 8 (over z, x).
Axes of the slice: x: 2, y: 2, z: 4, core: 2. Of those that a mesh axis runs over, the one named last changes fastest.
Arguments:
- velocity: float32 [3, 64, 32, 128], P(None, 'row', 'col'), may hold values from -6 to 6
- wall_counts: int32 [4], replicated, may hold values from 1 to 16, 32 in all
- x_first: float32 [128], replicated, may hold values from -0.5 to 0.5
- x_second: float32 [128], replicated, may hold values from -0.5 to 0.5
- y_first: float32 [32, 32], replicated, may hold values from -1 to 1
- y_second: float32 [32, 32], replicated, may hold values from -1 to 1
- z_first: float32 [32], replicated, may hold values from -1 to 1
- z_second: float32 [32], replicated, may hold values from -1 to 1
- metric_table: float32 [64], replicated, may hold values from 0.5 to 4
- metric_index: int32 [32], replicated, may hold values from 0 to 63
Outputs:
- tendency: float32 [3, 64, 32, 128], P(None, 'row', 'col')
The draws below stay inside these ranges and needn't reach their ends.
Inputs may be any that keep to these rules, and one draw needn't show every extreme that they name: Index r of row holds wall_counts[r] consecutive wall-normal planes, from the lower wall in order of r; they sum to 32. `metric_index`: entry of metric_table that scales the wall-normal derivative at each cell.
All inputs are finite; a program needn't handle non-finite values.
Results may differ from the reference program's by a relative error of at most 0.00012.
Values sent between devices are 32-bit elements; how exact they have to be, the bound alone decides.
No kernel may reach another device: no remote copies, remote signals or barrier semaphores. Data moves between devices by JAX's collectives and lax.ppermute only.
A program may use at most 64 MiB of HBM per device.

```python
import math
import jax
import jax.numpy as jnp
import numpy as np
from jax import lax

METRIC_LEVELS = 64
NX = 128
NY = 32
NZ = 32
SPLITS = 4
YMOST = 16


def place_ends(entries, rng, low, top_value):
    dims = entries.shape
    place = [jax.random.randint(jax.random.fold_in(rng, axis), (), 0, dims[axis]) for axis in range(len(dims))]
    entries = entries.at[tuple(place)].set(low)
    longest = dims.index(max(dims))
    place[longest] = (place[longest] + 1) % dims[longest]
    return entries.at[tuple(place)].set(top_value)


def shard_levels(rng, dims, pieces, least, largest):
    factor_of = 1.0
    for position, blocks in pieces:
        steps = jax.random.uniform(jax.random.fold_in(jax.random.fold_in(rng, 6), position), (blocks,), jnp.float32, least / len(pieces), largest / len(pieces))
        factor_of = factor_of * jnp.repeat(jnp.exp(steps), dims[position] // blocks).reshape((-1,) + (1,) * (len(dims) - 1 - position))
    return factor_of


def split_up(amount, total, bound, slope):
    loads = [(1 << 20) // math.isqrt(grade ** slope) + 1 for grade in range(2, amount + 1)]
    spare, given = total - bound - (amount - 1), [1] * (amount - 1)
    while spare > 0:
        candidates = [i for i in range(amount - 1) if given[i] < bound]
        pool, budget = sum([loads[i] for i in candidates]), spare
        for i in candidates:
            addition = min(bound - given[i], max(1, budget * loads[i] // pool), spare)
            given[i] = given[i] + addition
            spare = spare - addition
    return np.array([bound] + given)


def uneven(own_key, count, total, reach, slope):
    if count == 2:
        one = jax.random.randint(own_key, (), max(1, total - reach), min(reach, total - 1) + 1)
        return jnp.stack([one, total - one])
    tallies = jnp.asarray(split_up(count, total, reach, slope), jnp.int32)
    pairs = (count - 1) // 2
    source_of, receiver = tallies[1:1 + 2 * pairs:2], tallies[2:2 + 2 * pairs:2]
    slack = jnp.minimum(source_of - 1, reach - receiver)
    shifted = jax.random.randint(jax.random.fold_in(own_key, 1), (pairs,), 0, 1 << 20) % (slack + 1)
    tallies = tallies.at[1:1 + 2 * pairs:2].set(source_of - shifted).at[2:2 + 2 * pairs:2].set(receiver + shifted)
    return tallies[jax.random.permutation(jax.random.fold_in(own_key, 2), count)]


def bell_draw(rng, extent, deviation, most, split=(), kind=jnp.bfloat16):
    drawn = deviation * jax.random.normal(rng, extent, jnp.float32)
    if split:
        drawn = drawn * shard_levels(rng, extent, split, -0.22, 0.18)
    return jnp.clip(drawn, -most, most).astype(kind)


def setup_inputs(seed: int = 0) -> dict:
    key_list = jax.random.split(jax.random.key(seed), 11)
    return {
        "velocity": bell_draw(key_list[0], (3, SPLITS * YMOST, NZ, NX), 1.0, 6.0, ((1, 4), (2, 8)), jnp.float32),
        "wall_counts": uneven(key_list[1], SPLITS, NY, YMOST, 2).astype(jnp.int32),
        "x_first": bell_draw(key_list[2], (NX,), NX ** -0.5, 0.5, (), jnp.float32),
        "x_second": bell_draw(key_list[3], (NX,), NX ** -0.5, 0.5, (), jnp.float32),
        "y_first": bell_draw(key_list[4], (NY, NY), NY ** -0.5, 1.0, (), jnp.float32),
        "y_second": bell_draw(key_list[5], (NY, NY), NY ** -0.5, 1.0, (), jnp.float32),
        "z_first": bell_draw(key_list[6], (NZ,), NZ ** -0.5, 1.0, (), jnp.float32),
        "z_second": bell_draw(key_list[7], (NZ,), NZ ** -0.5, 1.0, (), jnp.float32),
        "metric_table": jnp.clip(jnp.exp(jax.random.uniform(key_list[8], (METRIC_LEVELS,), jnp.float32, math.log(0.5), math.log(4.0))), 0.5, 4.0),
        "metric_index": place_ends(jax.random.randint(key_list[9], (NY,), 0, METRIC_LEVELS), jax.random.fold_in(key_list[9], 1), 0, METRIC_LEVELS - 1).astype(jnp.int32),
    }


viscosity = 0.4
exact = lax.Precision.HIGHEST


def circulant(row):
    length = row.shape[0]
    index = (jnp.arange(length, dtype=jnp.int32)[:, None] - jnp.arange(length, dtype=jnp.int32)[None, :]) % length
    return row[index]


def reference(velocity, wall_counts, x_first, x_second, y_first, y_second, z_first, z_second, metric_table, metric_index):
    offsets = jnp.cumsum(wall_counts) - wall_counts
    cell = jnp.arange(NY, dtype=jnp.int32)
    owner = jnp.sum((cell[:, None] >= offsets[None, 1:]).astype(jnp.int32), axis=1).astype(jnp.int32)
    start = offsets[owner]
    plane = (owner * YMOST + cell - start).astype(jnp.int32)
    field = velocity[:, plane]
    metric = metric_table[metric_index]
    stream_first = circulant(x_first)
    stream_second = circulant(x_second)
    span_first = circulant(z_first)
    span_second = circulant(z_second)
    parts = []
    for comp in range(3):
        own = field[comp]
        x_term = viscosity * jnp.dot(own, stream_second, precision=exact) - jnp.dot(field[0] * own, stream_first, precision=exact)
        y_term = viscosity * jnp.einsum('jk,kzx->jzx', y_second, own, precision=exact) - metric[:, None, None] * jnp.einsum('jk,kzx->jzx', y_first, field[1] * own, precision=exact)
        z_term = viscosity * jnp.einsum('yzx,zw->ywx', own, span_second, precision=exact) - jnp.einsum('yzx,zw->ywx', field[2] * own, span_first, precision=exact)
        parts.append(x_term + y_term + z_term)
    live = jnp.stack(parts)
    result = jnp.zeros(velocity.shape, jnp.float32)
    return result.at[:, plane].set(live)
```

```python
import functools

import jax
import jax.numpy as jnp
from jax import lax
from jax.experimental import pallas as pl
from jax.experimental.pallas import tpu as pltpu
from jax.sharding import PartitionSpec as P

viscosity = 0.4
lanes = 128

VMEM = pltpu.VMEM
SMEM = pltpu.SMEM


def spec(space):
    return pl.BlockSpec(memory_space=space)


def halves(value):
    high = value.astype(jnp.bfloat16)
    low = (value - high.astype(jnp.float32)).astype(jnp.bfloat16)
    return high, low


def dot_split(left, right, transposed=False):
    dims = (((1,), (1 if transposed else 0,)), ((), ()))
    mul = functools.partial(lax.dot_general, dimension_numbers=dims, preferred_element_type=jnp.float32)
    lh, ll = halves(left)
    rh, rl = halves(right)
    return mul(lh, rh) + (mul(lh, rl) + mul(ll, rh))


def swap_blocks(parts, block):
    parts = list(parts)
    count = len(parts)
    lane = lax.broadcasted_iota(jnp.int32, parts[0].shape, 1) // block
    step = count // 2
    while step:
        low = (lane & step) == 0
        for i in range(count):
            if i & step:
                continue
            a, b = parts[i], parts[i | step]
            parts[i] = jnp.where(low, a, pltpu.roll(b, step * block, 1))
            parts[i | step] = jnp.where(low, pltpu.roll(a, lanes - step * block, 1), b)
        step //= 2
    return parts


def pack_kernel(cols, comps, field, *refs):
    outs, scratch = refs[:cols], refs[cols]
    block = field.shape[1] // cols
    per = lanes // block
    depth = field.shape[0] // comps
    rows = depth // per
    me = lax.axis_index("col")
    for tile in range(cols // per):
        for comp in range(comps):
            parts = [
                field[comp * depth + q * rows : comp * depth + (q + 1) * rows, tile * lanes : (tile + 1) * lanes]
                for q in range(per)
            ]
            for p, part in enumerate(swap_blocks(parts, block)):
                scratch[lax.rem(tile * per + p + cols - me, cols), comp * rows : (comp + 1) * rows] = part
    for s in range(cols):
        outs[s][...] = scratch[s]


def span_kernel(cols, comps, matrix, *refs):
    chunks, outs = refs[:cols], refs[cols:]
    rows = chunks[0].shape[0] // comps
    pick = lambda comp: jnp.concatenate(
        [chunks[(cols - s) % cols][comp * rows : (comp + 1) * rows] for s in range(cols)], axis=0
    )
    values = [pick(comp) for comp in range(comps)]
    right = jnp.concatenate(
        [jnp.concatenate([value, values[2] * value], axis=0) for value in values], axis=1
    )
    result = dot_split(matrix[...], right)
    for t in range(cols):
        for comp in range(comps):
            outs[t][comp * rows : (comp + 1) * rows] = result[
                t * rows : (t + 1) * rows, comp * lanes : (comp + 1) * lanes
            ]


def circulant_rows(row, length):
    return pltpu.roll(jnp.broadcast_to(row, (length, length)), 0, 1, stride=1, stride_axis=0)


def stream_kernel(
    rows,
    cols,
    comps,
    slots,
    zloc,
    wall_counts,
    z_first,
    z_second,
    metric_table,
    metric_index,
    field,
    x_first,
    x_second,
    y_first,
    y_second,
    x_part,
    z_matrix,
    y_matrix,
    scaled,
):
    depth = slots * zloc
    length = field.shape[1]
    cells_z = cols * zloc
    cells_y = y_first.shape[0]
    group = z_matrix.shape[0] // cols
    shape = z_matrix.shape
    half = shape[1] // 2
    r = lax.broadcasted_iota(jnp.int32, shape, 0)
    q = lax.broadcasted_iota(jnp.int32, shape, 1)
    second = q < half
    q = jnp.where(second, q, q - half)
    out_cell = (r // group) * zloc + r % zloc
    in_cell = (q // group) * zloc + q % zloc
    same = (r % group) // zloc == (q % group) // zloc
    gap = jnp.where(same, (in_cell - out_cell + cells_z) % cells_z, -1)
    line = lax.broadcasted_iota(jnp.int32, (1, shape[1]), 1) < half

    def fill(k, total):
        value = jnp.where(line, viscosity * z_second[k], -z_first[k])
        return jnp.where(gap == k, value, total)

    z_matrix[...] = lax.fori_loop(0, cells_z, fill, jnp.zeros(shape, jnp.float32), unroll=8)

    u = field[...]
    lead = u[:depth]
    left = jnp.concatenate(
        [u, jnp.concatenate([lead * u[c * depth : (c + 1) * depth] for c in range(comps)], axis=0)], axis=1
    )
    right = jnp.concatenate(
        [viscosity * circulant_rows(x_second[...], length), -circulant_rows(x_first[...], length)], axis=1
    )
    x_part[...] = dot_split(left, right, transposed=True)

    def scale(j, carry):
        scaled[pl.ds(j, 1), :] = y_first[pl.ds(j, 1), :] * -metric_table[metric_index[j]]
        return carry

    lax.fori_loop(0, cells_y, scale, 0, unroll=8)
    me = lax.axis_index("row")

    def start_of(index):
        return lax.fori_loop(0, rows, lambda i, acc: acc + jnp.where(i < index, wall_counts[i], 0), 0, unroll=True)

    own = lax.broadcasted_iota(jnp.int32, (depth, cells_y), 0) // zloc
    cell = lax.broadcasted_iota(jnp.int32, (depth, cells_y), 1)
    mine = ((own < wall_counts[me]) & (own + start_of(me) == cell)).astype(jnp.float32)
    exact = functools.partial(
        lax.dot_general, precision=lax.Precision.HIGHEST, preferred_element_type=jnp.float32
    )
    plain = (((1,), (0,)), ((), ()))
    turned = (((1,), (1,)), ((), ()))
    pair = [exact(mine, viscosity * y_second[...], plain), exact(mine, scaled[...], plain)]
    r = lax.broadcasted_iota(jnp.int32, (depth, depth), 0) % zloc
    q = lax.broadcasted_iota(jnp.int32, (depth, depth), 1) % zloc
    match = r == q
    for s in range(rows):
        other = lax.rem(me + rows - s, rows)
        theirs = ((own < wall_counts[other]) & (own + start_of(other) == cell)).astype(jnp.float32)
        for k in range(2):
            block = jnp.where(match, exact(pair[k], theirs, turned), 0.0)
            y_matrix[:, (2 * s + k) * depth : (2 * s + k + 1) * depth] = block


def wall_kernel(rows, comps, matrix, x_part, *refs):
    fields, out = refs[:rows], refs[rows]
    depth = x_part.shape[0] // comps
    pieces = []
    for comp in range(comps):
        stack = []
        for field in fields:
            value = field[comp * depth : (comp + 1) * depth]
            stack += [value, field[depth : 2 * depth] * value]
        pieces.append(jnp.concatenate(stack, axis=0))
    for comp in range(comps):
        out[comp * depth : (comp + 1) * depth] = x_part[comp * depth : (comp + 1) * depth] + dot_split(
            matrix[...], pieces[comp]
        )


def finish_kernel(cols, comps, zloc, wall_counts, total, *refs):
    chunks, out, scratch = refs[:cols], refs[cols], refs[cols + 1]
    block = out.shape[1] // cols
    per = lanes // block
    depth = out.shape[0] // comps
    rows = depth // per
    me = lax.axis_index("col")
    count = wall_counts[lax.axis_index("row")]
    for t in range(cols):
        scratch[lax.rem(me + cols - t, cols)] = chunks[t][...]
    for tile in range(cols // per):
        for comp in range(comps):
            parts = [scratch[tile * per + p, comp * rows : (comp + 1) * rows] for p in range(per)]
            for q, part in enumerate(swap_blocks(parts, block)):
                at = slice(comp * depth + q * rows, comp * depth + (q + 1) * rows)
                across = slice(tile * lanes, (tile + 1) * lanes)
                plane = (lax.broadcasted_iota(jnp.int32, part.shape, 0) + q * rows) // zloc
                out[at, across] = jnp.where(plane < count, total[at, across] + part, 0.0)


def local(
    velocity,
    wall_counts,
    x_first,
    x_second,
    y_first,
    y_second,
    z_first,
    z_second,
    metric_table,
    metric_index,
):
    rows = lax.axis_size("row")
    cols = lax.axis_size("col")
    comps, slots, zloc, length = velocity.shape
    depth = slots * zloc
    field = velocity.reshape(comps * depth, length)
    block = length // cols
    group = depth // (lanes // block)
    chunk = jax.ShapeDtypeStruct((comps * group, lanes), jnp.float32)
    scratch = pltpu.VMEM((cols,) + chunk.shape, jnp.float32)
    whole = jax.ShapeDtypeStruct(field.shape, jnp.float32)

    def shift(value, axis, size, step):
        return lax.ppermute(value, axis, [(i, (i + step) % size) for i in range(size)])

    chunks = pl.pallas_call(
        functools.partial(pack_kernel, cols, comps),
        out_shape=[chunk] * cols,
        in_specs=[spec(VMEM)],
        out_specs=[spec(VMEM)] * cols,
        scratch_shapes=[scratch],
        name="pack",
    )(field)
    received = [chunks[0]] + [shift(chunks[s], "col", cols, s) for s in range(1, cols)]
    fields = [field] + [shift(field, "row", rows, s) for s in range(1, rows)]
    x_part, z_matrix, y_matrix = pl.pallas_call(
        functools.partial(stream_kernel, rows, cols, comps, slots, zloc),
        out_shape=[
            whole,
            jax.ShapeDtypeStruct((cols * group, 2 * cols * group), jnp.float32),
            jax.ShapeDtypeStruct((depth, 2 * rows * depth), jnp.float32),
        ],
        in_specs=[spec(SMEM)] * 5 + [spec(VMEM)] * 5,
        out_specs=[spec(VMEM)] * 3,
        scratch_shapes=[pltpu.VMEM(y_first.shape, jnp.float32)],
        name="stream",
    )(
        wall_counts,
        z_first,
        z_second,
        metric_table,
        metric_index,
        field,
        x_first.reshape(1, length),
        x_second.reshape(1, length),
        y_first,
        y_second,
    )
    parts = pl.pallas_call(
        functools.partial(span_kernel, cols, comps),
        out_shape=[chunk] * cols,
        in_specs=[spec(VMEM)] * (cols + 1),
        out_specs=[spec(VMEM)] * cols,
        name="span",
    )(z_matrix, *received)
    returned = [parts[0]] + [shift(parts[t], "col", cols, t) for t in range(1, cols)]
    total = pl.pallas_call(
        functools.partial(wall_kernel, rows, comps),
        out_shape=whole,
        in_specs=[spec(VMEM)] * (rows + 2),
        out_specs=spec(VMEM),
        name="wall",
    )(y_matrix, x_part, *fields)
    result = pl.pallas_call(
        functools.partial(finish_kernel, cols, comps, zloc),
        out_shape=whole,
        in_specs=[spec(SMEM)] + [spec(VMEM)] * (cols + 1),
        out_specs=spec(VMEM),
        scratch_shapes=[scratch],
        name="finish",
    )(wall_counts, total, *returned)
    return result.reshape(velocity.shape)


def solution(mesh):
    in_specs = (P(None, "row", "col", None), P(), P(), P(), P(), P(), P(), P(), P(), P())
    out_specs = P(None, "row", "col", None)
    return jax.shard_map(local, mesh=mesh, in_specs=in_specs, out_specs=out_specs, check_vma=False)
```

```python
import functools

import jax
import jax.numpy as jnp
from jax import lax
from jax.experimental import pallas as pl
from jax.experimental.pallas import tpu as pltpu
from jax.sharding import PartitionSpec as P

viscosity = 0.4
lanes = 128

VMEM = pltpu.VMEM
SMEM = pltpu.SMEM


def spec(space):
    return pl.BlockSpec(memory_space=space)


def halves(value):
    high = value.astype(jnp.bfloat16)
    low = (value - high.astype(jnp.float32)).astype(jnp.bfloat16)
    return high, low


def dot_split(left, right, transposed=False):
    dims = (((1,), (1 if transposed else 0,)), ((), ()))
    mul = functools.partial(lax.dot_general, dimension_numbers=dims, preferred_element_type=jnp.float32)
    lh, ll = halves(left)
    rh, rl = halves(right)
    return mul(lh, rh) + (mul(lh, rl) + mul(ll, rh))


def circulant_rows(row, length):
    return pltpu.roll(jnp.broadcast_to(row, (length, length)), 0, 1, stride=1, stride_axis=0)


def stream_kernel(
    rows,
    cols,
    comps,
    slots,
    zloc,
    wall_counts,
    z_first,
    z_second,
    metric_table,
    metric_index,
    field,
    x_first,
    x_second,
    y_first,
    y_second,
    x_part,
    z_matrix,
    y_matrix,
    scaled,
):
    depth = slots * zloc
    length = field.shape[1]
    cells_z = cols * zloc
    cells_y = y_first.shape[0]
    group = z_matrix.shape[0]
    first_cell = lax.axis_index("col") * zloc
    shape = z_matrix.shape
    half = shape[1] // 2
    r = lax.broadcasted_iota(jnp.int32, shape, 0)
    q = lax.broadcasted_iota(jnp.int32, shape, 1)
    second = q < half
    q = jnp.where(second, q, q - half)
    out_cell = first_cell + r % zloc
    in_cell = (q // group) * zloc + q % zloc
    same = r // zloc == (q % group) // zloc
    gap = jnp.where(same, (in_cell - out_cell + cells_z) % cells_z, -1)
    line = lax.broadcasted_iota(jnp.int32, (1, shape[1]), 1) < half

    def fill(k, total):
        value = jnp.where(line, viscosity * z_second[k], -z_first[k])
        return jnp.where(gap == k, value, total)

    z_matrix[...] = lax.fori_loop(0, cells_z, fill, jnp.zeros(shape, jnp.float32), unroll=8)

    u = field[...]
    lead = u[:depth]
    left = jnp.concatenate(
        [u, jnp.concatenate([lead * u[c * depth : (c + 1) * depth] for c in range(comps)], axis=0)], axis=1
    )
    right = jnp.concatenate(
        [viscosity * circulant_rows(x_second[...], length), -circulant_rows(x_first[...], length)], axis=1
    )
    x_part[...] = dot_split(left, right, transposed=True)

    def scale(j, carry):
        scaled[pl.ds(j, 1), :] = y_first[pl.ds(j, 1), :] * -metric_table[metric_index[j]]
        return carry

    lax.fori_loop(0, cells_y, scale, 0, unroll=8)
    me = lax.axis_index("row")

    def start_of(index):
        return lax.fori_loop(0, rows, lambda i, acc: acc + jnp.where(i < index, wall_counts[i], 0), 0, unroll=True)

    own = lax.broadcasted_iota(jnp.int32, (depth, cells_y), 0) // zloc
    cell = lax.broadcasted_iota(jnp.int32, (depth, cells_y), 1)
    mine = ((own < wall_counts[me]) & (own + start_of(me) == cell)).astype(jnp.float32)
    exact = functools.partial(
        lax.dot_general, precision=lax.Precision.HIGHEST, preferred_element_type=jnp.float32
    )
    plain = (((1,), (0,)), ((), ()))
    turned = (((1,), (1,)), ((), ()))
    pair = [exact(mine, viscosity * y_second[...], plain), exact(mine, scaled[...], plain)]
    r = lax.broadcasted_iota(jnp.int32, (depth, depth), 0) % zloc
    q = lax.broadcasted_iota(jnp.int32, (depth, depth), 1) % zloc
    match = r == q
    for s in range(rows):
        theirs = ((own < wall_counts[s]) & (own + start_of(s) == cell)).astype(jnp.float32)
        for k in range(2):
            block = jnp.where(match, exact(pair[k], theirs, turned), 0.0)
            y_matrix[:, (2 * s + k) * depth : (2 * s + k + 1) * depth] = block


def join_kernel(comps, zloc, counts, z_matrix, y_matrix, x_part, row_fields, col_fields, out):
    rows, cols = row_fields.shape[0], col_fields.shape[0]
    depth = x_part.shape[0] // comps
    group = z_matrix.shape[0]
    count = counts[lax.axis_index("row")]
    length = x_part.shape[1]
    groups = depth // group
    for comp in range(comps):
        stack = []
        for r in range(rows):
            value = row_fields[r, comp * depth : (comp + 1) * depth]
            stack += [value, row_fields[r, depth : 2 * depth] * value]
        part = dot_split(y_matrix[...], jnp.concatenate(stack, axis=0))
        right = []
        for g in range(groups):
            at = comp * depth + g * group
            carry = (comps - 1) * depth + g * group
            value = jnp.concatenate([col_fields[p, at : at + group] for p in range(cols)], axis=0)
            lead = jnp.concatenate([col_fields[p, carry : carry + group] for p in range(cols)], axis=0)
            right.append(jnp.concatenate([value, lead * value], axis=0))
        wide = dot_split(z_matrix[...], jnp.concatenate(right, axis=1))
        span = jnp.concatenate([wide[:, g * length : (g + 1) * length] for g in range(groups)], axis=0)
        total = x_part[comp * depth : (comp + 1) * depth] + part + span
        plane = lax.broadcasted_iota(jnp.int32, total.shape, 0) // zloc
        out[comp * depth : (comp + 1) * depth] = jnp.where(plane < count, total, 0.0)


def local(
    velocity,
    wall_counts,
    x_first,
    x_second,
    y_first,
    y_second,
    z_first,
    z_second,
    metric_table,
    metric_index,
):
    rows = lax.axis_size("row")
    cols = lax.axis_size("col")
    comps, slots, zloc, length = velocity.shape
    depth = slots * zloc
    field = velocity.reshape(comps * depth, length)
    group = 8
    whole = jax.ShapeDtypeStruct(field.shape, jnp.float32)
    col_fields = lax.all_gather(field, "col")
    row_fields = lax.all_gather(field, "row")
    x_part, z_matrix, y_matrix = pl.pallas_call(
        functools.partial(stream_kernel, rows, cols, comps, slots, zloc),
        out_shape=[
            whole,
            jax.ShapeDtypeStruct((group, 2 * cols * group), jnp.float32),
            jax.ShapeDtypeStruct((depth, 2 * rows * depth), jnp.float32),
        ],
        in_specs=[spec(SMEM)] * 5 + [spec(VMEM)] * 5,
        out_specs=[spec(VMEM)] * 3,
        scratch_shapes=[pltpu.VMEM(y_first.shape, jnp.float32)],
        name="stream",
    )(
        wall_counts,
        z_first,
        z_second,
        metric_table,
        metric_index,
        field,
        x_first.reshape(1, length),
        x_second.reshape(1, length),
        y_first,
        y_second,
    )
    result = pl.pallas_call(
        functools.partial(join_kernel, comps, zloc),
        out_shape=whole,
        in_specs=[spec(SMEM)] + [spec(VMEM)] * 5,
        out_specs=spec(VMEM),
        name="join",
    )(wall_counts, z_matrix, y_matrix, x_part, row_fields, col_fields)
    return result.reshape(velocity.shape)


def solution(mesh):
    in_specs = (P(None, "row", "col", None), P(), P(), P(), P(), P(), P(), P(), P(), P())
    out_specs = P(None, "row", "col", None)
    return jax.shard_map(local, mesh=mesh, in_specs=in_specs, out_specs=out_specs, check_vma=False)
```

```python
import functools

import jax
import jax.numpy as jnp
from jax import lax
from jax.experimental import pallas as pl
from jax.experimental.pallas import tpu as pltpu
from jax.sharding import PartitionSpec as P

viscosity = 0.4
lanes = 128

VMEM = pltpu.VMEM
SMEM = pltpu.SMEM


def spec(space):
    return pl.BlockSpec(memory_space=space)


def halves(value):
    high = value.astype(jnp.bfloat16)
    low = (value - high.astype(jnp.float32)).astype(jnp.bfloat16)
    return high, low


def dot_split(left, right, transposed=False):
    dims = (((1,), (1 if transposed else 0,)), ((), ()))
    mul = functools.partial(lax.dot_general, dimension_numbers=dims, preferred_element_type=jnp.float32)
    lh, ll = halves(left)
    rh, rl = halves(right)
    return mul(lh, rh) + (mul(lh, rl) + mul(ll, rh))


def swap_blocks(parts, block):
    parts = list(parts)
    count = len(parts)
    lane = lax.broadcasted_iota(jnp.int32, parts[0].shape, 1) // block
    step = count // 2
    while step:
        low = (lane & step) == 0
        for i in range(count):
            if i & step:
                continue
            a, b = parts[i], parts[i | step]
            parts[i] = jnp.where(low, a, pltpu.roll(b, step * block, 1))
            parts[i | step] = jnp.where(low, pltpu.roll(a, lanes - step * block, 1), b)
        step //= 2
    return parts


def pack_kernel(comps, field, out):
    cols = out.shape[0]
    block = field.shape[1] // cols
    per = lanes // block
    depth = field.shape[0] // comps
    rows = depth // per
    for tile in range(cols // per):
        for comp in range(comps):
            parts = [
                field[comp * depth + q * rows : comp * depth + (q + 1) * rows, tile * lanes : (tile + 1) * lanes]
                for q in range(per)
            ]
            for p, part in enumerate(swap_blocks(parts, block)):
                out[tile * per + p, comp * rows : (comp + 1) * rows] = part


def span_kernel(comps, matrix, chunks, out):
    cols = out.shape[0]
    rows = out.shape[1] // comps
    values = [
        jnp.concatenate([chunks[p, comp * rows : (comp + 1) * rows] for p in range(cols)], axis=0)
        for comp in range(comps)
    ]
    right = jnp.concatenate(
        [jnp.concatenate([value, values[2] * value], axis=0) for value in values], axis=1
    )
    result = dot_split(matrix[...], right)
    for p in range(cols):
        for comp in range(comps):
            out[p, comp * rows : (comp + 1) * rows] = result[
                p * rows : (p + 1) * rows, comp * lanes : (comp + 1) * lanes
            ]


def circulant_rows(row, length):
    return pltpu.roll(jnp.broadcast_to(row, (length, length)), 0, 1, stride=1, stride_axis=0)


def stream_kernel(
    rows,
    cols,
    comps,
    slots,
    zloc,
    wall_counts,
    z_first,
    z_second,
    metric_table,
    metric_index,
    field,
    x_first,
    x_second,
    y_first,
    y_second,
    x_part,
    z_matrix,
    y_matrix,
    scaled,
):
    depth = slots * zloc
    length = field.shape[1]
    cells_z = cols * zloc
    cells_y = y_first.shape[0]
    group = z_matrix.shape[0] // cols
    shape = z_matrix.shape
    half = shape[1] // 2
    r = lax.broadcasted_iota(jnp.int32, shape, 0)
    q = lax.broadcasted_iota(jnp.int32, shape, 1)
    second = q < half
    q = jnp.where(second, q, q - half)
    out_cell = (r // group) * zloc + r % zloc
    in_cell = (q // group) * zloc + q % zloc
    same = (r % group) // zloc == (q % group) // zloc
    gap = jnp.where(same, (in_cell - out_cell + cells_z) % cells_z, -1)
    line = lax.broadcasted_iota(jnp.int32, (1, shape[1]), 1) < half

    def fill(k, total):
        value = jnp.where(line, viscosity * z_second[k], -z_first[k])
        return jnp.where(gap == k, value, total)

    z_matrix[...] = lax.fori_loop(0, cells_z, fill, jnp.zeros(shape, jnp.float32), unroll=8)

    u = field[...]
    lead = u[:depth]
    left = jnp.concatenate(
        [u, jnp.concatenate([lead * u[c * depth : (c + 1) * depth] for c in range(comps)], axis=0)], axis=1
    )
    right = jnp.concatenate(
        [viscosity * circulant_rows(x_second[...], length), -circulant_rows(x_first[...], length)], axis=1
    )
    x_part[...] = dot_split(left, right, transposed=True)

    def scale(j, carry):
        scaled[pl.ds(j, 1), :] = y_first[pl.ds(j, 1), :] * -metric_table[metric_index[j]]
        return carry

    lax.fori_loop(0, cells_y, scale, 0, unroll=8)
    me = lax.axis_index("row")

    def start_of(index):
        return lax.fori_loop(0, rows, lambda i, acc: acc + jnp.where(i < index, wall_counts[i], 0), 0, unroll=True)

    own = lax.broadcasted_iota(jnp.int32, (depth, cells_y), 0) // zloc
    cell = lax.broadcasted_iota(jnp.int32, (depth, cells_y), 1)
    mine = ((own < wall_counts[me]) & (own + start_of(me) == cell)).astype(jnp.float32)
    exact = functools.partial(
        lax.dot_general, precision=lax.Precision.HIGHEST, preferred_element_type=jnp.float32
    )
    plain = (((1,), (0,)), ((), ()))
    turned = (((1,), (1,)), ((), ()))
    pair = [exact(mine, viscosity * y_second[...], plain), exact(mine, scaled[...], plain)]
    r = lax.broadcasted_iota(jnp.int32, (depth, depth), 0) % zloc
    q = lax.broadcasted_iota(jnp.int32, (depth, depth), 1) % zloc
    match = r == q
    for s in range(rows):
        other = me ^ s
        theirs = ((own < wall_counts[other]) & (own + start_of(other) == cell)).astype(jnp.float32)
        for k in range(2):
            block = jnp.where(match, exact(pair[k], theirs, turned), 0.0)
            y_matrix[:, (2 * s + k) * depth : (2 * s + k + 1) * depth] = block


def wall_kernel(rows, comps, matrix, x_part, *refs):
    fields, out = refs[:rows], refs[rows]
    depth = x_part.shape[0] // comps
    pieces = []
    for comp in range(comps):
        stack = []
        for field in fields:
            value = field[comp * depth : (comp + 1) * depth]
            stack += [value, field[depth : 2 * depth] * value]
        pieces.append(jnp.concatenate(stack, axis=0))
    for comp in range(comps):
        out[comp * depth : (comp + 1) * depth] = x_part[comp * depth : (comp + 1) * depth] + dot_split(
            matrix[...], pieces[comp]
        )


def finish_kernel(comps, zloc, wall_counts, total, chunks, out):
    cols = chunks.shape[0]
    block = out.shape[1] // cols
    per = lanes // block
    depth = out.shape[0] // comps
    rows = depth // per
    count = wall_counts[lax.axis_index("row")]
    for tile in range(cols // per):
        for comp in range(comps):
            parts = [chunks[tile * per + p, comp * rows : (comp + 1) * rows] for p in range(per)]
            for q, part in enumerate(swap_blocks(parts, block)):
                at = slice(comp * depth + q * rows, comp * depth + (q + 1) * rows)
                across = slice(tile * lanes, (tile + 1) * lanes)
                plane = (lax.broadcasted_iota(jnp.int32, part.shape, 0) + q * rows) // zloc
                out[at, across] = jnp.where(plane < count, total[at, across] + part, 0.0)


def local(
    velocity,
    wall_counts,
    x_first,
    x_second,
    y_first,
    y_second,
    z_first,
    z_second,
    metric_table,
    metric_index,
):
    rows = lax.axis_size("row")
    cols = lax.axis_size("col")
    comps, slots, zloc, length = velocity.shape
    depth = slots * zloc
    field = velocity.reshape(comps * depth, length)
    block = length // cols
    group = depth // (lanes // block)
    chunks = jax.ShapeDtypeStruct((cols, comps * group, lanes), jnp.float32)
    whole = jax.ShapeDtypeStruct(field.shape, jnp.float32)

    def swap(value, step):
        return lax.ppermute(value, "row", [(i, i ^ step) for i in range(rows)])

    def turn(value):
        return lax.all_to_all(value, "col", split_axis=0, concat_axis=0, tiled=True)

    packed = pl.pallas_call(
        functools.partial(pack_kernel, comps),
        out_shape=chunks,
        in_specs=[spec(VMEM)],
        out_specs=spec(VMEM),
        name="pack",
    )(field)
    received = turn(packed)
    fields = [field] + [swap(field, s) for s in range(1, rows)]
    x_part, z_matrix, y_matrix = pl.pallas_call(
        functools.partial(stream_kernel, rows, cols, comps, slots, zloc),
        out_shape=[
            whole,
            jax.ShapeDtypeStruct((cols * group, 2 * cols * group), jnp.float32),
            jax.ShapeDtypeStruct((depth, 2 * rows * depth), jnp.float32),
        ],
        in_specs=[spec(SMEM)] * 5 + [spec(VMEM)] * 5,
        out_specs=[spec(VMEM)] * 3,
        scratch_shapes=[pltpu.VMEM(y_first.shape, jnp.float32)],
        name="stream",
    )(
        wall_counts,
        z_first,
        z_second,
        metric_table,
        metric_index,
        field,
        x_first.reshape(1, length),
        x_second.reshape(1, length),
        y_first,
        y_second,
    )
    parts = pl.pallas_call(
        functools.partial(span_kernel, comps),
        out_shape=chunks,
        in_specs=[spec(VMEM)] * 2,
        out_specs=spec(VMEM),
        name="span",
    )(z_matrix, received)
    returned = turn(parts)
    total = pl.pallas_call(
        functools.partial(wall_kernel, rows, comps),
        out_shape=whole,
        in_specs=[spec(VMEM)] * (rows + 2),
        out_specs=spec(VMEM),
        name="wall",
    )(y_matrix, x_part, *fields)
    result = pl.pallas_call(
        functools.partial(finish_kernel, comps, zloc),
        out_shape=whole,
        in_specs=[spec(SMEM)] + [spec(VMEM)] * 2,
        out_specs=spec(VMEM),
        name="finish",
    )(wall_counts, total, returned)
    return result.reshape(velocity.shape)


def solution(mesh):
    in_specs = (P(None, "row", "col", None), P(), P(), P(), P(), P(), P(), P(), P(), P())
    out_specs = P(None, "row", "col", None)
    return jax.shard_map(local, mesh=mesh, in_specs=in_specs, out_specs=out_specs, check_vma=False)
```

```python
import functools
import math

import jax
import jax.numpy as jnp
from jax import lax
from jax.experimental import pallas as pl
from jax.experimental.pallas import tpu as pltpu
from jax.sharding import PartitionSpec as P

viscosity = 0.4
lanes = 128

VMEM = pltpu.VMEM
SMEM = pltpu.SMEM


def halves(value):
    high = value.astype(jnp.bfloat16)
    low = (value - high.astype(jnp.float32)).astype(jnp.bfloat16)
    return high, low


def dot_split(left, right, transposed=False):
    dims = (((1,), (1 if transposed else 0,)), ((), ()))
    mul = functools.partial(lax.dot_general, dimension_numbers=dims, preferred_element_type=jnp.float32)
    lh, ll = halves(left)
    rh, rl = halves(right)
    return mul(lh, rh) + (mul(lh, rl) + mul(ll, rh))


def swap_blocks(parts, block):
    parts = list(parts)
    count = len(parts)
    lane = lax.broadcasted_iota(jnp.int32, parts[0].shape, 1) // block
    step = count // 2
    while step:
        low = (lane & step) == 0
        for i in range(count):
            if i & step:
                continue
            a, b = parts[i], parts[i | step]
            parts[i] = jnp.where(low, a, pltpu.roll(b, step * block, 1))
            parts[i | step] = jnp.where(low, pltpu.roll(a, lanes - step * block, 1), b)
        step //= 2
    return parts


def pack_kernel(comps, field, out):
    cols = out.shape[0]
    block = field.shape[1] // cols
    per = lanes // block
    depth = field.shape[0] // comps
    rows = depth // per
    for tile in range(cols // per):
        for comp in range(comps):
            parts = [
                field[comp * depth + q * rows : comp * depth + (q + 1) * rows, tile * lanes : (tile + 1) * lanes]
                for q in range(per)
            ]
            for p, part in enumerate(swap_blocks(parts, block)):
                out[tile * per + p, comp * rows : (comp + 1) * rows] = part


def span_kernel(comps, matrix, chunks, *refs):
    out = refs[-1]
    cols = out.shape[0]
    rows = out.shape[1] // comps
    values = [
        jnp.concatenate([chunks[p, comp * rows : (comp + 1) * rows] for p in range(cols)], axis=0)
        for comp in range(comps)
    ]
    right = jnp.concatenate(
        [jnp.concatenate([value, values[2] * value], axis=0) for value in values], axis=1
    )
    result = dot_split(matrix[...], right)
    for p in range(cols):
        for comp in range(comps):
            out[p, comp * rows : (comp + 1) * rows] = result[
                p * rows : (p + 1) * rows, comp * lanes : (comp + 1) * lanes
            ]


def circulant_rows(row, length):
    return pltpu.roll(jnp.broadcast_to(row, (length, length)), 0, 1, stride=1, stride_axis=0)


def span_matrix_kernel(zloc, z_first, z_second, field, packed, z_matrix, copied):
    cols = packed.shape[0]
    cells = cols * zloc
    group = z_matrix.shape[0] // cols
    shape = z_matrix.shape
    half = shape[1] // 2
    copied[...] = field[...]
    r = lax.broadcasted_iota(jnp.int32, shape, 0)
    q = lax.broadcasted_iota(jnp.int32, shape, 1)
    q = jnp.where(q < half, q, q - half)
    out_cell = (r // group) * zloc + r % zloc
    in_cell = (q // group) * zloc + q % zloc
    same = (r % group) // zloc == (q % group) // zloc
    gap = jnp.where(same, (in_cell - out_cell + cells) % cells, -1)
    line = lax.broadcasted_iota(jnp.int32, (1, shape[1]), 1) < half

    def fill(k, total):
        value = jnp.where(line, viscosity * z_second[k], -z_first[k])
        return jnp.where(gap == k, value, total)

    z_matrix[...] = lax.fori_loop(0, cells, fill, jnp.zeros(shape, jnp.float32), unroll=8)


def stream_kernel(
    rows,
    comps,
    slots,
    zloc,
    wall_counts,
    metric_table,
    metric_index,
    field,
    x_first,
    x_second,
    y_first,
    y_second,
    *refs,
):
    across = refs[: rows // 2 - 1]
    x_part, y_matrix, pair, scaled = refs[rows // 2 :]
    depth = slots * zloc
    length = field.shape[1]
    cells = y_first.shape[0]
    pair[0] = field[...]
    for i, other in enumerate(across):
        pair[i + 1] = other[...]

    u = field[...]
    lead = u[:depth]
    left = jnp.concatenate(
        [u, jnp.concatenate([lead * u[c * depth : (c + 1) * depth] for c in range(comps)], axis=0)], axis=1
    )
    right = jnp.concatenate(
        [viscosity * circulant_rows(x_second[...], length), -circulant_rows(x_first[...], length)], axis=1
    )
    x_part[...] = dot_split(left, right, transposed=True)

    def scale(j, carry):
        scaled[pl.ds(j, 1), :] = y_first[pl.ds(j, 1), :] * -metric_table[metric_index[j]]
        return carry

    lax.fori_loop(0, cells, scale, 0, unroll=8)
    me = lax.axis_index("row")

    def start_of(index):
        return lax.fori_loop(0, rows, lambda i, acc: acc + jnp.where(i < index, wall_counts[i], 0), 0, unroll=True)

    own = lax.broadcasted_iota(jnp.int32, (depth, cells), 0) // zloc
    cell = lax.broadcasted_iota(jnp.int32, (depth, cells), 1)
    mine = ((own < wall_counts[me]) & (own + start_of(me) == cell)).astype(jnp.float32)
    exact = functools.partial(
        lax.dot_general, precision=lax.Precision.HIGHEST, preferred_element_type=jnp.float32
    )
    plain = (((1,), (0,)), ((), ()))
    turned = (((1,), (1,)), ((), ()))
    both = [exact(mine, viscosity * y_second[...], plain), exact(mine, scaled[...], plain)]
    r = lax.broadcasted_iota(jnp.int32, (depth, depth), 0) % zloc
    q = lax.broadcasted_iota(jnp.int32, (depth, depth), 1) % zloc
    match = r == q
    for b in range(rows):
        other = me ^ (2 * b if b < rows // 2 else 2 * b + 1 - rows)
        theirs = ((own < wall_counts[other]) & (own + start_of(other) == cell)).astype(jnp.float32)
        for k in range(2):
            block = jnp.where(match, exact(both[k], theirs, turned), 0.0)
            y_matrix[:, (2 * b + k) * depth : (2 * b + k + 1) * depth] = block


def wall_kernel(comps, matrix, x_part, ours, theirs, out):
    depth = x_part.shape[0] // comps
    for comp in range(comps):
        at = slice(comp * depth, (comp + 1) * depth)
        stack = []
        for fields in (ours, theirs):
            for i in range(fields.shape[0]):
                value = fields[i, at]
                stack += [value, fields[i, depth : 2 * depth] * value]
        out[at] = x_part[at] + dot_split(matrix[...], jnp.concatenate(stack, axis=0))


def finish_kernel(comps, zloc, wall_counts, total, chunks, out):
    cols = chunks.shape[0]
    block = out.shape[1] // cols
    per = lanes // block
    depth = out.shape[0] // comps
    rows = depth // per
    count = wall_counts[lax.axis_index("row")]
    for tile in range(cols // per):
        for comp in range(comps):
            parts = [chunks[tile * per + p, comp * rows : (comp + 1) * rows] for p in range(per)]
            for q, part in enumerate(swap_blocks(parts, block)):
                at = slice(comp * depth + q * rows, comp * depth + (q + 1) * rows)
                across = slice(tile * lanes, (tile + 1) * lanes)
                plane = (lax.broadcasted_iota(jnp.int32, part.shape, 0) + q * rows) // zloc
                out[at, across] = jnp.where(plane < count, total[at, across] + part, 0.0)


def call(kernel, operands, spaces, results, name, scratch=()):
    results = [jax.ShapeDtypeStruct(shape, jnp.float32) for shape in results]
    held = sum(4 * math.prod(array.shape) for array in list(operands) + results)
    return pl.pallas_call(
        kernel,
        out_shape=results,
        in_specs=[pl.BlockSpec(memory_space=space) for space in spaces],
        out_specs=[pl.BlockSpec(memory_space=VMEM)] * len(results),
        scratch_shapes=[pltpu.VMEM(shape, jnp.float32) for shape in scratch],
        compiler_params=pltpu.CompilerParams(vmem_limit_bytes=(4 << 20) + 3 * held),
        name=name,
    )(*operands)


def local(
    velocity,
    wall_counts,
    x_first,
    x_second,
    y_first,
    y_second,
    z_first,
    z_second,
    metric_table,
    metric_index,
):
    rows = lax.axis_size("row")
    cols = lax.axis_size("col")
    comps, slots, zloc, length = velocity.shape
    depth = slots * zloc
    field = velocity.reshape(comps * depth, length)
    block = length // cols
    group = depth // (lanes // block)
    chunks = (cols, comps * group, lanes)

    def swap(value, step):
        return lax.ppermute(value, "row", [(i, i ^ step) for i in range(rows)])

    def turn(value):
        return lax.all_to_all(value, "col", split_axis=0, concat_axis=0, tiled=True)

    (packed,) = call(functools.partial(pack_kernel, comps), [field], [VMEM], [chunks], "pack")
    received = turn(packed)
    z_matrix, copied = call(
        functools.partial(span_matrix_kernel, zloc),
        [z_first, z_second, field, packed],
        [SMEM] * 2 + [VMEM, pl.ANY],
        [(cols * group, 2 * cols * group), field.shape],
        "span_matrix",
    )
    across = [swap(copied, step) for step in range(2, rows, 2)]
    (parts,) = call(
        functools.partial(span_kernel, comps),
        [z_matrix, received] + across,
        [VMEM] * 2 + [pl.ANY] * len(across),
        [chunks],
        "span",
    )
    returned = turn(parts)
    x_part, y_matrix, pair = call(
        functools.partial(stream_kernel, rows, comps, slots, zloc),
        [
            wall_counts,
            metric_table,
            metric_index,
            field,
            x_first.reshape(1, length),
            x_second.reshape(1, length),
            y_first,
            y_second,
        ]
        + across
        + [parts],
        [SMEM] * 3 + [VMEM] * (5 + len(across)) + [pl.ANY],
        [field.shape, (depth, 2 * rows * depth), (rows // 2,) + field.shape],
        "stream",
        [y_first.shape],
    )
    other = swap(pair, 1)
    (total,) = call(
        functools.partial(wall_kernel, comps), [y_matrix, x_part, pair, other], [VMEM] * 4, [field.shape], "wall"
    )
    (result,) = call(
        functools.partial(finish_kernel, comps, zloc),
        [wall_counts, total, returned],
        [SMEM] + [VMEM] * 2,
        [field.shape],
        "finish",
    )
    return result.reshape(velocity.shape)


def solution(mesh):
    in_specs = (P(None, "row", "col", None), P(), P(), P(), P(), P(), P(), P(), P(), P())
    out_specs = P(None, "row", "col", None)
    return jax.shard_map(local, mesh=mesh, in_specs=in_specs, out_specs=out_specs, check_vma=False)
```

```python
import functools
import math

import jax
import jax.numpy as jnp
from jax import lax
from jax.experimental import pallas as pl
from jax.experimental.pallas import tpu as pltpu
from jax.sharding import PartitionSpec as P

viscosity = 0.4
lanes = 128

VMEM = pltpu.VMEM
SMEM = pltpu.SMEM


def halves(value):
    high = value.astype(jnp.bfloat16)
    low = (value - high.astype(jnp.float32)).astype(jnp.bfloat16)
    return high, low


def dot_split(left, right, transposed=False):
    dims = (((1,), (1 if transposed else 0,)), ((), ()))
    mul = functools.partial(lax.dot_general, dimension_numbers=dims, preferred_element_type=jnp.float32)
    lh, ll = halves(left)
    rh, rl = halves(right)
    return mul(lh, rh) + (mul(lh, rl) + mul(ll, rh))


def swap_blocks(parts, block):
    parts = list(parts)
    count = len(parts)
    lane = lax.broadcasted_iota(jnp.int32, parts[0].shape, 1) // block
    step = count // 2
    while step:
        low = (lane & step) == 0
        for i in range(count):
            if i & step:
                continue
            a, b = parts[i], parts[i | step]
            parts[i] = jnp.where(low, a, pltpu.roll(b, step * block, 1))
            parts[i | step] = jnp.where(low, pltpu.roll(a, lanes - step * block, 1), b)
        step //= 2
    return parts


def pack_kernel(comps, line, field, partner, *refs):
    outs, scratch = refs[:line], refs[line]
    block = field.shape[1] // line
    per = lanes // block
    depth = field.shape[0] // comps
    rows = depth // per
    my = lax.axis_index("col") // 2
    for i, source in enumerate((field, partner)):
        for comp in range(comps):
            at = (i * comps + comp) * rows
            for tile in range(line // per):
                across = slice(tile * lanes, (tile + 1) * lanes)
                parts = [source[comp * depth + q * rows : comp * depth + (q + 1) * rows, across] for q in range(per)]
                for p, part in enumerate(swap_blocks(parts, block)):
                    scratch[tile * per + p, at : at + rows] = part
    for s in range(line):
        outs[s][...] = scratch[my ^ s]


def span_kernel(comps, line, matrix, *refs):
    chunks, outs = refs[:line], refs[-line:]
    rows = outs[0].shape[0] // comps
    values = [
        jnp.concatenate(
            [chunk[(i * comps + comp) * rows : (i * comps + comp + 1) * rows] for chunk in chunks for i in range(2)],
            axis=0,
        )
        for comp in range(comps)
    ]
    right = jnp.concatenate(
        [jnp.concatenate([value, values[2] * value], axis=0) for value in values], axis=1
    )
    result = dot_split(matrix[...], right)
    for t in range(line):
        for comp in range(comps):
            outs[t][comp * rows : (comp + 1) * rows] = result[
                t * rows : (t + 1) * rows, comp * lanes : (comp + 1) * lanes
            ]


def circulant_rows(row, length):
    return pltpu.roll(jnp.broadcast_to(row, (length, length)), 0, 1, stride=1, stride_axis=0)


def stream_kernel(
    rows,
    cols,
    comps,
    slots,
    zloc,
    wall_counts,
    z_first,
    z_second,
    metric_table,
    metric_index,
    field,
    x_first,
    x_second,
    y_first,
    y_second,
    x_part,
    y_matrix,
    z_matrix,
    scaled,
):
    depth = slots * zloc
    length = field.shape[1]
    cells = y_first.shape[0]

    cells_z = cols * zloc
    shape = z_matrix.shape
    half = shape[1] // 2
    group = shape[0] // (cols // 2)
    my = lax.axis_index("col") // 2
    low = lax.axis_index("col") % 2
    r = lax.broadcasted_iota(jnp.int32, shape, 0)
    q = lax.broadcasted_iota(jnp.int32, shape, 1)
    q = jnp.where(q < half, q, q - half)
    out_cell = (2 * ((r // group) ^ my) + low) * zloc + r % zloc
    in_cell = (2 * ((q // (2 * group)) ^ my) + (((q // group) % 2) ^ low)) * zloc + q % zloc
    same = (r % group) // zloc == (q % group) // zloc
    gap = jnp.where(same, (in_cell - out_cell + cells_z) % cells_z, -1)
    side = lax.broadcasted_iota(jnp.int32, (1, shape[1]), 1) < half

    def fill(k, total):
        value = jnp.where(side, viscosity * z_second[k], -z_first[k])
        return jnp.where(gap == k, value, total)

    z_matrix[...] = lax.fori_loop(0, cells_z, fill, jnp.zeros(shape, jnp.float32), unroll=8)

    u = field[...]
    lead = u[:depth]
    left = jnp.concatenate(
        [u, jnp.concatenate([lead * u[c * depth : (c + 1) * depth] for c in range(comps)], axis=0)], axis=1
    )
    right = jnp.concatenate(
        [viscosity * circulant_rows(x_second[...], length), -circulant_rows(x_first[...], length)], axis=1
    )
    x_part[...] = dot_split(left, right, transposed=True)

    def scale(j, carry):
        scaled[pl.ds(j, 1), :] = y_first[pl.ds(j, 1), :] * -metric_table[metric_index[j]]
        return carry

    lax.fori_loop(0, cells, scale, 0, unroll=8)
    me = lax.axis_index("row")

    def start_of(index):
        return lax.fori_loop(0, rows, lambda i, acc: acc + jnp.where(i < index, wall_counts[i], 0), 0, unroll=True)

    own = lax.broadcasted_iota(jnp.int32, (depth, cells), 0) // zloc
    cell = lax.broadcasted_iota(jnp.int32, (depth, cells), 1)
    mine = ((own < wall_counts[me]) & (own + start_of(me) == cell)).astype(jnp.float32)
    exact = functools.partial(
        lax.dot_general, precision=lax.Precision.HIGHEST, preferred_element_type=jnp.float32
    )
    plain = (((1,), (0,)), ((), ()))
    turned = (((1,), (1,)), ((), ()))
    both = [exact(mine, viscosity * y_second[...], plain), exact(mine, scaled[...], plain)]
    r = lax.broadcasted_iota(jnp.int32, (depth, depth), 0) % zloc
    q = lax.broadcasted_iota(jnp.int32, (depth, depth), 1) % zloc
    match = r == q
    for b in range(rows):
        other = me ^ (2 * b if b < rows // 2 else 2 * b + 1 - rows)
        theirs = ((own < wall_counts[other]) & (own + start_of(other) == cell)).astype(jnp.float32)
        for k in range(2):
            block = jnp.where(match, exact(both[k], theirs, turned), 0.0)
            y_matrix[:, (2 * b + k) * depth : (2 * b + k + 1) * depth] = block


def wall_kernel(comps, matrix, x_part, *refs):
    fields, out = refs[:-1], refs[-1]
    depth = x_part.shape[0] // comps
    for comp in range(comps):
        at = slice(comp * depth, (comp + 1) * depth)
        stack = []
        for field in fields:
            value = field[at]
            stack += [value, field[depth : 2 * depth] * value]
        out[at] = x_part[at] + dot_split(matrix[...], jnp.concatenate(stack, axis=0))


def finish_kernel(comps, line, zloc, wall_counts, total, *refs):
    chunks, out, scratch = refs[:line], refs[line], refs[line + 1]
    block = out.shape[1] // line
    per = lanes // block
    depth = out.shape[0] // comps
    rows = depth // per
    my = lax.axis_index("col") // 2
    count = wall_counts[lax.axis_index("row")]
    for t in range(line):
        scratch[my ^ t] = chunks[t][...]
    for tile in range(line // per):
        across = slice(tile * lanes, (tile + 1) * lanes)
        for comp in range(comps):
            parts = [scratch[tile * per + p, comp * rows : (comp + 1) * rows] for p in range(per)]
            for q, part in enumerate(swap_blocks(parts, block)):
                at = slice(comp * depth + q * rows, comp * depth + (q + 1) * rows)
                plane = (lax.broadcasted_iota(jnp.int32, part.shape, 0) + q * rows) // zloc
                out[at, across] = jnp.where(plane < count, total[at, across] + part, 0.0)


def call(kernel, operands, spaces, results, name, scratch=()):
    results = [jax.ShapeDtypeStruct(shape, jnp.float32) for shape in results]
    held = sum(4 * math.prod(array.shape) for array in list(operands) + results)
    return pl.pallas_call(
        kernel,
        out_shape=results,
        in_specs=[pl.BlockSpec(memory_space=space) for space in spaces],
        out_specs=[pl.BlockSpec(memory_space=VMEM)] * len(results),
        scratch_shapes=[pltpu.VMEM(shape, jnp.float32) for shape in scratch],
        compiler_params=pltpu.CompilerParams(vmem_limit_bytes=(4 << 20) + 3 * held),
        name=name,
    )(*operands)


def local(
    velocity,
    wall_counts,
    x_first,
    x_second,
    y_first,
    y_second,
    z_first,
    z_second,
    metric_table,
    metric_index,
):
    rows = lax.axis_size("row")
    cols = lax.axis_size("col")
    comps, slots, zloc, length = velocity.shape
    depth = slots * zloc
    field = velocity.reshape(comps * depth, length)
    line = cols // 2
    group = depth // (lanes // (length // line))
    chunk = (comps * group, lanes)

    def along(value, step):
        return lax.ppermute(value, "col", [(i, i ^ step) for i in range(cols)])

    def across(value, step):
        return lax.ppermute(value, "row", [(i, i ^ step) for i in range(rows)])

    partner = along(field, 1)
    far = [across(field, step) for step in range(2, rows, 2)]
    near = across(field, 1)
    x_part, y_matrix, z_matrix = call(
        functools.partial(stream_kernel, rows, cols, comps, slots, zloc),
        [
            wall_counts,
            z_first,
            z_second,
            metric_table,
            metric_index,
            field,
            x_first.reshape(1, length),
            x_second.reshape(1, length),
            y_first,
            y_second,
        ],
        [SMEM] * 5 + [VMEM] * 5,
        [field.shape, (depth, 2 * rows * depth), (line * group, 4 * line * group)],
        "stream",
        [y_first.shape],
    )
    chunks = call(
        functools.partial(pack_kernel, comps, line),
        [field, partner],
        [VMEM] * 2,
        [(2 * comps * group, lanes)] * line,
        "pack",
        [(line, 2 * comps * group, lanes)],
    )
    received = [chunks[0]] + [along(chunks[s], 2 * s) for s in range(1, line)]
    parts = call(
        functools.partial(span_kernel, comps, line),
        [z_matrix] + received + far + [near],
        [VMEM] * (line + 1) + [pl.ANY] * (rows // 2),
        [chunk] * line,
        "span",
    )
    returned = [parts[0]] + [along(parts[t], 2 * t) for t in range(1, line)]
    (total,) = call(
        functools.partial(wall_kernel, comps),
        [y_matrix, x_part, field] + far + [near] + [across(value, 1) for value in far],
        [VMEM] * (rows + 2),
        [field.shape],
        "wall",
    )
    (result,) = call(
        functools.partial(finish_kernel, comps, line, zloc),
        [wall_counts, total] + returned,
        [SMEM] + [VMEM] * (line + 1),
        [field.shape],
        "finish",
        [(line,) + chunk],
    )
    return result.reshape(velocity.shape)


def solution(mesh):
    in_specs = (P(None, "row", "col", None), P(), P(), P(), P(), P(), P(), P(), P(), P())
    out_specs = P(None, "row", "col", None)
    return jax.shard_map(local, mesh=mesh, in_specs=in_specs, out_specs=out_specs, check_vma=False)
```

```python
import functools
import math

import jax
import jax.numpy as jnp
from jax import lax
from jax.experimental import pallas as pl
from jax.experimental.pallas import tpu as pltpu
from jax.sharding import PartitionSpec as P

viscosity = 0.4
lanes = 128

VMEM = pltpu.VMEM
SMEM = pltpu.SMEM


def halves(value):
    high = value.astype(jnp.bfloat16)
    low = (value - high.astype(jnp.float32)).astype(jnp.bfloat16)
    return high, low


def dot_split(left, right, transposed=False):
    dims = (((1,), (1 if transposed else 0,)), ((), ()))
    mul = functools.partial(lax.dot_general, dimension_numbers=dims, preferred_element_type=jnp.float32)
    lh, ll = halves(left)
    rh, rl = halves(right)
    return mul(lh, rh) + (mul(lh, rl) + mul(ll, rh))


def swap_blocks(parts, block):
    parts = list(parts)
    count = len(parts)
    lane = lax.broadcasted_iota(jnp.int32, parts[0].shape, 1) // block
    step = count // 2
    while step:
        low = (lane & step) == 0
        for i in range(count):
            if i & step:
                continue
            a, b = parts[i], parts[i | step]
            parts[i] = jnp.where(low, a, pltpu.roll(b, step * block, 1))
            parts[i | step] = jnp.where(low, pltpu.roll(a, lanes - step * block, 1), b)
        step //= 2
    return parts


def pack_kernel(comps, line, field, *refs):
    outs, scratch = refs[:line], refs[line]
    block = field.shape[1] // line
    per = lanes // block
    depth = field.shape[0] // comps
    rows = depth // per
    my = lax.axis_index("col") // 2
    for comp in range(comps):
        for tile in range(line // per):
            across = slice(tile * lanes, (tile + 1) * lanes)
            parts = [field[comp * depth + q * rows : comp * depth + (q + 1) * rows, across] for q in range(per)]
            for p, part in enumerate(swap_blocks(parts, block)):
                scratch[tile * per + p, comp * rows : (comp + 1) * rows] = part
    for s in range(line):
        outs[s][...] = scratch[my ^ s]


def span_kernel(comps, line, matrix, mask, *refs):
    chunks, (ours, theirs, pair) = refs[:line], refs[-3:]
    for i in range(pair.shape[0]):
        pair[i] = refs[line + i][...]
    group = mask.shape[0]
    values = [
        jnp.concatenate([chunk[comp * group : (comp + 1) * group] for chunk in chunks], axis=0)
        for comp in range(comps)
    ]
    right = jnp.concatenate(
        [jnp.concatenate([value, values[2] * value], axis=0) for value in values], axis=1
    )
    result = dot_split(matrix[...], right)
    live = jnp.concatenate([mask[...]] * line, axis=0)
    side = line * group
    for comp in range(comps):
        across = slice(comp * lanes, (comp + 1) * lanes)
        ours[comp] = live * result[:side, across]
        theirs[comp] = live * result[side:, across]


def add_kernel(comps, line, ours, met, after, *outs):
    group = ours.shape[1] // line
    for t in range(line):
        for comp in range(comps):
            at = slice(t * group, (t + 1) * group)
            outs[t][comp * group : (comp + 1) * group] = ours[comp, at] + met[comp, at]


def circulant_rows(row, length):
    return pltpu.roll(jnp.broadcast_to(row, (length, length)), 0, 1, stride=1, stride_axis=0)


def stream_kernel(
    rows,
    cols,
    comps,
    slots,
    zloc,
    wall_counts,
    z_first,
    z_second,
    metric_table,
    metric_index,
    field,
    x_first,
    x_second,
    y_first,
    y_second,
    after,
    x_part,
    y_matrix,
    z_matrix,
    mask,
    scaled,
):
    depth = slots * zloc
    length = field.shape[1]
    cells = y_first.shape[0]
    me = lax.axis_index("row")

    cells_z = cols * zloc
    group = mask.shape[0]
    shape = z_matrix.shape
    half = shape[1] // 2
    side = shape[0] // 2
    my = lax.axis_index("col") // 2
    low = lax.axis_index("col") % 2
    r = lax.broadcasted_iota(jnp.int32, shape, 0)
    q = lax.broadcasted_iota(jnp.int32, shape, 1)
    other = jnp.where(r < side, low, 1 - low)
    r = jnp.where(r < side, r, r - side)
    q = jnp.where(q < half, q, q - half)
    out_cell = (2 * ((r // group) ^ my) + other) * zloc + r % zloc
    in_cell = (2 * ((q // group) ^ my) + low) * zloc + q % zloc
    same = (r % group) // zloc == (q % group) // zloc
    gap = jnp.where(same, (in_cell - out_cell + cells_z) % cells_z, -1)
    kind = lax.broadcasted_iota(jnp.int32, (1, shape[1]), 1) < half

    def fill(k, total):
        value = jnp.where(kind, viscosity * z_second[k], -z_first[k])
        return jnp.where(gap == k, value, total)

    z_matrix[...] = lax.fori_loop(0, cells_z, fill, jnp.zeros(shape, jnp.float32), unroll=8)
    per = depth // group
    plane = lax.broadcasted_iota(jnp.int32, mask.shape, 0) // zloc
    plane += lax.broadcasted_iota(jnp.int32, mask.shape, 1) // (lanes // per) * (group // zloc)
    mask[...] = (plane < wall_counts[me]).astype(jnp.float32)

    u = field[...]
    lead = u[:depth]
    left = jnp.concatenate(
        [u, jnp.concatenate([lead * u[c * depth : (c + 1) * depth] for c in range(comps)], axis=0)], axis=1
    )
    right = jnp.concatenate(
        [viscosity * circulant_rows(x_second[...], length), -circulant_rows(x_first[...], length)], axis=1
    )
    plane = lax.broadcasted_iota(jnp.int32, field.shape, 0) % depth // zloc
    x_part[...] = jnp.where(plane < wall_counts[me], dot_split(left, right, transposed=True), 0.0)

    def scale(j, carry):
        scaled[pl.ds(j, 1), :] = y_first[pl.ds(j, 1), :] * -metric_table[metric_index[j]]
        return carry

    lax.fori_loop(0, cells, scale, 0, unroll=8)

    def start_of(index):
        return lax.fori_loop(0, rows, lambda i, acc: acc + jnp.where(i < index, wall_counts[i], 0), 0, unroll=True)

    own = lax.broadcasted_iota(jnp.int32, (depth, cells), 0) // zloc
    cell = lax.broadcasted_iota(jnp.int32, (depth, cells), 1)
    mine = ((own < wall_counts[me]) & (own + start_of(me) == cell)).astype(jnp.float32)
    exact = functools.partial(
        lax.dot_general, precision=lax.Precision.HIGHEST, preferred_element_type=jnp.float32
    )
    plain = (((1,), (0,)), ((), ()))
    turned = (((1,), (1,)), ((), ()))
    both = [exact(mine, viscosity * y_second[...], plain), exact(mine, scaled[...], plain)]
    r = lax.broadcasted_iota(jnp.int32, (depth, depth), 0) % zloc
    q = lax.broadcasted_iota(jnp.int32, (depth, depth), 1) % zloc
    match = r == q
    for b in range(rows):
        other = me ^ (2 * b if b < rows // 2 else 2 * b + 1 - rows)
        theirs = ((own < wall_counts[other]) & (own + start_of(other) == cell)).astype(jnp.float32)
        for k in range(2):
            block = jnp.where(match, exact(both[k], theirs, turned), 0.0)
            y_matrix[:, (2 * b + k) * depth : (2 * b + k + 1) * depth] = block


def wall_kernel(comps, matrix, x_part, ours, theirs, out):
    depth = x_part.shape[0] // comps
    for comp in range(comps):
        at = slice(comp * depth, (comp + 1) * depth)
        stack = []
        for fields in (ours, theirs):
            for i in range(fields.shape[0]):
                value = fields[i, at]
                stack += [value, fields[i, depth : 2 * depth] * value]
        out[at] = x_part[at] + dot_split(matrix[...], jnp.concatenate(stack, axis=0))


def finish_kernel(comps, line, total, *refs):
    chunks, out, scratch = refs[:line], refs[line], refs[line + 1]
    block = out.shape[1] // line
    per = lanes // block
    depth = out.shape[0] // comps
    rows = depth // per
    my = lax.axis_index("col") // 2
    for t in range(line):
        scratch[my ^ t] = chunks[t][...]
    for tile in range(line // per):
        across = slice(tile * lanes, (tile + 1) * lanes)
        for comp in range(comps):
            parts = [scratch[tile * per + p, comp * rows : (comp + 1) * rows] for p in range(per)]
            for q, part in enumerate(swap_blocks(parts, block)):
                at = slice(comp * depth + q * rows, comp * depth + (q + 1) * rows)
                out[at, across] = total[at, across] + part


def call(kernel, operands, spaces, results, name, scratch=()):
    results = [jax.ShapeDtypeStruct(shape, jnp.float32) for shape in results]
    held = sum(4 * math.prod(array.shape) for array in list(operands) + results)
    return pl.pallas_call(
        kernel,
        out_shape=results,
        in_specs=[pl.BlockSpec(memory_space=space) for space in spaces],
        out_specs=[pl.BlockSpec(memory_space=VMEM)] * len(results),
        scratch_shapes=[pltpu.VMEM(shape, jnp.float32) for shape in scratch],
        compiler_params=pltpu.CompilerParams(vmem_limit_bytes=(4 << 20) + 3 * held),
        name=name,
    )(*operands)


def local(
    velocity,
    wall_counts,
    x_first,
    x_second,
    y_first,
    y_second,
    z_first,
    z_second,
    metric_table,
    metric_index,
):
    rows = lax.axis_size("row")
    cols = lax.axis_size("col")
    comps, slots, zloc, length = velocity.shape
    depth = slots * zloc
    field = velocity.reshape(comps * depth, length)
    line = cols // 2
    group = depth // (lanes // (length // line))
    chunk = (comps * group, lanes)

    def along(value, step):
        return lax.ppermute(value, "col", [(i, i ^ step) for i in range(cols)])

    def across(value, step):
        return lax.ppermute(value, "row", [(i, i ^ step) for i in range(rows)])

    far = [across(field, step) for step in range(2, rows, 2)]
    chunks = call(functools.partial(pack_kernel, comps, line), [field], [VMEM], [chunk] * line, "pack", [(line,) + chunk])
    received = [chunks[0]] + [None] * (line - 1)
    for s in reversed(range(1, line)):
        received[s] = along(chunks[s], 2 * s)
    x_part, y_matrix, z_matrix, mask = call(
        functools.partial(stream_kernel, rows, cols, comps, slots, zloc),
        [
            wall_counts,
            z_first,
            z_second,
            metric_table,
            metric_index,
            field,
            x_first.reshape(1, length),
            x_second.reshape(1, length),
            y_first,
            y_second,
            chunks[0],
        ],
        [SMEM] * 5 + [VMEM] * 5 + [pl.ANY],
        [field.shape, (depth, 2 * rows * depth), (2 * line * group, 2 * line * group), (group, lanes)],
        "stream",
        [y_first.shape],
    )
    ours, theirs, pair = call(
        functools.partial(span_kernel, comps, line),
        [z_matrix, mask] + received + [field] + far,
        [VMEM] * (line + 2 + rows // 2),
        [(comps, line * group, lanes)] * 2 + [(rows // 2,) + field.shape],
        "span",
    )
    met = along(theirs, 1)
    other = across(pair, 1)
    (total,) = call(
        functools.partial(wall_kernel, comps), [y_matrix, x_part, pair, other], [VMEM] * 4, [field.shape], "wall"
    )
    parts = call(
        functools.partial(add_kernel, comps, line),
        [ours, met, total],
        [VMEM] * 2 + [pl.ANY],
        [chunk] * line,
        "add",
    )
    returned = [parts[0]] + [None] * (line - 1)
    for t in reversed(range(1, line)):
        returned[t] = along(parts[t], 2 * t)
    (result,) = call(
        functools.partial(finish_kernel, comps, line),
        [total] + returned,
        [VMEM] * (line + 1),
        [field.shape],
        "finish",
        [(line,) + chunk],
    )
    return result.reshape(velocity.shape)


def solution(mesh):
    in_specs = (P(None, "row", "col", None), P(), P(), P(), P(), P(), P(), P(), P(), P())
    out_specs = P(None, "row", "col", None)
    return jax.shard_map(local, mesh=mesh, in_specs=in_specs, out_specs=out_specs, check_vma=False)
```

```python
import functools
import math

import jax
import jax.numpy as jnp
from jax import lax
from jax.experimental import pallas as pl
from jax.experimental.pallas import tpu as pltpu
from jax.sharding import PartitionSpec as P

viscosity = 0.4
quad = 4

VMEM = pltpu.VMEM
SMEM = pltpu.SMEM


def halves(value):
    high = value.astype(jnp.bfloat16)
    low = (value - high.astype(jnp.float32)).astype(jnp.bfloat16)
    return high, low


def dot_split(left, right, transposed=False):
    dims = (((1,), (1 if transposed else 0,)), ((), ()))
    mul = functools.partial(lax.dot_general, dimension_numbers=dims, preferred_element_type=jnp.float32)
    lh, ll = halves(left)
    rh, rl = halves(right)
    return mul(lh, rh) + (mul(lh, rl) + mul(ll, rh))


def span_kernel(comps, matrix, field, *refs):
    parts, pair = refs[-quad - 1 : -1], refs[-1]
    pair[0] = field[...]
    for i in range(1, pair.shape[0]):
        pair[i] = refs[i - 1][...]
    sources = (field,) + refs[pair.shape[0] - 1 : -quad - 1]
    depth, length = field.shape[0] // comps, field.shape[1]
    group = matrix.shape[0] // quad
    right = []
    for comp in range(comps):
        for at in range(0, depth, group):
            stack = [source[comp * depth + at : comp * depth + at + group] for source in sources]
            stack += [value * source[2 * depth + at : 2 * depth + at + group] for value, source in zip(stack, sources)]
            right.append(jnp.concatenate(stack, axis=0))
    result = dot_split(matrix[...], jnp.concatenate(right, axis=1))
    for t in range(quad):
        for i in range(len(right)):
            parts[t][i * group : (i + 1) * group] = result[
                t * group : (t + 1) * group, i * length : (i + 1) * length
            ]


def circulant_rows(row, length):
    return pltpu.roll(jnp.broadcast_to(row, (length, length)), 0, 1, stride=1, stride_axis=0)


def stream_kernel(
    rows,
    cols,
    comps,
    slots,
    zloc,
    wall_counts,
    z_first,
    z_second,
    metric_table,
    metric_index,
    field,
    x_first,
    x_second,
    y_first,
    y_second,
    x_part,
    y_matrix,
    z_matrix,
    mask,
    scaled,
):
    depth = slots * zloc
    length = field.shape[1]
    cells = y_first.shape[0]
    me = lax.axis_index("row")
    mask[...] = (lax.broadcasted_iota(jnp.int32, mask.shape, 0) // zloc < wall_counts[me]).astype(jnp.float32)

    cells_z = cols * zloc
    shape = z_matrix.shape
    half = shape[1] // 2
    group = shape[0] // quad
    mine = lax.axis_index("col")
    r = lax.broadcasted_iota(jnp.int32, shape, 0)
    q = lax.broadcasted_iota(jnp.int32, shape, 1)
    q = jnp.where(q < half, q, q - half)
    out_cell = ((r // group) ^ mine) * zloc + r % zloc
    in_cell = ((quad * (q // group)) ^ mine) * zloc + q % zloc
    same = (r % group) // zloc == (q % group) // zloc
    gap = jnp.where(same, (in_cell - out_cell + cells_z) % cells_z, -1)
    kind = lax.broadcasted_iota(jnp.int32, (1, shape[1]), 1) < half

    def fill(k, total):
        value = jnp.where(kind, viscosity * z_second[k], -z_first[k])
        return jnp.where(gap == k, value, total)

    z_matrix[...] = lax.fori_loop(0, cells_z, fill, jnp.zeros(shape, jnp.float32), unroll=8)

    u = field[...]
    lead = u[:depth]
    left = jnp.concatenate(
        [u, jnp.concatenate([lead * u[c * depth : (c + 1) * depth] for c in range(comps)], axis=0)], axis=1
    )
    right = jnp.concatenate(
        [viscosity * circulant_rows(x_second[...], length), -circulant_rows(x_first[...], length)], axis=1
    )
    x_part[...] = dot_split(left, right, transposed=True)

    def scale(j, carry):
        scaled[pl.ds(j, 1), :] = y_first[pl.ds(j, 1), :] * -metric_table[metric_index[j]]
        return carry

    lax.fori_loop(0, cells, scale, 0, unroll=8)

    def start_of(index):
        return lax.fori_loop(0, rows, lambda i, acc: acc + jnp.where(i < index, wall_counts[i], 0), 0, unroll=True)

    own = lax.broadcasted_iota(jnp.int32, (depth, cells), 0) // zloc
    cell = lax.broadcasted_iota(jnp.int32, (depth, cells), 1)
    mine = ((own < wall_counts[me]) & (own + start_of(me) == cell)).astype(jnp.float32)
    exact = functools.partial(
        lax.dot_general, precision=lax.Precision.HIGHEST, preferred_element_type=jnp.float32
    )
    plain = (((1,), (0,)), ((), ()))
    turned = (((1,), (1,)), ((), ()))
    both = [exact(mine, viscosity * y_second[...], plain), exact(mine, scaled[...], plain)]
    r = lax.broadcasted_iota(jnp.int32, (depth, depth), 0) % zloc
    q = lax.broadcasted_iota(jnp.int32, (depth, depth), 1) % zloc
    match = r == q
    for b in range(rows):
        other = me ^ (2 * b if b < rows // 2 else 2 * b + 1 - rows)
        theirs = ((own < wall_counts[other]) & (own + start_of(other) == cell)).astype(jnp.float32)
        for k in range(2):
            block = jnp.where(match, exact(both[k], theirs, turned), 0.0)
            y_matrix[:, (2 * b + k) * depth : (2 * b + k + 1) * depth] = block


def wall_kernel(comps, matrix, x_part, z_part, ours, theirs, out):
    depth = x_part.shape[0] // comps
    for comp in range(comps):
        at = slice(comp * depth, (comp + 1) * depth)
        stack = []
        for fields in (ours, theirs):
            for i in range(fields.shape[0]):
                value = fields[i, at]
                stack += [value, fields[i, depth : 2 * depth] * value]
        out[at] = x_part[at] + z_part[at] + dot_split(matrix[...], jnp.concatenate(stack, axis=0))


def finish_kernel(comps, mask, *refs):
    parts, out = refs[:-1], refs[-1]
    depth = mask.shape[0]
    for comp in range(comps):
        at = slice(comp * depth, (comp + 1) * depth)
        out[at] = jnp.where(mask[...] > 0, sum(part[at] for part in parts[1:]) + parts[0][at], 0.0)


def call(kernel, operands, spaces, results, name, scratch=()):
    results = [jax.ShapeDtypeStruct(shape, jnp.float32) for shape in results]
    held = sum(4 * math.prod(array.shape) for array in list(operands) + results)
    return pl.pallas_call(
        kernel,
        out_shape=results,
        in_specs=[pl.BlockSpec(memory_space=space) for space in spaces],
        out_specs=[pl.BlockSpec(memory_space=VMEM)] * len(results),
        scratch_shapes=[pltpu.VMEM(shape, jnp.float32) for shape in scratch],
        compiler_params=pltpu.CompilerParams(vmem_limit_bytes=(4 << 20) + 3 * held),
        name=name,
    )(*operands)


def local(
    velocity,
    wall_counts,
    x_first,
    x_second,
    y_first,
    y_second,
    z_first,
    z_second,
    metric_table,
    metric_index,
):
    rows = lax.axis_size("row")
    cols = lax.axis_size("col")
    comps, slots, zloc, length = velocity.shape
    depth = slots * zloc
    field = velocity.reshape(comps * depth, length)
    group = min(depth, 32)
    sources = cols // quad

    def along(value, step):
        return lax.ppermute(value, "col", [(i, i ^ step) for i in range(cols)])

    def across(value, step):
        return lax.ppermute(value, "row", [(i, i ^ step) for i in range(rows)])

    gathered = [along(field, quad * i) for i in range(1, sources)]
    far = [across(field, step) for step in range(2, rows, 2)]
    x_part, y_matrix, z_matrix, mask = call(
        functools.partial(stream_kernel, rows, cols, comps, slots, zloc),
        [
            wall_counts,
            z_first,
            z_second,
            metric_table,
            metric_index,
            field,
            x_first.reshape(1, length),
            x_second.reshape(1, length),
            y_first,
            y_second,
        ],
        [SMEM] * 5 + [VMEM] * 5,
        [field.shape, (depth, 2 * rows * depth), (quad * group, 2 * sources * group), (depth, length)],
        "stream",
        [y_first.shape],
    )
    *parts, pair = call(
        functools.partial(span_kernel, comps),
        [z_matrix, field] + far + gathered,
        [VMEM] * (rows // 2 + sources),
        [field.shape] * quad + [(rows // 2,) + field.shape],
        "span",
    )
    returned = [along(parts[t], t) for t in reversed(range(1, quad))]
    other = across(pair, 1)
    (total,) = call(
        functools.partial(wall_kernel, comps),
        [y_matrix, x_part, parts[0], pair, other],
        [VMEM] * 5,
        [field.shape],
        "wall",
    )
    (result,) = call(
        functools.partial(finish_kernel, comps),
        [mask, total] + returned,
        [VMEM] * (quad + 1),
        [field.shape],
        "finish",
    )
    return result.reshape(velocity.shape)


def solution(mesh):
    in_specs = (P(None, "row", "col", None), P(), P(), P(), P(), P(), P(), P(), P(), P())
    out_specs = P(None, "row", "col", None)
    return jax.shard_map(local, mesh=mesh, in_specs=in_specs, out_specs=out_specs, check_vma=False)
```

```python
import functools
import math

import jax
import jax.numpy as jnp
from jax import lax
from jax.experimental import pallas as pl
from jax.experimental.pallas import tpu as pltpu
from jax.sharding import PartitionSpec as P

viscosity = 0.4
quad = 4

VMEM = pltpu.VMEM
SMEM = pltpu.SMEM


def halves(value):
    high = value.astype(jnp.bfloat16)
    low = (value - high.astype(jnp.float32)).astype(jnp.bfloat16)
    return high, low


def dot_split(left, right, transposed=False):
    dims = (((1,), (1 if transposed else 0,)), ((), ()))
    mul = functools.partial(lax.dot_general, dimension_numbers=dims, preferred_element_type=jnp.float32)
    lh, ll = halves(left)
    rh, rl = halves(right)
    return mul(lh, rh) + (mul(lh, rl) + mul(ll, rh))


def span_kernel(comps, matrix, field, *refs):
    parts, pair = refs[-quad - 1 : -1], refs[-1]
    pair[0] = field[...]
    for i in range(1, pair.shape[0]):
        pair[i] = refs[i - 1][...]
    sources = (field,) + refs[pair.shape[0] - 1 : -quad - 1]
    depth, length = field.shape[0] // comps, field.shape[1]
    group = matrix.shape[0] // quad
    right = []
    for comp in range(comps):
        for at in range(0, depth, group):
            stack = [source[comp * depth + at : comp * depth + at + group] for source in sources]
            stack += [value * source[2 * depth + at : 2 * depth + at + group] for value, source in zip(stack, sources)]
            right.append(jnp.concatenate(stack, axis=0))
    result = dot_split(matrix[...], jnp.concatenate(right, axis=1))
    for t in range(quad):
        for i in range(len(right)):
            parts[t][i * group : (i + 1) * group] = result[
                t * group : (t + 1) * group, i * length : (i + 1) * length
            ]


def circulant_rows(row, length):
    return pltpu.roll(jnp.broadcast_to(row, (length, length)), 0, 1, stride=1, stride_axis=0)


def stream_kernel(
    cols, comps, zloc, wall_counts, z_first, z_second, field, x_first, x_second, x_part, z_matrix, mask
):
    depth = mask.shape[0]
    length = field.shape[1]
    count = wall_counts[lax.axis_index("row")]
    mask[...] = (lax.broadcasted_iota(jnp.int32, mask.shape, 0) // zloc < count).astype(jnp.float32)

    cells_z = cols * zloc
    shape = z_matrix.shape
    half = shape[1] // 2
    group = shape[0] // quad
    mine = lax.axis_index("col")
    r = lax.broadcasted_iota(jnp.int32, shape, 0)
    q = lax.broadcasted_iota(jnp.int32, shape, 1)
    q = jnp.where(q < half, q, q - half)
    out_cell = ((r // group) ^ mine) * zloc + r % zloc
    in_cell = ((quad * (q // group)) ^ mine) * zloc + q % zloc
    same = (r % group) // zloc == (q % group) // zloc
    gap = jnp.where(same, (in_cell - out_cell + cells_z) % cells_z, -1)
    kind = lax.broadcasted_iota(jnp.int32, (1, shape[1]), 1) < half

    def fill(k, total):
        value = jnp.where(kind, viscosity * z_second[k], -z_first[k])
        return jnp.where(gap == k, value, total)

    z_matrix[...] = lax.fori_loop(0, cells_z, fill, jnp.zeros(shape, jnp.float32), unroll=8)

    u = field[...]
    lead = u[:depth]
    left = jnp.concatenate(
        [u, jnp.concatenate([lead * u[c * depth : (c + 1) * depth] for c in range(comps)], axis=0)], axis=1
    )
    right = jnp.concatenate(
        [viscosity * circulant_rows(x_second[...], length), -circulant_rows(x_first[...], length)], axis=1
    )
    x_part[...] = dot_split(left, right, transposed=True)


def wall_kernel(
    rows,
    comps,
    zloc,
    wall_counts,
    metric_table,
    metric_index,
    y_first,
    y_second,
    x_part,
    z_part,
    ours,
    theirs,
    out,
    matrix,
    scaled,
):
    depth = x_part.shape[0] // comps
    cells = y_first.shape[0]

    def scale(j, carry):
        scaled[pl.ds(j, 1), :] = y_first[pl.ds(j, 1), :] * -metric_table[metric_index[j]]
        return carry

    lax.fori_loop(0, cells, scale, 0, unroll=8)
    me = lax.axis_index("row")

    def start_of(index):
        return lax.fori_loop(0, rows, lambda i, acc: acc + jnp.where(i < index, wall_counts[i], 0), 0, unroll=True)

    own = lax.broadcasted_iota(jnp.int32, (depth, cells), 0) // zloc
    cell = lax.broadcasted_iota(jnp.int32, (depth, cells), 1)
    mine = ((own < wall_counts[me]) & (own + start_of(me) == cell)).astype(jnp.float32)
    exact = functools.partial(
        lax.dot_general, precision=lax.Precision.HIGHEST, preferred_element_type=jnp.float32
    )
    plain = (((1,), (0,)), ((), ()))
    turned = (((1,), (1,)), ((), ()))
    both = [exact(mine, viscosity * y_second[...], plain), exact(mine, scaled[...], plain)]
    r = lax.broadcasted_iota(jnp.int32, (depth, depth), 0) % zloc
    q = lax.broadcasted_iota(jnp.int32, (depth, depth), 1) % zloc
    match = r == q
    for b in range(rows):
        other = me ^ (2 * b if b < rows // 2 else 2 * b + 1 - rows)
        spots = ((own < wall_counts[other]) & (own + start_of(other) == cell)).astype(jnp.float32)
        for k in range(2):
            block = jnp.where(match, exact(both[k], spots, turned), 0.0)
            matrix[:, (2 * b + k) * depth : (2 * b + k + 1) * depth] = block

    for comp in range(comps):
        at = slice(comp * depth, (comp + 1) * depth)
        stack = []
        for fields in (ours, theirs):
            for i in range(fields.shape[0]):
                value = fields[i, at]
                stack += [value, fields[i, depth : 2 * depth] * value]
        out[at] = x_part[at] + z_part[at] + dot_split(matrix[...], jnp.concatenate(stack, axis=0))


def finish_kernel(comps, mask, *refs):
    parts, out = refs[:-1], refs[-1]
    depth = mask.shape[0]
    for comp in range(comps):
        at = slice(comp * depth, (comp + 1) * depth)
        out[at] = jnp.where(mask[...] > 0, sum(part[at] for part in parts[1:]) + parts[0][at], 0.0)


def call(kernel, operands, spaces, results, name, scratch=()):
    results = [jax.ShapeDtypeStruct(shape, jnp.float32) for shape in results]
    held = sum(4 * math.prod(array.shape) for array in list(operands) + results)
    return pl.pallas_call(
        kernel,
        out_shape=results,
        in_specs=[pl.BlockSpec(memory_space=space) for space in spaces],
        out_specs=[pl.BlockSpec(memory_space=VMEM)] * len(results),
        scratch_shapes=[pltpu.VMEM(shape, jnp.float32) for shape in scratch],
        compiler_params=pltpu.CompilerParams(vmem_limit_bytes=(4 << 20) + 3 * held),
        name=name,
    )(*operands)


def local(
    velocity,
    wall_counts,
    x_first,
    x_second,
    y_first,
    y_second,
    z_first,
    z_second,
    metric_table,
    metric_index,
):
    rows = lax.axis_size("row")
    cols = lax.axis_size("col")
    comps, slots, zloc, length = velocity.shape
    depth = slots * zloc
    field = velocity.reshape(comps * depth, length)
    group = min(depth, 32)
    sources = cols // quad

    def along(value, step):
        return lax.ppermute(value, "col", [(i, i ^ step) for i in range(cols)])

    def across(value, step):
        return lax.ppermute(value, "row", [(i, i ^ step) for i in range(rows)])

    gathered = [along(field, quad * i) for i in range(1, sources)]
    far = [across(field, step) for step in range(2, rows, 2)]
    x_part, z_matrix, mask = call(
        functools.partial(stream_kernel, cols, comps, zloc),
        [wall_counts, z_first, z_second, field, x_first.reshape(1, length), x_second.reshape(1, length)],
        [SMEM] * 3 + [VMEM] * 3,
        [field.shape, (quad * group, 2 * sources * group), (depth, length)],
        "stream",
    )
    *parts, pair = call(
        functools.partial(span_kernel, comps),
        [z_matrix, field] + far + gathered,
        [VMEM] * (rows // 2 + sources),
        [field.shape] * quad + [(rows // 2,) + field.shape],
        "span",
    )
    returned = [along(parts[t], t) for t in reversed(range(1, quad))]
    other = across(pair, 1)
    (total,) = call(
        functools.partial(wall_kernel, rows, comps, zloc),
        [wall_counts, metric_table, metric_index, y_first, y_second, x_part, parts[0], pair, other],
        [SMEM] * 3 + [VMEM] * 6,
        [field.shape],
        "wall",
        [(depth, 2 * rows * depth), y_first.shape],
    )
    (result,) = call(
        functools.partial(finish_kernel, comps),
        [mask, total] + returned,
        [VMEM] * (quad + 1),
        [field.shape],
        "finish",
    )
    return result.reshape(velocity.shape)


def solution(mesh):
    in_specs = (P(None, "row", "col", None), P(), P(), P(), P(), P(), P(), P(), P(), P())
    out_specs = P(None, "row", "col", None)
    return jax.shard_map(local, mesh=mesh, in_specs=in_specs, out_specs=out_specs, check_vma=False)
```

```python
import functools
import math

import jax
import jax.numpy as jnp
from jax import lax
from jax.experimental import pallas as pl
from jax.experimental.pallas import tpu as pltpu
from jax.sharding import PartitionSpec as P

viscosity = 0.4
quad = 4

VMEM = pltpu.VMEM
SMEM = pltpu.SMEM


def halves(value):
    high = value.astype(jnp.bfloat16)
    low = (value - high.astype(jnp.float32)).astype(jnp.bfloat16)
    return high, low


def dot_split(left, right, transposed=False):
    dims = (((1,), (1 if transposed else 0,)), ((), ()))
    mul = functools.partial(lax.dot_general, dimension_numbers=dims, preferred_element_type=jnp.float32)
    lh, ll = halves(left)
    rh, rl = halves(right)
    return mul(lh, rh) + (mul(lh, rl) + mul(ll, rh))


def fan(cols):
    return max(quad, cols // quad)


def span_kernel(comps, count, matrix, field, *refs):
    parts, pair = refs[-count - 1 : -1], refs[-1]
    pair[0] = field[...]
    for i in range(1, pair.shape[0]):
        pair[i] = refs[i - 1][...]
    sources = (field,) + refs[pair.shape[0] - 1 : -count - 1]
    depth, length = field.shape[0] // comps, field.shape[1]
    group = matrix.shape[0] // count
    right = []
    for comp in range(comps):
        for at in range(0, depth, group):
            stack = [source[comp * depth + at : comp * depth + at + group] for source in sources]
            stack += [value * source[2 * depth + at : 2 * depth + at + group] for value, source in zip(stack, sources)]
            right.append(jnp.concatenate(stack, axis=0))
    result = dot_split(matrix[...], jnp.concatenate(right, axis=1))
    for t in range(count):
        for i in range(len(right)):
            parts[t][i * group : (i + 1) * group] = result[
                t * group : (t + 1) * group, i * length : (i + 1) * length
            ]


def circulant_rows(row, length):
    return pltpu.roll(jnp.broadcast_to(row, (length, length)), 0, 1, stride=1, stride_axis=0)


def stream_kernel(
    cols, comps, zloc, wall_counts, z_first, z_second, field, x_first, x_second, x_part, z_matrix, mask
):
    depth = mask.shape[0]
    length = field.shape[1]
    count = wall_counts[lax.axis_index("row")]
    mask[...] = (lax.broadcasted_iota(jnp.int32, mask.shape, 0) // zloc < count).astype(jnp.float32)

    cells_z = cols * zloc
    shape = z_matrix.shape
    half = shape[1] // 2
    group = half // fan(cols)
    mine = lax.axis_index("col")
    odd = lax.axis_index("row") % 2
    wide = cols // quad
    far_step, far_count = jnp.where(odd == 0, quad, 1), jnp.where(odd == 0, wide, quad)
    near_step, near_count = jnp.where(odd == 0, 1, quad), jnp.where(odd == 0, quad, wide)
    r = lax.broadcasted_iota(jnp.int32, shape, 0)
    q = lax.broadcasted_iota(jnp.int32, shape, 1)
    q = jnp.where(q < half, q, q - half)
    t, s = r // group, q // group
    out_cell = ((near_step * t) ^ mine) * zloc + r % zloc
    in_cell = ((far_step * s) ^ mine) * zloc + q % zloc
    used = (t < near_count) & (s < far_count) & ((r % group) // zloc == (q % group) // zloc)
    gap = jnp.where(used, (in_cell - out_cell + cells_z) % cells_z, -1)
    kind = lax.broadcasted_iota(jnp.int32, (1, shape[1]), 1) < half

    def fill(k, total):
        value = jnp.where(kind, viscosity * z_second[k], -z_first[k])
        return jnp.where(gap == k, value, total)

    z_matrix[...] = lax.fori_loop(0, cells_z, fill, jnp.zeros(shape, jnp.float32), unroll=8)

    u = field[...]
    lead = u[:depth]
    left = jnp.concatenate(
        [u, jnp.concatenate([lead * u[c * depth : (c + 1) * depth] for c in range(comps)], axis=0)], axis=1
    )
    right = jnp.concatenate(
        [viscosity * circulant_rows(x_second[...], length), -circulant_rows(x_first[...], length)], axis=1
    )
    x_part[...] = dot_split(left, right, transposed=True)


def wall_kernel(
    rows,
    comps,
    zloc,
    wall_counts,
    metric_table,
    metric_index,
    y_first,
    y_second,
    x_part,
    z_part,
    ours,
    theirs,
    out,
    matrix,
    scaled,
):
    depth = x_part.shape[0] // comps
    cells = y_first.shape[0]

    def scale(j, carry):
        scaled[pl.ds(j, 1), :] = y_first[pl.ds(j, 1), :] * -metric_table[metric_index[j]]
        return carry

    lax.fori_loop(0, cells, scale, 0, unroll=8)
    me = lax.axis_index("row")

    def start_of(index):
        return lax.fori_loop(0, rows, lambda i, acc: acc + jnp.where(i < index, wall_counts[i], 0), 0, unroll=True)

    own = lax.broadcasted_iota(jnp.int32, (depth, cells), 0) // zloc
    cell = lax.broadcasted_iota(jnp.int32, (depth, cells), 1)
    mine = ((own < wall_counts[me]) & (own + start_of(me) == cell)).astype(jnp.float32)
    exact = functools.partial(
        lax.dot_general, precision=lax.Precision.HIGHEST, preferred_element_type=jnp.float32
    )
    plain = (((1,), (0,)), ((), ()))
    turned = (((1,), (1,)), ((), ()))
    both = [exact(mine, viscosity * y_second[...], plain), exact(mine, scaled[...], plain)]
    r = lax.broadcasted_iota(jnp.int32, (depth, depth), 0) % zloc
    q = lax.broadcasted_iota(jnp.int32, (depth, depth), 1) % zloc
    match = r == q
    for b in range(rows):
        other = me ^ (2 * b if b < rows // 2 else 2 * b + 1 - rows)
        spots = ((own < wall_counts[other]) & (own + start_of(other) == cell)).astype(jnp.float32)
        for k in range(2):
            block = jnp.where(match, exact(both[k], spots, turned), 0.0)
            matrix[:, (2 * b + k) * depth : (2 * b + k + 1) * depth] = block

    for comp in range(comps):
        at = slice(comp * depth, (comp + 1) * depth)
        stack = []
        for fields in (ours, theirs):
            for i in range(fields.shape[0]):
                value = fields[i, at]
                stack += [value, fields[i, depth : 2 * depth] * value]
        out[at] = x_part[at] + z_part[at] + dot_split(matrix[...], jnp.concatenate(stack, axis=0))


def finish_kernel(comps, mask, *refs):
    parts, out = refs[:-1], refs[-1]
    depth = mask.shape[0]
    for comp in range(comps):
        at = slice(comp * depth, (comp + 1) * depth)
        out[at] = jnp.where(mask[...] > 0, sum(part[at] for part in parts[1:]) + parts[0][at], 0.0)


def call(kernel, operands, spaces, results, name, scratch=()):
    results = [jax.ShapeDtypeStruct(shape, jnp.float32) for shape in results]
    held = sum(4 * math.prod(array.shape) for array in list(operands) + results)
    return pl.pallas_call(
        kernel,
        out_shape=results,
        in_specs=[pl.BlockSpec(memory_space=space) for space in spaces],
        out_specs=[pl.BlockSpec(memory_space=VMEM)] * len(results),
        scratch_shapes=[pltpu.VMEM(shape, jnp.float32) for shape in scratch],
        compiler_params=pltpu.CompilerParams(vmem_limit_bytes=(4 << 20) + 3 * held),
        name=name,
    )(*operands)


def local(
    velocity,
    wall_counts,
    x_first,
    x_second,
    y_first,
    y_second,
    z_first,
    z_second,
    metric_table,
    metric_index,
):
    rows = lax.axis_size("row")
    cols = lax.axis_size("col")
    comps, slots, zloc, length = velocity.shape
    depth = slots * zloc
    field = velocity.reshape(comps * depth, length)
    group = min(depth, 32)
    count = fan(cols)

    def along(value, index, steps):
        limits = [cols // quad if step == quad else quad for step in steps]
        return lax.ppermute(
            value,
            ("row", "col"),
            [
                (r * cols + c, r * cols + (c ^ (steps[r % 2] * index)))
                for r in range(rows)
                for c in range(cols)
                if index < limits[r % 2]
            ],
        )

    def across(value, step):
        return lax.ppermute(value, "row", [(i, i ^ step) for i in range(rows)])

    gathered = [along(field, i, (quad, 1)) for i in range(1, count)]
    far = [across(field, step) for step in range(2, rows, 2)]
    x_part, z_matrix, mask = call(
        functools.partial(stream_kernel, cols, comps, zloc),
        [wall_counts, z_first, z_second, field, x_first.reshape(1, length), x_second.reshape(1, length)],
        [SMEM] * 3 + [VMEM] * 3,
        [field.shape, (count * group, 2 * count * group), (depth, length)],
        "stream",
    )
    *parts, pair = call(
        functools.partial(span_kernel, comps, count),
        [z_matrix, field] + far + gathered,
        [VMEM] * (rows // 2 + count),
        [field.shape] * count + [(rows // 2,) + field.shape],
        "span",
    )
    returned = [along(parts[t], t, (1, quad)) for t in range(1, count)]
    other = across(pair, 1)
    (total,) = call(
        functools.partial(wall_kernel, rows, comps, zloc),
        [wall_counts, metric_table, metric_index, y_first, y_second, x_part, parts[0], pair, other],
        [SMEM] * 3 + [VMEM] * 6,
        [field.shape],
        "wall",
        [(depth, 2 * rows * depth), y_first.shape],
    )
    (result,) = call(
        functools.partial(finish_kernel, comps),
        [mask, total] + returned,
        [VMEM] * (count + 1),
        [field.shape],
        "finish",
    )
    return result.reshape(velocity.shape)


def solution(mesh):
    in_specs = (P(None, "row", "col", None), P(), P(), P(), P(), P(), P(), P(), P(), P())
    out_specs = P(None, "row", "col", None)
    return jax.shard_map(local, mesh=mesh, in_specs=in_specs, out_specs=out_specs, check_vma=False)
```

```python
import functools
import math

import jax
import jax.numpy as jnp
from jax import lax
from jax.experimental import pallas as pl
from jax.experimental.pallas import tpu as pltpu
from jax.sharding import PartitionSpec as P

viscosity = 0.4
quad = 4

VMEM = pltpu.VMEM
SMEM = pltpu.SMEM


def halves(value):
    high = value.astype(jnp.bfloat16)
    low = (value - high.astype(jnp.float32)).astype(jnp.bfloat16)
    return high, low


def dot_split(left, right, transposed=False):
    dims = (((1,), (1 if transposed else 0,)), ((), ()))
    mul = functools.partial(lax.dot_general, dimension_numbers=dims, preferred_element_type=jnp.float32)
    lh, ll = halves(left)
    rh, rl = halves(right)
    return mul(lh, rh) + (mul(lh, rl) + mul(ll, rh))


def fan(cols):
    return max(quad, cols // quad)


def span_kernel(comps, count, matrix, field, *refs):
    parts, pair = refs[-count - 1 : -1], refs[-1]
    pair[0] = field[...]
    for i in range(1, pair.shape[0]):
        pair[i] = refs[i - 1][...]
    sources = (field,) + refs[pair.shape[0] - 1 : -count - 1]
    depth, length = field.shape[0] // comps, field.shape[1]
    group = matrix.shape[0] // count
    right = []
    for comp in range(comps):
        for at in range(0, depth, group):
            stack = [source[comp * depth + at : comp * depth + at + group] for source in sources]
            stack += [value * source[2 * depth + at : 2 * depth + at + group] for value, source in zip(stack, sources)]
            right.append(jnp.concatenate(stack, axis=0))
    result = dot_split(matrix[...], jnp.concatenate(right, axis=1))
    for t in range(count):
        for i in range(len(right)):
            parts[t][i * group : (i + 1) * group] = result[
                t * group : (t + 1) * group, i * length : (i + 1) * length
            ]


def circulant_rows(row, length):
    return pltpu.roll(jnp.broadcast_to(row, (length, length)), 0, 1, stride=1, stride_axis=0)


def stream_kernel(
    cols, comps, zloc, wall_counts, z_first, z_second, field, x_first, x_second, x_part, z_matrix, mask
):
    depth = mask.shape[0]
    length = field.shape[1]
    count = wall_counts[lax.axis_index("row")]
    mask[...] = (lax.broadcasted_iota(jnp.int32, mask.shape, 0) // zloc < count).astype(jnp.float32)

    cells_z = cols * zloc
    shape = z_matrix.shape
    half = shape[1] // 2
    group = half // fan(cols)
    mine = lax.axis_index("col")
    odd = lax.axis_index("row") % 2
    wide = cols // quad
    far_step, far_count = jnp.where(odd == 0, quad, 1), jnp.where(odd == 0, wide, quad)
    near_step, near_count = jnp.where(odd == 0, 1, quad), jnp.where(odd == 0, quad, wide)
    r = lax.broadcasted_iota(jnp.int32, shape, 0)
    q = lax.broadcasted_iota(jnp.int32, shape, 1)
    q = jnp.where(q < half, q, q - half)
    t, s = r // group, q // group
    out_cell = ((near_step * t) ^ mine) * zloc + r % zloc
    in_cell = ((far_step * s) ^ mine) * zloc + q % zloc
    used = (t < near_count) & (s < far_count) & ((r % group) // zloc == (q % group) // zloc)
    gap = jnp.where(used, (in_cell - out_cell + cells_z) % cells_z, -1)
    kind = lax.broadcasted_iota(jnp.int32, (1, shape[1]), 1) < half

    def fill(k, total):
        value = jnp.where(kind, viscosity * z_second[k], -z_first[k])
        return jnp.where(gap == k, value, total)

    z_matrix[...] = lax.fori_loop(0, cells_z, fill, jnp.zeros(shape, jnp.float32), unroll=8)

    u = field[...]
    lead = u[:depth]
    left = jnp.concatenate(
        [u, jnp.concatenate([lead * u[c * depth : (c + 1) * depth] for c in range(comps)], axis=0)], axis=1
    )
    right = jnp.concatenate(
        [viscosity * circulant_rows(x_second[...], length), -circulant_rows(x_first[...], length)], axis=1
    )
    x_part[...] = dot_split(left, right, transposed=True)


def wall_kernel(
    rows,
    comps,
    zloc,
    wall_counts,
    metric_table,
    metric_index,
    y_first,
    y_second,
    x_part,
    z_part,
    ours,
    theirs,
    out,
    matrix,
    scaled,
):
    depth = x_part.shape[0] // comps
    cells = y_first.shape[0]

    def scale(j, carry):
        scaled[pl.ds(j, 1), :] = y_first[pl.ds(j, 1), :] * -metric_table[metric_index[j]]
        return carry

    lax.fori_loop(0, cells, scale, 0, unroll=8)
    me = lax.axis_index("row")

    def start_of(index):
        return lax.fori_loop(0, rows, lambda i, acc: acc + jnp.where(i < index, wall_counts[i], 0), 0, unroll=True)

    own = lax.broadcasted_iota(jnp.int32, (depth, cells), 0) // zloc
    cell = lax.broadcasted_iota(jnp.int32, (depth, cells), 1)
    mine = ((own < wall_counts[me]) & (own + start_of(me) == cell)).astype(jnp.float32)
    exact = functools.partial(
        lax.dot_general, precision=lax.Precision.HIGHEST, preferred_element_type=jnp.float32
    )
    plain = (((1,), (0,)), ((), ()))
    turned = (((1,), (1,)), ((), ()))
    both = [exact(mine, viscosity * y_second[...], plain), exact(mine, scaled[...], plain)]
    r = lax.broadcasted_iota(jnp.int32, (depth, depth), 0) % zloc
    q = lax.broadcasted_iota(jnp.int32, (depth, depth), 1) % zloc
    match = r == q
    for b in range(rows):
        other = me ^ (2 * b if b < rows // 2 else 2 * b + 1 - rows)
        spots = ((own < wall_counts[other]) & (own + start_of(other) == cell)).astype(jnp.float32)
        for k in range(2):
            block = jnp.where(match, exact(both[k], spots, turned), 0.0)
            matrix[:, (2 * b + k) * depth : (2 * b + k + 1) * depth] = block

    for comp in range(comps):
        at = slice(comp * depth, (comp + 1) * depth)
        stack = []
        for fields in (ours, theirs):
            for i in range(fields.shape[0]):
                value = fields[i, at]
                stack += [value, fields[i, depth : 2 * depth] * value]
        out[at] = x_part[at] + z_part[at] + dot_split(matrix[...], jnp.concatenate(stack, axis=0))


def finish_kernel(comps, mask, *refs):
    parts, out = refs[:-1], refs[-1]
    depth = mask.shape[0]
    for comp in range(comps):
        at = slice(comp * depth, (comp + 1) * depth)
        out[at] = jnp.where(mask[...] > 0, sum(part[at] for part in parts[1:]) + parts[0][at], 0.0)


def call(kernel, operands, spaces, results, name, scratch=()):
    results = [jax.ShapeDtypeStruct(shape, jnp.float32) for shape in results]
    held = sum(4 * math.prod(array.shape) for array in list(operands) + results)
    return pl.pallas_call(
        kernel,
        out_shape=results,
        in_specs=[pl.BlockSpec(memory_space=space) for space in spaces],
        out_specs=[pl.BlockSpec(memory_space=VMEM)] * len(results),
        scratch_shapes=[pltpu.VMEM(shape, jnp.float32) for shape in scratch],
        compiler_params=pltpu.CompilerParams(vmem_limit_bytes=(4 << 20) + 3 * held),
        name=name,
    )(*operands)


def local(
    velocity,
    wall_counts,
    x_first,
    x_second,
    y_first,
    y_second,
    z_first,
    z_second,
    metric_table,
    metric_index,
):
    rows = lax.axis_size("row")
    cols = lax.axis_size("col")
    comps, slots, zloc, length = velocity.shape
    depth = slots * zloc
    field = velocity.reshape(comps * depth, length)
    group = min(depth, 32)
    count = fan(cols)

    def along(value, index, steps):
        limits = [cols // quad if step == quad else quad for step in steps]
        return lax.ppermute(
            value,
            ("row", "col"),
            [
                (r * cols + c, r * cols + (c ^ (steps[r % 2] * index if index < limits[r % 2] else 0)))
                for r in range(rows)
                for c in range(cols)
            ],
        )

    def across(value, step):
        return lax.ppermute(value, "row", [(i, i ^ step) for i in range(rows)])

    gathered = [along(field, i, (quad, 1)) for i in range(1, count)]
    far = [across(field, step) for step in range(2, rows, 2)]
    x_part, z_matrix, mask = call(
        functools.partial(stream_kernel, cols, comps, zloc),
        [wall_counts, z_first, z_second, field, x_first.reshape(1, length), x_second.reshape(1, length)],
        [SMEM] * 3 + [VMEM] * 3,
        [field.shape, (count * group, 2 * count * group), (depth, length)],
        "stream",
    )
    *parts, pair = call(
        functools.partial(span_kernel, comps, count),
        [z_matrix, field] + far + gathered,
        [VMEM] * (rows // 2 + count),
        [field.shape] * count + [(rows // 2,) + field.shape],
        "span",
    )
    returned = [along(parts[t], t, (1, quad)) for t in range(1, count)]
    other = across(pair, 1)
    (total,) = call(
        functools.partial(wall_kernel, rows, comps, zloc),
        [wall_counts, metric_table, metric_index, y_first, y_second, x_part, parts[0], pair, other],
        [SMEM] * 3 + [VMEM] * 6,
        [field.shape],
        "wall",
        [(depth, 2 * rows * depth), y_first.shape],
    )
    (result,) = call(
        functools.partial(finish_kernel, comps),
        [mask, total] + returned,
        [VMEM] * (count + 1),
        [field.shape],
        "finish",
    )
    return result.reshape(velocity.shape)


def solution(mesh):
    in_specs = (P(None, "row", "col", None), P(), P(), P(), P(), P(), P(), P(), P(), P())
    out_specs = P(None, "row", "col", None)
    return jax.shard_map(local, mesh=mesh, in_specs=in_specs, out_specs=out_specs, check_vma=False)
```

```python
import functools
import math

import jax
import jax.numpy as jnp
from jax import lax
from jax.experimental import pallas as pl
from jax.experimental.pallas import tpu as pltpu
from jax.sharding import PartitionSpec as P

viscosity = 0.4
quad = 4

VMEM = pltpu.VMEM
SMEM = pltpu.SMEM


def halves(value):
    high = value.astype(jnp.bfloat16)
    low = (value - high.astype(jnp.float32)).astype(jnp.bfloat16)
    return high, low


def by_parity(odd, pair):
    return jnp.where(odd == 1, *reversed(pair))


def dot_split(left, right, transposed=False):
    dims = (((1,), (1 if transposed else 0,)), ((), ()))
    mul = functools.partial(lax.dot_general, dimension_numbers=dims, preferred_element_type=jnp.float32)
    lh, ll = halves(left)
    rh, rl = halves(right)
    return mul(lh, rh) + (mul(lh, rl) + mul(ll, rh))


def span_kernel(comps, hand_on, matrix, field, *refs):
    count = len(hand_on)
    sources, parts = (field,) + refs[-count - 1 :: -1], refs[-count:]
    odd = lax.axis_index("row") % 2
    depth, length = field.shape[0] // comps, field.shape[1]
    group = matrix.shape[0] // count
    right = []
    for comp in range(comps):
        for at in range(0, depth, group):
            stack = [source[comp * depth + at : comp * depth + at + group] for source in sources]
            stack += [value * source[2 * depth + at : 2 * depth + at + group] for value, source in zip(stack, sources)]
            right.append(jnp.concatenate(stack, axis=0))
    result = dot_split(matrix[...], jnp.concatenate(right, axis=1))
    for t in range(count):
        for i in range(len(right)):
            at = slice(i * group, (i + 1) * group)
            value = result[t * group : (t + 1) * group, i * length : (i + 1) * length]
            if any(hand_on[t]):
                value = jnp.where(by_parity(odd, hand_on[t]), field[at], value)
            parts[t][at] = value


def circulant_rows(row, length):
    return pltpu.roll(jnp.broadcast_to(row, (length, length)), 0, 1, stride=1, stride_axis=0)


def stream_kernel(
    cols, comps, zloc, wall_counts, z_first, z_second, field, x_first, x_second, x_part, z_matrix, mask
):
    depth = mask.shape[0]
    length = field.shape[1]
    count = wall_counts[lax.axis_index("row")]
    mask[...] = (lax.broadcasted_iota(jnp.int32, mask.shape, 0) // zloc < count).astype(jnp.float32)

    cells_z = cols * zloc
    shape = z_matrix.shape
    half = shape[1] // 2
    group = half // max(quad, cols // quad)
    mine = lax.axis_index("col")
    odd = lax.axis_index("row") % 2
    r = lax.broadcasted_iota(jnp.int32, shape, 0)
    q = lax.broadcasted_iota(jnp.int32, shape, 1)
    q = jnp.where(q < half, q, q - half)
    t, s = r // group, q // group
    into = by_parity(odd, (inner_step(t), quad * t))
    outof = by_parity(odd, (quad * s, inner_step(s)))
    out_cell = (into ^ mine) * zloc + r % zloc
    in_cell = (outof ^ mine) * zloc + q % zloc
    used = (t < by_parity(odd, (quad, cols // quad))) & (s < by_parity(odd, (cols // quad, quad)))
    used &= (r % group) // zloc == (q % group) // zloc
    gap = jnp.where(used, (in_cell - out_cell + cells_z) % cells_z, -1)
    kind = lax.broadcasted_iota(jnp.int32, (1, shape[1]), 1) < half

    def fill(k, total):
        value = jnp.where(kind, viscosity * z_second[k], -z_first[k])
        return jnp.where(gap == k, value, total)

    z_matrix[...] = lax.fori_loop(0, cells_z, fill, jnp.zeros(shape, jnp.float32), unroll=8)

    u = field[...]
    lead = u[:depth]
    left = jnp.concatenate(
        [u, jnp.concatenate([lead * u[c * depth : (c + 1) * depth] for c in range(comps)], axis=0)], axis=1
    )
    right = jnp.concatenate(
        [viscosity * circulant_rows(x_second[...], length), -circulant_rows(x_first[...], length)], axis=1
    )
    x_part[...] = dot_split(left, right, transposed=True)


def wall_matrix_kernel(rows, zloc, wall_counts, metric_table, metric_index, y_first, y_second, after, matrix):
    cells = y_first.shape[0]
    depth = matrix.shape[0] // 2
    me = lax.axis_index("row")
    plain = functools.partial(
        lax.dot_general, dimension_numbers=(((1,), (0,)), ((), ())), preferred_element_type=jnp.float32
    )
    turned = functools.partial(
        lax.dot_general, dimension_numbers=(((1,), (1,)), ((), ())), preferred_element_type=jnp.float32
    )

    def spots(index):
        start = lax.fori_loop(0, rows, lambda i, acc: acc + jnp.where(i < index, wall_counts[i], 0), 0, unroll=True)
        plane = lax.broadcasted_iota(jnp.int32, (depth, cells), 0) // zloc
        cell = lax.broadcasted_iota(jnp.int32, (depth, cells), 1)
        return ((plane < wall_counts[index]) & (plane + start == cell)).astype(jnp.float32)

    levels = metric_table.shape[1]
    entry = (lax.broadcasted_iota(jnp.int32, (levels, cells), 0) == metric_index[...]).astype(jnp.float32)
    table = jnp.broadcast_to(metric_table[...], (8, levels))
    metric = plain(table, entry, precision=lax.Precision.HIGHEST)[:1]
    ends = jnp.concatenate([spots(me), spots(me ^ 1)], axis=0)
    scale = jnp.sum(ends * metric, axis=1, keepdims=True)
    pick = ends.astype(jnp.bfloat16)
    second = sum(plain(pick, part) for part in halves(viscosity * y_second[...]))
    first = -scale * sum(plain(pick, part) for part in halves(y_first[...]))
    other = jnp.concatenate([spots(me ^ step) for step in range(0, rows, 2)], axis=0).astype(jnp.bfloat16)
    wide = sum(turned(part, other) for part in halves(jnp.concatenate([second, first], axis=0)))
    match = lax.broadcasted_iota(jnp.int32, wide.shape, 0) % zloc == lax.broadcasted_iota(jnp.int32, wide.shape, 1) % zloc
    wide = jnp.where(match, wide, 0.0)
    for b in range(rows // 2):
        for k in range(2):
            matrix[:, (2 * b + k) * depth : (2 * b + k + 1) * depth] = wide[
                2 * k * depth : 2 * (k + 1) * depth, b * depth : (b + 1) * depth
            ]


def wall_kernel(comps, matrix, x_part, z_part, field, *refs):
    far, (total, away) = refs[:-2], refs[-2:]
    odd = lax.axis_index("row") % 2
    depth = x_part.shape[0] // comps
    fields = [field[...]] + [by_parity(odd, (even[...], other[...])) for even, other in zip(far[::2], far[1::2])]
    for comp in range(comps):
        at = slice(comp * depth, (comp + 1) * depth)
        stack = []
        for value in fields:
            stack += [value[at], value[depth : 2 * depth] * value[at]]
        result = dot_split(matrix[...], jnp.concatenate(stack, axis=0))
        total[at] = x_part[at] + z_part[at] + result[:depth]
        away[at] = result[depth:]


def finish_kernel(comps, use, mask, total, near, *refs):
    parts, out = refs[:-1], refs[-1]
    odd = lax.axis_index("row") % 2
    depth = mask.shape[0]
    for comp in range(comps):
        at = slice(comp * depth, (comp + 1) * depth)
        value = total[at] + near[at]
        for part, pair in zip(parts, use):
            value += part[at] if all(pair) else jnp.where(by_parity(odd, pair), part[at], 0.0)
        out[at] = jnp.where(mask[...] > 0, value, 0.0)


def inner_step(index):
    return (quad - index) % quad


def plan(rows, cols):
    wide = cols // quad
    steps = {"outer": [quad * i for i in range(1, wide)], "inner": [inner_step(i) for i in range(1, quad)]}
    order = (("outer", "inner"), ("inner", "outer"))
    count = max(wide, quad) - 1
    stages = [[[None, None] for _ in range(count)] for _ in range(2)] + [[]]
    found = []
    for parity in range(2):
        wanted = list(range(2, rows, 2))
        spots = {}
        for stage in range(2):
            own = steps[order[parity][stage]]
            for i in range(count):
                if i < len(own):
                    stages[stage][i][parity] = ("col", own[i])
                else:
                    step = wanted.pop(0) if wanted else None
                    stages[stage][i][parity] = ("row", step or 2)
                    if step:
                        spots[step] = (stage, i)
        for i, step in enumerate(wanted):
            if i == len(stages[2]):
                stages[2].append([("row", 2), ("row", 2)])
            stages[2][i][parity] = ("row", step)
            spots[step] = (2, i)
        found.append(spots)
    return stages, found


def call(kernel, operands, spaces, results, name, scratch=()):
    results = [jax.ShapeDtypeStruct(shape, jnp.float32) for shape in results]
    held = sum(4 * math.prod(array.shape) for array in list(operands) + results)
    return pl.pallas_call(
        kernel,
        out_shape=results,
        in_specs=[pl.BlockSpec(memory_space=space) for space in spaces],
        out_specs=[pl.BlockSpec(memory_space=VMEM)] * len(results),
        scratch_shapes=[pltpu.VMEM(shape, jnp.float32) for shape in scratch],
        compiler_params=pltpu.CompilerParams(vmem_limit_bytes=(4 << 20) + 3 * held),
        name=name,
    )(*operands)


def local(
    velocity,
    wall_counts,
    x_first,
    x_second,
    y_first,
    y_second,
    z_first,
    z_second,
    metric_table,
    metric_index,
):
    rows = lax.axis_size("row")
    cols = lax.axis_size("col")
    comps, slots, zloc, length = velocity.shape
    depth = slots * zloc
    field = velocity.reshape(comps * depth, length)
    group = min(depth, 32)
    stages, found = plan(rows, cols)
    count = len(stages[0]) + 1

    def trade(value, moves):
        pairs = []
        for r in range(rows):
            for c in range(cols):
                axis, step = moves[r % 2]
                to = (r ^ step, c) if axis == "row" else (r, c ^ step)
                pairs.append((r * cols + c, to[0] * cols + to[1]))
        return lax.ppermute(value, ("row", "col"), pairs)

    gathered = [trade(field, moves) for moves in stages[0]]
    extra = [trade(field, moves) for moves in stages[2]]
    x_part, z_matrix, mask = call(
        functools.partial(stream_kernel, cols, comps, zloc),
        [wall_counts, z_first, z_second, field, x_first.reshape(1, length), x_second.reshape(1, length)],
        [SMEM] * 3 + [VMEM] * 3,
        [field.shape, (count * group, 2 * count * group), (depth, length)],
        "stream",
    )
    hand_on = [(False, False)] + [
        tuple((1, i) in found[parity].values() for parity in range(2)) for i in range(count - 1)
    ]
    parts = call(
        functools.partial(span_kernel, comps, hand_on),
        [z_matrix, field] + gathered[::-1],
        [VMEM] * (count + 1),
        [field.shape] * count,
        "span",
    )
    returned = [trade(part, moves) for part, moves in zip(parts[1:], stages[1])]
    (y_matrix,) = call(
        functools.partial(wall_matrix_kernel, rows, zloc),
        [wall_counts, metric_table.reshape(1, -1), metric_index.reshape(1, -1), y_first, y_second, parts[0]],
        [SMEM] + [VMEM] * 4 + [pl.ANY],
        [(2 * depth, rows * depth)],
        "wall_matrix",
    )
    arrived = (gathered, returned, extra)
    far = [arrived[stage][i] for step in range(2, rows, 2) for stage, i in (found[0][step], found[1][step])]
    total, away = call(
        functools.partial(wall_kernel, comps),
        [y_matrix, x_part, parts[0], field] + far,
        [VMEM] * (4 + len(far)),
        [field.shape] * 2,
        "wall",
    )
    near = trade(away, (("row", 1), ("row", 1)))
    use = [tuple(moves[parity][0] == "col" for parity in range(2)) for moves in stages[1]]
    (result,) = call(
        functools.partial(finish_kernel, comps, use),
        [mask, total, near] + returned,
        [VMEM] * (count + 2),
        [field.shape],
        "finish",
    )
    return result.reshape(velocity.shape)


def solution(mesh):
    in_specs = (P(None, "row", "col", None), P(), P(), P(), P(), P(), P(), P(), P(), P())
    out_specs = P(None, "row", "col", None)
    return jax.shard_map(local, mesh=mesh, in_specs=in_specs, out_specs=out_specs, check_vma=False)
```

```python
import functools
import math

import jax
import jax.numpy as jnp
from jax import lax
from jax.experimental import pallas as pl
from jax.experimental.pallas import tpu as pltpu
from jax.sharding import PartitionSpec as P

viscosity = 0.4
quad = 4

VMEM = pltpu.VMEM
SMEM = pltpu.SMEM


def halves(value):
    high = value.astype(jnp.bfloat16)
    low = (value - high.astype(jnp.float32)).astype(jnp.bfloat16)
    return high, low


def dot_split(left, right, transposed=False):
    dims = (((1,), (1 if transposed else 0,)), ((), ()))
    mul = functools.partial(lax.dot_general, dimension_numbers=dims, preferred_element_type=jnp.float32)
    lh, ll = halves(left)
    rh, rl = halves(right)
    return mul(lh, rh) + (mul(lh, rl) + mul(ll, rh))


def span_kernel(comps, sources, matrix, *refs):
    fields, parts = refs[:sources], refs[-quad:]
    depth, length = fields[0].shape[0] // comps, fields[0].shape[1]
    group = matrix.shape[0] // quad
    right = []
    for comp in range(comps):
        for at in range(0, depth, group):
            stack = [field[comp * depth + at : comp * depth + at + group] for field in fields]
            stack += [value * field[2 * depth + at : 2 * depth + at + group] for value, field in zip(stack, fields)]
            right.append(jnp.concatenate(stack, axis=0))
    result = dot_split(matrix[...], jnp.concatenate(right, axis=1))
    for t in range(quad):
        for i in range(len(right)):
            parts[t][i * group : (i + 1) * group] = result[
                t * group : (t + 1) * group, i * length : (i + 1) * length
            ]


def circulant_rows(row, length):
    return pltpu.roll(jnp.broadcast_to(row, (length, length)), 0, 1, stride=1, stride_axis=0)


def stream_kernel(
    cols, comps, zloc, wall_counts, z_first, z_second, field, x_first, x_second, x_part, z_matrix, mask
):
    depth = mask.shape[0]
    length = field.shape[1]
    count = wall_counts[lax.axis_index("row")]
    mask[...] = (lax.broadcasted_iota(jnp.int32, mask.shape, 0) // zloc < count).astype(jnp.float32)

    cells_z = cols * zloc
    shape = z_matrix.shape
    half = shape[1] // 2
    group = shape[0] // quad
    mine = lax.axis_index("col")
    r = lax.broadcasted_iota(jnp.int32, shape, 0)
    q = lax.broadcasted_iota(jnp.int32, shape, 1)
    q = jnp.where(q < half, q, q - half)
    out_cell = ((r // group) ^ mine) * zloc + r % zloc
    in_cell = ((quad * (q // group)) ^ mine) * zloc + q % zloc
    same = (r % group) // zloc == (q % group) // zloc
    gap = jnp.where(same, (in_cell - out_cell + cells_z) % cells_z, -1)
    kind = lax.broadcasted_iota(jnp.int32, (1, shape[1]), 1) < half

    def fill(k, total):
        value = jnp.where(kind, viscosity * z_second[k], -z_first[k])
        return jnp.where(gap == k, value, total)

    z_matrix[...] = lax.fori_loop(0, cells_z, fill, jnp.zeros(shape, jnp.float32), unroll=8)

    u = field[...]
    lead = u[:depth]
    left = jnp.concatenate(
        [u, jnp.concatenate([lead * u[c * depth : (c + 1) * depth] for c in range(comps)], axis=0)], axis=1
    )
    right = jnp.concatenate(
        [viscosity * circulant_rows(x_second[...], length), -circulant_rows(x_first[...], length)], axis=1
    )
    x_part[...] = dot_split(left, right, transposed=True)


def wall_matrix_kernel(rows, zloc, wall_counts, metric_table, metric_index, y_first, y_second, after, matrix):
    cells = y_first.shape[0]
    depth = matrix.shape[0] // 2
    me = lax.axis_index("row")
    plain = functools.partial(
        lax.dot_general, dimension_numbers=(((1,), (0,)), ((), ())), preferred_element_type=jnp.float32
    )
    turned = functools.partial(
        lax.dot_general, dimension_numbers=(((1,), (1,)), ((), ())), preferred_element_type=jnp.float32
    )

    def spots(index):
        start = lax.fori_loop(0, rows, lambda i, acc: acc + jnp.where(i < index, wall_counts[i], 0), 0, unroll=True)
        plane = lax.broadcasted_iota(jnp.int32, (depth, cells), 0) // zloc
        cell = lax.broadcasted_iota(jnp.int32, (depth, cells), 1)
        return ((plane < wall_counts[index]) & (plane + start == cell)).astype(jnp.float32)

    levels = metric_table.shape[1]
    entry = (lax.broadcasted_iota(jnp.int32, (levels, cells), 0) == metric_index[...]).astype(jnp.float32)
    table = jnp.broadcast_to(metric_table[...], (8, levels))
    metric = plain(table, entry, precision=lax.Precision.HIGHEST)[:1]
    ends = jnp.concatenate([spots(me), spots(me ^ 1)], axis=0)
    scale = jnp.sum(ends * metric, axis=1, keepdims=True)
    pick = ends.astype(jnp.bfloat16)
    second = sum(plain(pick, part) for part in halves(viscosity * y_second[...]))
    first = -scale * sum(plain(pick, part) for part in halves(y_first[...]))
    other = jnp.concatenate([spots(me ^ step) for step in range(0, rows, 2)], axis=0).astype(jnp.bfloat16)
    wide = sum(turned(part, other) for part in halves(jnp.concatenate([second, first], axis=0)))
    match = lax.broadcasted_iota(jnp.int32, wide.shape, 0) % zloc == lax.broadcasted_iota(jnp.int32, wide.shape, 1) % zloc
    wide = jnp.where(match, wide, 0.0)
    for b in range(rows // 2):
        for k in range(2):
            matrix[:, (2 * b + k) * depth : (2 * b + k + 1) * depth] = wide[
                2 * k * depth : 2 * (k + 1) * depth, b * depth : (b + 1) * depth
            ]


def wall_kernel(comps, matrix, x_part, z_part, *refs):
    fields, (total, away) = refs[:-2], refs[-2:]
    depth = x_part.shape[0] // comps
    for comp in range(comps):
        at = slice(comp * depth, (comp + 1) * depth)
        stack = []
        for field in fields:
            stack += [field[at], field[depth : 2 * depth] * field[at]]
        result = dot_split(matrix[...], jnp.concatenate(stack, axis=0))
        total[at] = x_part[at] + z_part[at] + result[:depth]
        away[at] = result[depth:]


def finish_kernel(comps, mask, *refs):
    parts, out = refs[:-1], refs[-1]
    depth = mask.shape[0]
    for comp in range(comps):
        at = slice(comp * depth, (comp + 1) * depth)
        out[at] = jnp.where(mask[...] > 0, sum(part[at] for part in parts[1:]) + parts[0][at], 0.0)


def call(kernel, operands, spaces, results, name, scratch=()):
    results = [jax.ShapeDtypeStruct(shape, jnp.float32) for shape in results]
    held = sum(4 * math.prod(array.shape) for array in list(operands) + results)
    return pl.pallas_call(
        kernel,
        out_shape=results,
        in_specs=[pl.BlockSpec(memory_space=space) for space in spaces],
        out_specs=[pl.BlockSpec(memory_space=VMEM)] * len(results),
        scratch_shapes=[pltpu.VMEM(shape, jnp.float32) for shape in scratch],
        compiler_params=pltpu.CompilerParams(vmem_limit_bytes=(4 << 20) + 3 * held),
        name=name,
    )(*operands)


def local(
    velocity,
    wall_counts,
    x_first,
    x_second,
    y_first,
    y_second,
    z_first,
    z_second,
    metric_table,
    metric_index,
):
    rows = lax.axis_size("row")
    cols = lax.axis_size("col")
    comps, slots, zloc, length = velocity.shape
    depth = slots * zloc
    field = velocity.reshape(comps * depth, length)
    group = min(depth, 32)
    sources = cols // quad

    def along(value, step):
        return lax.ppermute(value, "col", [(i, i ^ step) for i in range(cols)])

    def across(value, step):
        return lax.ppermute(value, "row", [(i, i ^ step) for i in range(rows)])

    gathered = [along(field, quad * i) for i in range(1, sources)]
    far = [across(field, step) for step in range(2, rows, 2)]
    x_part, z_matrix, mask = call(
        functools.partial(stream_kernel, cols, comps, zloc),
        [wall_counts, z_first, z_second, field, x_first.reshape(1, length), x_second.reshape(1, length)],
        [SMEM] * 3 + [VMEM] * 3,
        [field.shape, (quad * group, 2 * sources * group), (depth, length)],
        "stream",
    )
    parts = call(
        functools.partial(span_kernel, comps, sources),
        [z_matrix, field] + gathered + far,
        [VMEM] * (1 + sources) + [pl.ANY] * len(far),
        [field.shape] * quad,
        "span",
    )
    returned = [along(parts[t], t) for t in reversed(range(1, quad))]
    (y_matrix,) = call(
        functools.partial(wall_matrix_kernel, rows, zloc),
        [wall_counts, metric_table.reshape(1, -1), metric_index.reshape(1, -1), y_first, y_second, parts[0]],
        [SMEM] + [VMEM] * 4 + [pl.ANY],
        [(2 * depth, rows * depth)],
        "wall_matrix",
    )
    total, away = call(
        functools.partial(wall_kernel, comps),
        [y_matrix, x_part, parts[0], field] + far,
        [VMEM] * (4 + len(far)),
        [field.shape] * 2,
        "wall",
    )
    near = across(away, 1)
    (result,) = call(
        functools.partial(finish_kernel, comps),
        [mask, total, near] + returned,
        [VMEM] * (quad + 2),
        [field.shape],
        "finish",
    )
    return result.reshape(velocity.shape)


def solution(mesh):
    in_specs = (P(None, "row", "col", None), P(), P(), P(), P(), P(), P(), P(), P(), P())
    out_specs = P(None, "row", "col", None)
    return jax.shard_map(local, mesh=mesh, in_specs=in_specs, out_specs=out_specs, check_vma=False)
```

```python
import functools
import math

import jax
import jax.numpy as jnp
from jax import lax
from jax.experimental import pallas as pl
from jax.experimental.pallas import tpu as pltpu
from jax.sharding import PartitionSpec as P

viscosity = 0.4
quad = 4

VMEM = pltpu.VMEM
SMEM = pltpu.SMEM


def halves(value):
    high = value.astype(jnp.bfloat16)
    low = (value - high.astype(jnp.float32)).astype(jnp.bfloat16)
    return high, low


def dot_split(left, right, transposed=False):
    dims = (((1,), (1 if transposed else 0,)), ((), ()))
    mul = functools.partial(lax.dot_general, dimension_numbers=dims, preferred_element_type=jnp.float32)
    lh, ll = halves(left)
    rh, rl = halves(right)
    return mul(lh, rh) + (mul(lh, rl) + mul(ll, rh))


def span_kernel(comps, sources, matrix, *refs):
    fields, parts = refs[-quad - sources : -quad], refs[-quad:]
    depth, length = fields[0].shape[0] // comps, fields[0].shape[1]
    group = matrix.shape[0] // quad
    right = []
    for comp in range(comps):
        for at in range(0, depth, group):
            stack = [field[comp * depth + at : comp * depth + at + group] for field in fields]
            stack += [value * field[2 * depth + at : 2 * depth + at + group] for value, field in zip(stack, fields)]
            right.append(jnp.concatenate(stack, axis=0))
    result = dot_split(matrix[...], jnp.concatenate(right, axis=1))
    for t in range(quad):
        for i in range(len(right)):
            parts[t][i * group : (i + 1) * group] = result[
                t * group : (t + 1) * group, i * length : (i + 1) * length
            ]


def circulant_rows(row, length):
    return pltpu.roll(jnp.broadcast_to(row, (length, length)), 0, 1, stride=1, stride_axis=0)


def stream_kernel(
    cols, comps, zloc, wall_counts, z_first, z_second, field, x_first, x_second, x_part, z_matrix, mask
):
    depth = mask.shape[0]
    length = field.shape[1]
    count = wall_counts[lax.axis_index("row")]
    mask[...] = (lax.broadcasted_iota(jnp.int32, mask.shape, 0) // zloc < count).astype(jnp.float32)

    cells_z = cols * zloc
    shape = z_matrix.shape
    half = shape[1] // 2
    group = shape[0] // quad
    mine = lax.axis_index("col")
    r = lax.broadcasted_iota(jnp.int32, shape, 0)
    q = lax.broadcasted_iota(jnp.int32, shape, 1)
    q = jnp.where(q < half, q, q - half)
    out_cell = ((r // group) ^ mine) * zloc + r % zloc
    in_cell = ((quad * (q // group)) ^ mine) * zloc + q % zloc
    same = (r % group) // zloc == (q % group) // zloc
    gap = jnp.where(same, (in_cell - out_cell + cells_z) % cells_z, -1)
    kind = lax.broadcasted_iota(jnp.int32, (1, shape[1]), 1) < half

    def fill(k, total):
        value = jnp.where(kind, viscosity * z_second[k], -z_first[k])
        return jnp.where(gap == k, value, total)

    z_matrix[...] = lax.fori_loop(0, cells_z, fill, jnp.zeros(shape, jnp.float32), unroll=8)

    u = field[...]
    lead = u[:depth]
    left = jnp.concatenate(
        [u, jnp.concatenate([lead * u[c * depth : (c + 1) * depth] for c in range(comps)], axis=0)], axis=1
    )
    right = jnp.concatenate(
        [viscosity * circulant_rows(x_second[...], length), -circulant_rows(x_first[...], length)], axis=1
    )
    x_part[...] = dot_split(left, right, transposed=True)


def wall_matrix_kernel(rows, zloc, wall_counts, metric_table, metric_index, y_first, y_second, after, matrix):
    cells = y_first.shape[0]
    depth = matrix.shape[0] // 2
    me = lax.axis_index("row")
    plain = functools.partial(
        lax.dot_general, dimension_numbers=(((1,), (0,)), ((), ())), preferred_element_type=jnp.float32
    )
    turned = functools.partial(
        lax.dot_general, dimension_numbers=(((1,), (1,)), ((), ())), preferred_element_type=jnp.float32
    )

    def spots(index):
        start = lax.fori_loop(0, rows, lambda i, acc: acc + jnp.where(i < index, wall_counts[i], 0), 0, unroll=True)
        plane = lax.broadcasted_iota(jnp.int32, (depth, cells), 0) // zloc
        cell = lax.broadcasted_iota(jnp.int32, (depth, cells), 1)
        return ((plane < wall_counts[index]) & (plane + start == cell)).astype(jnp.float32)

    levels = metric_table.shape[1]
    entry = (lax.broadcasted_iota(jnp.int32, (levels, cells), 0) == metric_index[...]).astype(jnp.float32)
    table = jnp.broadcast_to(metric_table[...], (8, levels))
    metric = plain(table, entry, precision=lax.Precision.HIGHEST)[:1]
    ends = jnp.concatenate([spots(me), spots(me ^ 1)], axis=0)
    scale = jnp.sum(ends * metric, axis=1, keepdims=True)
    pick = ends.astype(jnp.bfloat16)
    second = sum(plain(pick, part) for part in halves(viscosity * y_second[...]))
    first = -scale * sum(plain(pick, part) for part in halves(y_first[...]))
    other = jnp.concatenate([spots(me ^ step) for step in range(0, rows, 2)], axis=0).astype(jnp.bfloat16)
    wide = sum(turned(part, other) for part in halves(jnp.concatenate([second, first], axis=0)))
    match = lax.broadcasted_iota(jnp.int32, wide.shape, 0) % zloc == lax.broadcasted_iota(jnp.int32, wide.shape, 1) % zloc
    wide = jnp.where(match, wide, 0.0)
    for b in range(rows // 2):
        for k in range(2):
            matrix[:, (2 * b + k) * depth : (2 * b + k + 1) * depth] = wide[
                2 * k * depth : 2 * (k + 1) * depth, b * depth : (b + 1) * depth
            ]


def wall_kernel(comps, matrix, x_part, z_part, *refs):
    fields, (total, away) = refs[:-2], refs[-2:]
    depth = x_part.shape[0] // comps
    for comp in range(comps):
        at = slice(comp * depth, (comp + 1) * depth)
        stack = []
        for field in fields:
            stack += [field[at], field[depth : 2 * depth] * field[at]]
        result = dot_split(matrix[...], jnp.concatenate(stack, axis=0))
        total[at] = x_part[at] + z_part[at] + result[:depth]
        away[at] = result[depth:]


def finish_kernel(comps, mask, *refs):
    parts, out = refs[:-1], refs[-1]
    depth = mask.shape[0]
    for comp in range(comps):
        at = slice(comp * depth, (comp + 1) * depth)
        out[at] = jnp.where(mask[...] > 0, sum(part[at] for part in parts[1:]) + parts[0][at], 0.0)


def call(kernel, operands, spaces, results, name, scratch=()):
    results = [jax.ShapeDtypeStruct(shape, jnp.float32) for shape in results]
    held = sum(4 * math.prod(array.shape) for array in list(operands) + results)
    return pl.pallas_call(
        kernel,
        out_shape=results,
        in_specs=[pl.BlockSpec(memory_space=space) for space in spaces],
        out_specs=[pl.BlockSpec(memory_space=VMEM)] * len(results),
        scratch_shapes=[pltpu.VMEM(shape, jnp.float32) for shape in scratch],
        compiler_params=pltpu.CompilerParams(vmem_limit_bytes=(4 << 20) + 3 * held),
        name=name,
    )(*operands)


def local(
    velocity,
    wall_counts,
    x_first,
    x_second,
    y_first,
    y_second,
    z_first,
    z_second,
    metric_table,
    metric_index,
):
    rows = lax.axis_size("row")
    cols = lax.axis_size("col")
    comps, slots, zloc, length = velocity.shape
    depth = slots * zloc
    field = velocity.reshape(comps * depth, length)
    group = min(depth, 32)
    sources = cols // quad

    def along(value, step):
        return lax.ppermute(value, "col", [(i, i ^ step) for i in range(cols)])

    def across(value, step):
        return lax.ppermute(value, "row", [(i, i ^ step) for i in range(rows)])

    gathered = [along(field, quad * i) for i in range(1, sources)]
    far = [across(field, step) for step in range(2, rows, 2)]
    x_part, z_matrix, mask = call(
        functools.partial(stream_kernel, cols, comps, zloc),
        [wall_counts, z_first, z_second, field, x_first.reshape(1, length), x_second.reshape(1, length)],
        [SMEM] * 3 + [VMEM] * 3,
        [field.shape, (quad * group, 2 * sources * group), (depth, length)],
        "stream",
    )
    parts = call(
        functools.partial(span_kernel, comps, sources),
        [z_matrix] + far + [field] + gathered,
        [VMEM] + [pl.ANY] * len(far) + [VMEM] * sources,
        [field.shape] * quad,
        "span",
    )
    returned = [along(parts[t], t) for t in reversed(range(1, quad))]
    (y_matrix,) = call(
        functools.partial(wall_matrix_kernel, rows, zloc),
        [wall_counts, metric_table.reshape(1, -1), metric_index.reshape(1, -1), y_first, y_second, parts[0]],
        [SMEM] + [VMEM] * 4 + [pl.ANY],
        [(2 * depth, rows * depth)],
        "wall_matrix",
    )
    total, away = call(
        functools.partial(wall_kernel, comps),
        [y_matrix, x_part, parts[0], field] + far,
        [VMEM] * (4 + len(far)),
        [field.shape] * 2,
        "wall",
    )
    near = across(away, 1)
    (result,) = call(
        functools.partial(finish_kernel, comps),
        [mask, total, near] + returned,
        [VMEM] * (quad + 2),
        [field.shape],
        "finish",
    )
    return result.reshape(velocity.shape)


def solution(mesh):
    in_specs = (P(None, "row", "col", None), P(), P(), P(), P(), P(), P(), P(), P(), P())
    out_specs = P(None, "row", "col", None)
    return jax.shard_map(local, mesh=mesh, in_specs=in_specs, out_specs=out_specs, check_vma=False)
```

```python
import functools
import math

import jax
import jax.numpy as jnp
from jax import lax
from jax.experimental import pallas as pl
from jax.experimental.pallas import tpu as pltpu
from jax.sharding import PartitionSpec as P

viscosity = 0.4
quad = 4

VMEM = pltpu.VMEM
SMEM = pltpu.SMEM


def halves(value):
    high = value.astype(jnp.bfloat16)
    low = (value - high.astype(jnp.float32)).astype(jnp.bfloat16)
    return high, low


def dot_split(left, right, transposed=False):
    dims = (((1,), (1 if transposed else 0,)), ((), ()))
    mul = functools.partial(lax.dot_general, dimension_numbers=dims, preferred_element_type=jnp.float32)
    lh, ll = halves(left)
    rh, rl = halves(right)
    return mul(lh, rh) + (mul(lh, rl) + mul(ll, rh))


def span_kernel(comps, sources, matrix, *refs):
    fields, parts = refs[-quad - sources : -quad], refs[-quad:]
    depth, length = fields[0].shape[0] // comps, fields[0].shape[1]
    group = matrix.shape[0] // quad
    right = []
    for comp in range(comps):
        for at in range(0, depth, group):
            stack = [field[comp * depth + at : comp * depth + at + group] for field in fields]
            stack += [value * field[2 * depth + at : 2 * depth + at + group] for value, field in zip(stack, fields)]
            right.append(jnp.concatenate(stack, axis=0))
    result = dot_split(matrix[...], jnp.concatenate(right, axis=1))
    for t in range(quad):
        for i in range(len(right)):
            parts[t][i * group : (i + 1) * group] = result[
                t * group : (t + 1) * group, i * length : (i + 1) * length
            ]


def circulant_rows(row, length):
    return pltpu.roll(jnp.broadcast_to(row, (length, length)), 0, 1, stride=1, stride_axis=0)


def stream_kernel(
    cols, comps, zloc, wall_counts, z_first, z_second, field, x_first, x_second, x_part, z_matrix, mask
):
    depth = mask.shape[0]
    length = field.shape[1]
    count = wall_counts[lax.axis_index("row")]
    mask[...] = (lax.broadcasted_iota(jnp.int32, mask.shape, 0) // zloc < count).astype(jnp.float32)

    cells_z = cols * zloc
    shape = z_matrix.shape
    half = shape[1] // 2
    group = shape[0] // quad
    mine = lax.axis_index("col")
    r = lax.broadcasted_iota(jnp.int32, shape, 0)
    q = lax.broadcasted_iota(jnp.int32, shape, 1)
    q = jnp.where(q < half, q, q - half)
    out_cell = ((r // group) ^ mine) * zloc + r % zloc
    in_cell = ((quad * (q // group)) ^ mine) * zloc + q % zloc
    same = (r % group) // zloc == (q % group) // zloc
    gap = jnp.where(same, (in_cell - out_cell + cells_z) % cells_z, -1)
    kind = lax.broadcasted_iota(jnp.int32, (1, shape[1]), 1) < half

    def fill(k, total):
        value = jnp.where(kind, viscosity * z_second[k], -z_first[k])
        return jnp.where(gap == k, value, total)

    z_matrix[...] = lax.fori_loop(0, cells_z, fill, jnp.zeros(shape, jnp.float32), unroll=8)

    u = field[...]
    lead = u[:depth]
    left = jnp.concatenate(
        [u, jnp.concatenate([lead * u[c * depth : (c + 1) * depth] for c in range(comps)], axis=0)], axis=1
    )
    right = jnp.concatenate(
        [viscosity * circulant_rows(x_second[...], length), -circulant_rows(x_first[...], length)], axis=1
    )
    x_part[...] = dot_split(left, right, transposed=True)


def wall_matrix_kernel(rows, zloc, wall_counts, metric_table, metric_index, y_first, y_second, after, matrix):
    cells = y_first.shape[0]
    depth = matrix.shape[0] // 2
    me = lax.axis_index("row")
    plain = functools.partial(
        lax.dot_general, dimension_numbers=(((1,), (0,)), ((), ())), preferred_element_type=jnp.float32
    )
    turned = functools.partial(
        lax.dot_general, dimension_numbers=(((1,), (1,)), ((), ())), preferred_element_type=jnp.float32
    )

    def spots(index):
        start = lax.fori_loop(0, rows, lambda i, acc: acc + jnp.where(i < index, wall_counts[i], 0), 0, unroll=True)
        plane = lax.broadcasted_iota(jnp.int32, (depth, cells), 0) // zloc
        cell = lax.broadcasted_iota(jnp.int32, (depth, cells), 1)
        return ((plane < wall_counts[index]) & (plane + start == cell)).astype(jnp.float32)

    levels = metric_table.shape[1]
    entry = (lax.broadcasted_iota(jnp.int32, (levels, cells), 0) == metric_index[...]).astype(jnp.float32)
    table = jnp.broadcast_to(metric_table[...], (8, levels))
    metric = plain(table, entry, precision=lax.Precision.HIGHEST)[:1]
    ends = jnp.concatenate([spots(me), spots(me ^ 1)], axis=0)
    scale = jnp.sum(ends * metric, axis=1, keepdims=True)
    pick = ends.astype(jnp.bfloat16)
    second = sum(plain(pick, part) for part in halves(viscosity * y_second[...]))
    first = -scale * sum(plain(pick, part) for part in halves(y_first[...]))
    other = jnp.concatenate([spots(me ^ step) for step in range(0, rows, 2)], axis=0).astype(jnp.bfloat16)
    wide = sum(turned(part, other) for part in halves(jnp.concatenate([second, first], axis=0)))
    match = lax.broadcasted_iota(jnp.int32, wide.shape, 0) % zloc == lax.broadcasted_iota(jnp.int32, wide.shape, 1) % zloc
    wide = jnp.where(match, wide, 0.0)
    for b in range(rows // 2):
        for k in range(2):
            matrix[:, (2 * b + k) * depth : (2 * b + k + 1) * depth] = wide[
                2 * k * depth : 2 * (k + 1) * depth, b * depth : (b + 1) * depth
            ]


def wall_kernel(comps, matrix, x_part, z_part, *refs):
    fields, (total, away) = refs[:-2], refs[-2:]
    depth = x_part.shape[0] // comps
    for comp in range(comps):
        at = slice(comp * depth, (comp + 1) * depth)
        stack = []
        for field in fields:
            stack += [field[at], field[depth : 2 * depth] * field[at]]
        result = dot_split(matrix[...], jnp.concatenate(stack, axis=0))
        total[at] = x_part[at] + z_part[at] + result[:depth]
        away[at] = result[depth:]


def finish_kernel(comps, mask, *refs):
    parts, out = refs[:-1], refs[-1]
    depth = mask.shape[0]
    for comp in range(comps):
        at = slice(comp * depth, (comp + 1) * depth)
        out[at] = jnp.where(mask[...] > 0, sum(part[at] for part in parts[1:]) + parts[0][at], 0.0)


def call(kernel, operands, spaces, results, name, scratch=()):
    results = [jax.ShapeDtypeStruct(shape, jnp.float32) for shape in results]
    held = sum(4 * math.prod(array.shape) for array in list(operands) + results)
    return pl.pallas_call(
        kernel,
        out_shape=results,
        in_specs=[pl.BlockSpec(memory_space=space) for space in spaces],
        out_specs=[pl.BlockSpec(memory_space=VMEM)] * len(results),
        scratch_shapes=[pltpu.VMEM(shape, jnp.float32) for shape in scratch],
        compiler_params=pltpu.CompilerParams(vmem_limit_bytes=(4 << 20) + 3 * held),
        name=name,
    )(*operands)


def local(
    velocity,
    wall_counts,
    x_first,
    x_second,
    y_first,
    y_second,
    z_first,
    z_second,
    metric_table,
    metric_index,
):
    rows = lax.axis_size("row")
    cols = lax.axis_size("col")
    comps, slots, zloc, length = velocity.shape
    depth = slots * zloc
    field = velocity.reshape(comps * depth, length)
    group = min(depth, 32)
    sources = cols // quad

    def along(value, step):
        return lax.ppermute(value, "col", [(i, i ^ step) for i in range(cols)])

    def across(value, step):
        return lax.ppermute(value, "row", [(i, i ^ step) for i in range(rows)])

    gathered = [along(field, quad * i) for i in range(1, sources)]
    far = [across(field, step) for step in range(2, rows, 2)]
    x_part, z_matrix, mask = call(
        functools.partial(stream_kernel, cols, comps, zloc),
        [wall_counts, z_first, z_second, field, x_first.reshape(1, length), x_second.reshape(1, length)],
        [SMEM] * 3 + [VMEM] * 3,
        [field.shape, (quad * group, 2 * sources * group), (depth, length)],
        "stream",
    )
    parts = call(
        functools.partial(span_kernel, comps, sources),
        [z_matrix] + far + [field] + gathered,
        [VMEM] + [pl.ANY] * len(far) + [VMEM] * sources,
        [field.shape] * quad,
        "span",
    )
    returned = [along(parts[t], t) for t in range(1, quad)]
    (y_matrix,) = call(
        functools.partial(wall_matrix_kernel, rows, zloc),
        [wall_counts, metric_table.reshape(1, -1), metric_index.reshape(1, -1), y_first, y_second, parts[0]],
        [SMEM] + [VMEM] * 4 + [pl.ANY],
        [(2 * depth, rows * depth)],
        "wall_matrix",
    )
    total, away = call(
        functools.partial(wall_kernel, comps),
        [y_matrix, x_part, parts[0], field] + far,
        [VMEM] * (4 + len(far)),
        [field.shape] * 2,
        "wall",
    )
    near = across(away, 1)
    (result,) = call(
        functools.partial(finish_kernel, comps),
        [mask, total, near] + returned,
        [VMEM] * (quad + 2),
        [field.shape],
        "finish",
    )
    return result.reshape(velocity.shape)


def solution(mesh):
    in_specs = (P(None, "row", "col", None), P(), P(), P(), P(), P(), P(), P(), P(), P())
    out_specs = P(None, "row", "col", None)
    return jax.shard_map(local, mesh=mesh, in_specs=in_specs, out_specs=out_specs, check_vma=False)
```

```python
import functools
import math

import jax
import jax.numpy as jnp
from jax import lax
from jax.experimental import pallas as pl
from jax.experimental.pallas import tpu as pltpu
from jax.sharding import PartitionSpec as P

viscosity = 0.4
quad = 4

VMEM = pltpu.VMEM
SMEM = pltpu.SMEM


def halves(value):
    high = value.astype(jnp.bfloat16)
    low = (value - high.astype(jnp.float32)).astype(jnp.bfloat16)
    return high, low


def dot_split(left, right, transposed=False):
    dims = (((1,), (1 if transposed else 0,)), ((), ()))
    mul = functools.partial(lax.dot_general, dimension_numbers=dims, preferred_element_type=jnp.float32)
    lh, ll = halves(left)
    rh, rl = halves(right)
    return mul(lh, rh) + (mul(lh, rl) + mul(ll, rh))


def span_kernel(comps, sources, matrix, *refs):
    fields, parts = refs[-quad - sources : -quad], refs[-quad:]
    depth, length = fields[0].shape[0] // comps, fields[0].shape[1]
    group = matrix.shape[0] // quad
    right = []
    for comp in range(comps):
        for at in range(0, depth, group):
            stack = [field[comp * depth + at : comp * depth + at + group] for field in fields]
            stack += [value * field[2 * depth + at : 2 * depth + at + group] for value, field in zip(stack, fields)]
            right.append(jnp.concatenate(stack, axis=0))
    result = dot_split(matrix[...], jnp.concatenate(right, axis=1))
    for t in range(quad):
        for i in range(len(right)):
            parts[t][i * group : (i + 1) * group] = result[
                t * group : (t + 1) * group, i * length : (i + 1) * length
            ]


def circulant_rows(row, length):
    return pltpu.roll(jnp.broadcast_to(row, (length, length)), 0, 1, stride=1, stride_axis=0)


def stream_kernel(
    cols, comps, zloc, wall_counts, z_first, z_second, field, x_first, x_second, x_part, z_matrix, mask
):
    depth = mask.shape[0]
    length = field.shape[1]
    count = wall_counts[lax.axis_index("row")]
    mask[...] = (lax.broadcasted_iota(jnp.int32, mask.shape, 0) // zloc < count).astype(jnp.float32)

    cells_z = cols * zloc
    shape = z_matrix.shape
    half = shape[1] // 2
    group = shape[0] // quad
    mine = lax.axis_index("col")
    r = lax.broadcasted_iota(jnp.int32, shape, 0)
    q = lax.broadcasted_iota(jnp.int32, shape, 1)
    q = jnp.where(q < half, q, q - half)
    out_cell = ((r // group) ^ mine) * zloc + r % zloc
    in_cell = ((quad * (q // group)) ^ mine) * zloc + q % zloc
    same = (r % group) // zloc == (q % group) // zloc
    gap = jnp.where(same, (in_cell - out_cell + cells_z) % cells_z, -1)
    kind = lax.broadcasted_iota(jnp.int32, (1, shape[1]), 1) < half

    def fill(k, total):
        value = jnp.where(kind, viscosity * z_second[k], -z_first[k])
        return jnp.where(gap == k, value, total)

    z_matrix[...] = lax.fori_loop(0, cells_z, fill, jnp.zeros(shape, jnp.float32), unroll=8)

    u = field[...]
    lead = u[:depth]
    left = jnp.concatenate(
        [u, jnp.concatenate([lead * u[c * depth : (c + 1) * depth] for c in range(comps)], axis=0)], axis=1
    )
    right = jnp.concatenate(
        [viscosity * circulant_rows(x_second[...], length), -circulant_rows(x_first[...], length)], axis=1
    )
    x_part[...] = dot_split(left, right, transposed=True)


def wall_matrix_kernel(rows, zloc, wall_counts, metric_table, metric_index, y_first, y_second, after, matrix):
    cells = y_first.shape[0]
    depth = matrix.shape[0] // 2
    me = lax.axis_index("row")
    plain = functools.partial(
        lax.dot_general, dimension_numbers=(((1,), (0,)), ((), ())), preferred_element_type=jnp.float32
    )
    turned = functools.partial(
        lax.dot_general, dimension_numbers=(((1,), (1,)), ((), ())), preferred_element_type=jnp.float32
    )

    def spots(index):
        start = lax.fori_loop(0, rows, lambda i, acc: acc + jnp.where(i < index, wall_counts[i], 0), 0, unroll=True)
        plane = lax.broadcasted_iota(jnp.int32, (depth, cells), 0) // zloc
        cell = lax.broadcasted_iota(jnp.int32, (depth, cells), 1)
        return ((plane < wall_counts[index]) & (plane + start == cell)).astype(jnp.float32)

    levels = metric_table.shape[1]
    entry = (lax.broadcasted_iota(jnp.int32, (levels, cells), 0) == metric_index[...]).astype(jnp.float32)
    table = jnp.broadcast_to(metric_table[...], (8, levels))
    metric = plain(table, entry, precision=lax.Precision.HIGHEST)[:1]
    ends = jnp.concatenate([spots(me), spots(me ^ 1)], axis=0)
    scale = jnp.sum(ends * metric, axis=1, keepdims=True)
    pick = ends.astype(jnp.bfloat16)
    second = sum(plain(pick, part) for part in halves(viscosity * y_second[...]))
    first = -scale * sum(plain(pick, part) for part in halves(y_first[...]))
    other = jnp.concatenate([spots(me ^ step) for step in range(0, rows, 2)], axis=0).astype(jnp.bfloat16)
    wide = sum(turned(part, other) for part in halves(jnp.concatenate([second, first], axis=0)))
    match = lax.broadcasted_iota(jnp.int32, wide.shape, 0) % zloc == lax.broadcasted_iota(jnp.int32, wide.shape, 1) % zloc
    wide = jnp.where(match, wide, 0.0)
    for b in range(rows // 2):
        for k in range(2):
            matrix[:, (2 * b + k) * depth : (2 * b + k + 1) * depth] = wide[
                2 * k * depth : 2 * (k + 1) * depth, b * depth : (b + 1) * depth
            ]


def wall_kernel(comps, matrix, x_part, z_part, *refs):
    fields, (total, away) = refs[:-2], refs[-2:]
    depth = x_part.shape[0] // comps
    for comp in range(comps):
        at = slice(comp * depth, (comp + 1) * depth)
        stack = []
        for field in fields:
            stack += [field[at], field[depth : 2 * depth] * field[at]]
        result = dot_split(matrix[...], jnp.concatenate(stack, axis=0))
        total[at] = x_part[at] + z_part[at] + result[:depth]
        away[at] = result[depth:]


def finish_kernel(comps, mask, *refs):
    parts, out = refs[:-1], refs[-1]
    depth = mask.shape[0]
    for comp in range(comps):
        at = slice(comp * depth, (comp + 1) * depth)
        out[at] = jnp.where(mask[...] > 0, sum(part[at] for part in parts[1:]) + parts[0][at], 0.0)


def call(kernel, operands, spaces, results, name, scratch=()):
    results = [jax.ShapeDtypeStruct(shape, jnp.float32) for shape in results]
    held = sum(4 * math.prod(array.shape) for array in list(operands) + results)
    return pl.pallas_call(
        kernel,
        out_shape=results,
        in_specs=[pl.BlockSpec(memory_space=space) for space in spaces],
        out_specs=[pl.BlockSpec(memory_space=VMEM)] * len(results),
        scratch_shapes=[pltpu.VMEM(shape, jnp.float32) for shape in scratch],
        compiler_params=pltpu.CompilerParams(vmem_limit_bytes=(4 << 20) + 3 * held),
        name=name,
    )(*operands)


def local(
    velocity,
    wall_counts,
    x_first,
    x_second,
    y_first,
    y_second,
    z_first,
    z_second,
    metric_table,
    metric_index,
):
    rows = lax.axis_size("row")
    cols = lax.axis_size("col")
    comps, slots, zloc, length = velocity.shape
    depth = slots * zloc
    field = velocity.reshape(comps * depth, length)
    group = min(depth, 32)
    sources = cols // quad

    def along(value, step):
        return lax.ppermute(value, "col", [(i, i ^ step) for i in range(cols)])

    def across(value, step):
        return lax.ppermute(value, "row", [(i, i ^ step) for i in range(rows)])

    gathered = [along(field, quad * i) for i in range(1, sources)]
    far = [across(field, step) for step in range(2, rows, 2)]
    x_part, z_matrix, mask = call(
        functools.partial(stream_kernel, cols, comps, zloc),
        [wall_counts, z_first, z_second, field, x_first.reshape(1, length), x_second.reshape(1, length)],
        [SMEM] * 3 + [VMEM] * 3,
        [field.shape, (quad * group, 2 * sources * group), (depth, length)],
        "stream",
    )
    parts = call(
        functools.partial(span_kernel, comps, sources),
        [z_matrix, field] + gathered,
        [VMEM] * (1 + sources),
        [field.shape] * quad,
        "span",
    )
    returned = [along(parts[t], t) for t in reversed(range(1, quad))]
    (y_matrix,) = call(
        functools.partial(wall_matrix_kernel, rows, zloc),
        [wall_counts, metric_table.reshape(1, -1), metric_index.reshape(1, -1), y_first, y_second, parts[0]],
        [SMEM] + [VMEM] * 4 + [pl.ANY],
        [(2 * depth, rows * depth)],
        "wall_matrix",
    )
    total, away = call(
        functools.partial(wall_kernel, comps),
        [y_matrix, x_part, parts[0], field] + far,
        [VMEM] * (4 + len(far)),
        [field.shape] * 2,
        "wall",
    )
    near = across(away, 1)
    (result,) = call(
        functools.partial(finish_kernel, comps),
        [mask, total, near] + returned,
        [VMEM] * (quad + 2),
        [field.shape],
        "finish",
    )
    return result.reshape(velocity.shape)


def solution(mesh):
    in_specs = (P(None, "row", "col", None), P(), P(), P(), P(), P(), P(), P(), P(), P())
    out_specs = P(None, "row", "col", None)
    return jax.shard_map(local, mesh=mesh, in_specs=in_specs, out_specs=out_specs, check_vma=False)
```

```python
import functools
import math

import jax
import jax.numpy as jnp
from jax import lax
from jax.experimental import pallas as pl
from jax.experimental.pallas import tpu as pltpu
from jax.sharding import PartitionSpec as P

viscosity = 0.4
quad = 4

VMEM = pltpu.VMEM
SMEM = pltpu.SMEM


def halves(value):
    high = value.astype(jnp.bfloat16)
    low = (value - high.astype(jnp.float32)).astype(jnp.bfloat16)
    return high, low


def dot_split(left, right, transposed=False):
    dims = (((1,), (1 if transposed else 0,)), ((), ()))
    mul = functools.partial(lax.dot_general, dimension_numbers=dims, preferred_element_type=jnp.float32)
    lh, ll = halves(left)
    rh, rl = halves(right)
    return mul(lh, rh) + (mul(lh, rl) + mul(ll, rh))


def span_kernel(comps, sources, matrix, *refs):
    fields, parts = refs[-quad - sources : -quad], refs[-quad:]
    depth, length = fields[0].shape[0] // comps, fields[0].shape[1]
    group = matrix.shape[0] // quad
    right = []
    for comp in range(comps):
        for at in range(0, depth, group):
            stack = [field[comp * depth + at : comp * depth + at + group] for field in fields]
            stack += [value * field[2 * depth + at : 2 * depth + at + group] for value, field in zip(stack, fields)]
            right.append(jnp.concatenate(stack, axis=0))
    result = dot_split(matrix[...], jnp.concatenate(right, axis=1))
    for t in range(quad):
        for i in range(len(right)):
            parts[t][i * group : (i + 1) * group] = result[
                t * group : (t + 1) * group, i * length : (i + 1) * length
            ]


def circulant_rows(row, length):
    return pltpu.roll(jnp.broadcast_to(row, (length, length)), 0, 1, stride=1, stride_axis=0)


def stream_kernel(
    cols, comps, zloc, wall_counts, z_first, z_second, field, x_first, x_second, x_part, z_matrix, mask, held
):
    held[...] = field[...]
    depth = mask.shape[0]
    length = field.shape[1]
    count = wall_counts[lax.axis_index("row")]
    mask[...] = (lax.broadcasted_iota(jnp.int32, mask.shape, 0) // zloc < count).astype(jnp.float32)

    cells_z = cols * zloc
    shape = z_matrix.shape
    half = shape[1] // 2
    group = shape[0] // quad
    mine = lax.axis_index("col")
    r = lax.broadcasted_iota(jnp.int32, shape, 0)
    q = lax.broadcasted_iota(jnp.int32, shape, 1)
    q = jnp.where(q < half, q, q - half)
    out_cell = ((r // group) ^ mine) * zloc + r % zloc
    in_cell = ((quad * (q // group)) ^ mine) * zloc + q % zloc
    same = (r % group) // zloc == (q % group) // zloc
    gap = jnp.where(same, (in_cell - out_cell + cells_z) % cells_z, -1)
    kind = lax.broadcasted_iota(jnp.int32, (1, shape[1]), 1) < half

    def fill(k, total):
        value = jnp.where(kind, viscosity * z_second[k], -z_first[k])
        return jnp.where(gap == k, value, total)

    z_matrix[...] = lax.fori_loop(0, cells_z, fill, jnp.zeros(shape, jnp.float32), unroll=8)

    u = field[...]
    lead = u[:depth]
    left = jnp.concatenate(
        [u, jnp.concatenate([lead * u[c * depth : (c + 1) * depth] for c in range(comps)], axis=0)], axis=1
    )
    right = jnp.concatenate(
        [viscosity * circulant_rows(x_second[...], length), -circulant_rows(x_first[...], length)], axis=1
    )
    x_part[...] = dot_split(left, right, transposed=True)


def wall_matrix_kernel(rows, zloc, wall_counts, metric_table, metric_index, y_first, y_second, after, matrix):
    cells = y_first.shape[0]
    depth = matrix.shape[0] // 2
    me = lax.axis_index("row")
    plain = functools.partial(
        lax.dot_general, dimension_numbers=(((1,), (0,)), ((), ())), preferred_element_type=jnp.float32
    )
    turned = functools.partial(
        lax.dot_general, dimension_numbers=(((1,), (1,)), ((), ())), preferred_element_type=jnp.float32
    )

    def spots(index):
        start = lax.fori_loop(0, rows, lambda i, acc: acc + jnp.where(i < index, wall_counts[i], 0), 0, unroll=True)
        plane = lax.broadcasted_iota(jnp.int32, (depth, cells), 0) // zloc
        cell = lax.broadcasted_iota(jnp.int32, (depth, cells), 1)
        return ((plane < wall_counts[index]) & (plane + start == cell)).astype(jnp.float32)

    levels = metric_table.shape[1]
    entry = (lax.broadcasted_iota(jnp.int32, (levels, cells), 0) == metric_index[...]).astype(jnp.float32)
    table = jnp.broadcast_to(metric_table[...], (8, levels))
    metric = plain(table, entry, precision=lax.Precision.HIGHEST)[:1]
    ends = jnp.concatenate([spots(me), spots(me ^ 1)], axis=0)
    scale = jnp.sum(ends * metric, axis=1, keepdims=True)
    pick = ends.astype(jnp.bfloat16)
    second = sum(plain(pick, part) for part in halves(viscosity * y_second[...]))
    first = -scale * sum(plain(pick, part) for part in halves(y_first[...]))
    other = jnp.concatenate([spots(me ^ step) for step in range(0, rows, 2)], axis=0).astype(jnp.bfloat16)
    wide = sum(turned(part, other) for part in halves(jnp.concatenate([second, first], axis=0)))
    match = lax.broadcasted_iota(jnp.int32, wide.shape, 0) % zloc == lax.broadcasted_iota(jnp.int32, wide.shape, 1) % zloc
    wide = jnp.where(match, wide, 0.0)
    for b in range(rows // 2):
        for k in range(2):
            matrix[:, (2 * b + k) * depth : (2 * b + k + 1) * depth] = wide[
                2 * k * depth : 2 * (k + 1) * depth, b * depth : (b + 1) * depth
            ]


def wall_kernel(comps, matrix, x_part, z_part, *refs):
    fields, (total, away) = refs[:-2], refs[-2:]
    depth = x_part.shape[0] // comps
    for comp in range(comps):
        at = slice(comp * depth, (comp + 1) * depth)
        stack = []
        for field in fields:
            stack += [field[at], field[depth : 2 * depth] * field[at]]
        result = dot_split(matrix[...], jnp.concatenate(stack, axis=0))
        total[at] = x_part[at] + z_part[at] + result[:depth]
        away[at] = result[depth:]


def finish_kernel(comps, mask, *refs):
    parts, out = refs[:-1], refs[-1]
    depth = mask.shape[0]
    for comp in range(comps):
        at = slice(comp * depth, (comp + 1) * depth)
        out[at] = jnp.where(mask[...] > 0, sum(part[at] for part in parts[1:]) + parts[0][at], 0.0)


def call(kernel, operands, spaces, results, name, scratch=()):
    results = [jax.ShapeDtypeStruct(shape, jnp.float32) for shape in results]
    held = sum(4 * math.prod(array.shape) for array in list(operands) + results)
    return pl.pallas_call(
        kernel,
        out_shape=results,
        in_specs=[pl.BlockSpec(memory_space=space) for space in spaces],
        out_specs=[pl.BlockSpec(memory_space=VMEM)] * len(results),
        scratch_shapes=[pltpu.VMEM(shape, jnp.float32) for shape in scratch],
        compiler_params=pltpu.CompilerParams(vmem_limit_bytes=(4 << 20) + 3 * held),
        name=name,
    )(*operands)


def local(
    velocity,
    wall_counts,
    x_first,
    x_second,
    y_first,
    y_second,
    z_first,
    z_second,
    metric_table,
    metric_index,
):
    rows = lax.axis_size("row")
    cols = lax.axis_size("col")
    comps, slots, zloc, length = velocity.shape
    depth = slots * zloc
    field = velocity.reshape(comps * depth, length)
    group = min(depth, 32)
    sources = cols // quad

    def along(value, step):
        return lax.ppermute(value, "col", [(i, i ^ step) for i in range(cols)])

    def across(value, step):
        return lax.ppermute(value, "row", [(i, i ^ step) for i in range(rows)])

    gathered = [along(field, quad * i) for i in range(1, sources)]
    x_part, z_matrix, mask, held = call(
        functools.partial(stream_kernel, cols, comps, zloc),
        [wall_counts, z_first, z_second, field, x_first.reshape(1, length), x_second.reshape(1, length)],
        [SMEM] * 3 + [VMEM] * 3,
        [field.shape, (quad * group, 2 * sources * group), (depth, length), field.shape],
        "stream",
    )
    far = [across(held, step) for step in range(2, rows, 2)]
    parts = call(
        functools.partial(span_kernel, comps, sources),
        [z_matrix, field] + gathered,
        [VMEM] * (1 + sources),
        [field.shape] * quad,
        "span",
    )
    returned = [along(parts[t], t) for t in reversed(range(1, quad))]
    (y_matrix,) = call(
        functools.partial(wall_matrix_kernel, rows, zloc),
        [wall_counts, metric_table.reshape(1, -1), metric_index.reshape(1, -1), y_first, y_second, parts[0]],
        [SMEM] + [VMEM] * 4 + [pl.ANY],
        [(2 * depth, rows * depth)],
        "wall_matrix",
    )
    total, away = call(
        functools.partial(wall_kernel, comps),
        [y_matrix, x_part, parts[0], field] + far,
        [VMEM] * (4 + len(far)),
        [field.shape] * 2,
        "wall",
    )
    near = across(away, 1)
    (result,) = call(
        functools.partial(finish_kernel, comps),
        [mask, total, near] + returned,
        [VMEM] * (quad + 2),
        [field.shape],
        "finish",
    )
    return result.reshape(velocity.shape)


def solution(mesh):
    in_specs = (P(None, "row", "col", None), P(), P(), P(), P(), P(), P(), P(), P(), P())
    out_specs = P(None, "row", "col", None)
    return jax.shard_map(local, mesh=mesh, in_specs=in_specs, out_specs=out_specs, check_vma=False)
```

```python
import functools
import math

import jax
import jax.numpy as jnp
from jax import lax
from jax.experimental import pallas as pl
from jax.experimental.pallas import tpu as pltpu
from jax.sharding import PartitionSpec as P

viscosity = 0.4
quad = 4

VMEM = pltpu.VMEM
SMEM = pltpu.SMEM


def halves(value):
    high = value.astype(jnp.bfloat16)
    low = (value - high.astype(jnp.float32)).astype(jnp.bfloat16)
    return high, low


def dot_split(left, right, transposed=False):
    dims = (((1,), (1 if transposed else 0,)), ((), ()))
    mul = functools.partial(lax.dot_general, dimension_numbers=dims, preferred_element_type=jnp.float32)
    lh, ll = halves(left)
    rh, rl = halves(right)
    return mul(lh, rh) + (mul(lh, rl) + mul(ll, rh))


def span_kernel(comps, sources, pieces, matrix, *refs):
    fields, parts = refs[:sources], refs[sources:]
    depth, length = fields[0].shape[0] // comps, fields[0].shape[1]
    group = matrix.shape[0] // quad
    right = []
    for comp in range(comps):
        for at in range(0, depth, group):
            stack = [field[comp * depth + at : comp * depth + at + group] for field in fields]
            stack += [value * field[2 * depth + at : 2 * depth + at + group] for value, field in zip(stack, fields)]
            right.append(jnp.concatenate(stack, axis=0))
    result = dot_split(matrix[...], jnp.concatenate(right, axis=1))
    for part, (t, low, high) in zip(parts, pieces):
        for at in range(low, high, group):
            i = at // group
            part[at - low : at - low + group] = result[t * group : (t + 1) * group, i * length : (i + 1) * length]


def circulant_rows(row, length):
    return pltpu.roll(jnp.broadcast_to(row, (length, length)), 0, 1, stride=1, stride_axis=0)


def stream_kernel(
    cols, comps, zloc, wall_counts, z_first, z_second, field, x_first, x_second, x_part, z_matrix, mask, held
):
    held[...] = field[...]
    depth = mask.shape[0]
    length = field.shape[1]
    count = wall_counts[lax.axis_index("row")]
    mask[...] = (lax.broadcasted_iota(jnp.int32, mask.shape, 0) // zloc < count).astype(jnp.float32)

    cells_z = cols * zloc
    shape = z_matrix.shape
    half = shape[1] // 2
    group = shape[0] // quad
    mine = lax.axis_index("col")
    r = lax.broadcasted_iota(jnp.int32, shape, 0)
    q = lax.broadcasted_iota(jnp.int32, shape, 1)
    q = jnp.where(q < half, q, q - half)
    out_cell = ((r // group) ^ mine) * zloc + r % zloc
    in_cell = ((quad * (q // group)) ^ mine) * zloc + q % zloc
    same = (r % group) // zloc == (q % group) // zloc
    gap = jnp.where(same, (in_cell - out_cell + cells_z) % cells_z, -1)
    kind = lax.broadcasted_iota(jnp.int32, (1, shape[1]), 1) < half

    def fill(k, total):
        value = jnp.where(kind, viscosity * z_second[k], -z_first[k])
        return jnp.where(gap == k, value, total)

    z_matrix[...] = lax.fori_loop(0, cells_z, fill, jnp.zeros(shape, jnp.float32), unroll=8)

    u = field[...]
    lead = u[:depth]
    left = jnp.concatenate(
        [u, jnp.concatenate([lead * u[c * depth : (c + 1) * depth] for c in range(comps)], axis=0)], axis=1
    )
    right = jnp.concatenate(
        [viscosity * circulant_rows(x_second[...], length), -circulant_rows(x_first[...], length)], axis=1
    )
    x_part[...] = dot_split(left, right, transposed=True)


def wall_matrix_kernel(rows, zloc, wall_counts, metric_table, metric_index, y_first, y_second, after, matrix):
    cells = y_first.shape[0]
    depth = matrix.shape[0] // 2
    me = lax.axis_index("row")
    plain = functools.partial(
        lax.dot_general, dimension_numbers=(((1,), (0,)), ((), ())), preferred_element_type=jnp.float32
    )
    turned = functools.partial(
        lax.dot_general, dimension_numbers=(((1,), (1,)), ((), ())), preferred_element_type=jnp.float32
    )

    def spots(index):
        start = lax.fori_loop(0, rows, lambda i, acc: acc + jnp.where(i < index, wall_counts[i], 0), 0, unroll=True)
        plane = lax.broadcasted_iota(jnp.int32, (depth, cells), 0) // zloc
        cell = lax.broadcasted_iota(jnp.int32, (depth, cells), 1)
        return ((plane < wall_counts[index]) & (plane + start == cell)).astype(jnp.float32)

    levels = metric_table.shape[1]
    entry = (lax.broadcasted_iota(jnp.int32, (levels, cells), 0) == metric_index[...]).astype(jnp.float32)
    table = jnp.broadcast_to(metric_table[...], (8, levels))
    metric = plain(table, entry, precision=lax.Precision.HIGHEST)[:1]
    ends = jnp.concatenate([spots(me), spots(me ^ 1)], axis=0)
    scale = jnp.sum(ends * metric, axis=1, keepdims=True)
    pick = ends.astype(jnp.bfloat16)
    second = sum(plain(pick, part) for part in halves(viscosity * y_second[...]))
    first = -scale * sum(plain(pick, part) for part in halves(y_first[...]))
    other = jnp.concatenate([spots(me ^ step) for step in range(0, rows, 2)], axis=0).astype(jnp.bfloat16)
    wide = sum(turned(part, other) for part in halves(jnp.concatenate([second, first], axis=0)))
    match = lax.broadcasted_iota(jnp.int32, wide.shape, 0) % zloc == lax.broadcasted_iota(jnp.int32, wide.shape, 1) % zloc
    wide = jnp.where(match, wide, 0.0)
    for b in range(rows // 2):
        for k in range(2):
            matrix[:, (2 * b + k) * depth : (2 * b + k + 1) * depth] = wide[
                2 * k * depth : 2 * (k + 1) * depth, b * depth : (b + 1) * depth
            ]


def wall_kernel(comps, matrix, x_part, z_part, *refs):
    fields, (total, away) = refs[:-2], refs[-2:]
    depth = x_part.shape[0] // comps
    for comp in range(comps):
        at = slice(comp * depth, (comp + 1) * depth)
        stack = []
        for field in fields:
            stack += [field[at], field[depth : 2 * depth] * field[at]]
        result = dot_split(matrix[...], jnp.concatenate(stack, axis=0))
        total[at] = x_part[at] + z_part[at] + result[:depth]
        away[at] = result[depth:]


def finish_kernel(comps, pieces, mask, total, near, *refs):
    parts, out = refs[:-1], refs[-1]
    depth = mask.shape[0]
    for comp in range(comps):
        at = slice(comp * depth, (comp + 1) * depth)
        value = total[at] + near[at]
        for part, (_, low, high) in zip(parts, pieces):
            if low <= at.start and at.stop <= high:
                value += part[at.start - low : at.stop - low]
        out[at] = jnp.where(mask[...] > 0, value, 0.0)


def call(kernel, operands, spaces, results, name, scratch=()):
    results = [jax.ShapeDtypeStruct(shape, jnp.float32) for shape in results]
    held = sum(4 * math.prod(array.shape) for array in list(operands) + results)
    return pl.pallas_call(
        kernel,
        out_shape=results,
        in_specs=[pl.BlockSpec(memory_space=space) for space in spaces],
        out_specs=[pl.BlockSpec(memory_space=VMEM)] * len(results),
        scratch_shapes=[pltpu.VMEM(shape, jnp.float32) for shape in scratch],
        compiler_params=pltpu.CompilerParams(vmem_limit_bytes=(4 << 20) + 3 * held),
        name=name,
    )(*operands)


def local(
    velocity,
    wall_counts,
    x_first,
    x_second,
    y_first,
    y_second,
    z_first,
    z_second,
    metric_table,
    metric_index,
):
    rows = lax.axis_size("row")
    cols = lax.axis_size("col")
    comps, slots, zloc, length = velocity.shape
    depth = slots * zloc
    field = velocity.reshape(comps * depth, length)
    group = min(depth, 32)
    sources = cols // quad
    rest = comps * depth
    pieces = [(t, 0, rest) for t in (0, 3, 2)] + [(1, 0, rest - depth), (1, rest - depth, rest)]

    def along(value, step):
        return lax.ppermute(value, "col", [(i, i ^ step) for i in range(cols)])

    def across(value, step):
        return lax.ppermute(value, "row", [(i, i ^ step) for i in range(rows)])

    gathered = [along(field, quad * i) for i in range(1, sources)]
    x_part, z_matrix, mask, held = call(
        functools.partial(stream_kernel, cols, comps, zloc),
        [wall_counts, z_first, z_second, field, x_first.reshape(1, length), x_second.reshape(1, length)],
        [SMEM] * 3 + [VMEM] * 3,
        [field.shape, (quad * group, 2 * sources * group), (depth, length), field.shape],
        "stream",
    )
    far = [across(held, step) for step in range(2, rows, 2)]
    parts = call(
        functools.partial(span_kernel, comps, sources, pieces),
        [z_matrix, field] + gathered,
        [VMEM] * (1 + sources),
        [(high - low, length) for _, low, high in pieces],
        "span",
    )
    returned = [along(part, t) for part, (t, _, _) in zip(parts[1:], pieces[1:])]
    (y_matrix,) = call(
        functools.partial(wall_matrix_kernel, rows, zloc),
        [wall_counts, metric_table.reshape(1, -1), metric_index.reshape(1, -1), y_first, y_second, parts[0]],
        [SMEM] + [VMEM] * 4 + [pl.ANY],
        [(2 * depth, rows * depth)],
        "wall_matrix",
    )
    total, away = call(
        functools.partial(wall_kernel, comps),
        [y_matrix, x_part, parts[0], field] + far,
        [VMEM] * (4 + len(far)),
        [field.shape] * 2,
        "wall",
    )
    near = across(away, 1)
    (result,) = call(
        functools.partial(finish_kernel, comps, pieces[1:]),
        [mask, total, near] + returned,
        [VMEM] * (3 + len(returned)),
        [field.shape],
        "finish",
    )
    return result.reshape(velocity.shape)


def solution(mesh):
    in_specs = (P(None, "row", "col", None), P(), P(), P(), P(), P(), P(), P(), P(), P())
    out_specs = P(None, "row", "col", None)
    return jax.shard_map(local, mesh=mesh, in_specs=in_specs, out_specs=out_specs, check_vma=False)
```

```python
import functools
import math

import jax
import jax.numpy as jnp
from jax import lax
from jax.experimental import pallas as pl
from jax.experimental.pallas import tpu as pltpu
from jax.sharding import PartitionSpec as P

viscosity = 0.4
quad = 4

VMEM = pltpu.VMEM
SMEM = pltpu.SMEM


def halves(value):
    high = value.astype(jnp.bfloat16)
    low = (value - high.astype(jnp.float32)).astype(jnp.bfloat16)
    return high, low


def dot_split(left, right, transposed=False):
    dims = (((1,), (1 if transposed else 0,)), ((), ()))
    mul = functools.partial(lax.dot_general, dimension_numbers=dims, preferred_element_type=jnp.float32)
    lh, ll = halves(left)
    rh, rl = halves(right)
    return mul(lh, rh) + (mul(lh, rl) + mul(ll, rh))


def span_kernel(comps, sources, pieces, matrix, *refs):
    fields, parts = refs[:sources], refs[sources:]
    depth, length = fields[0].shape[0] // comps, fields[0].shape[1]
    group = matrix.shape[0] // quad
    right = []
    for comp in range(comps):
        for at in range(0, depth, group):
            stack = [field[comp * depth + at : comp * depth + at + group] for field in fields]
            stack += [value * field[2 * depth + at : 2 * depth + at + group] for value, field in zip(stack, fields)]
            right.append(jnp.concatenate(stack, axis=0))
    result = dot_split(matrix[...], jnp.concatenate(right, axis=1))
    for part, (t, low, high) in zip(parts, pieces):
        for at in range(low, high, group):
            i = at // group
            part[at - low : at - low + group] = result[t * group : (t + 1) * group, i * length : (i + 1) * length]


def circulant_rows(row, length):
    return pltpu.roll(jnp.broadcast_to(row, (length, length)), 0, 1, stride=1, stride_axis=0)


def stream_kernel(
    cols, comps, zloc, wall_counts, z_first, z_second, field, x_first, x_second, x_part, z_matrix, mask, held
):
    held[...] = field[...]
    depth = mask.shape[0]
    length = field.shape[1]
    count = wall_counts[lax.axis_index("row")]
    mask[...] = (lax.broadcasted_iota(jnp.int32, mask.shape, 0) // zloc < count).astype(jnp.float32)

    cells_z = cols * zloc
    shape = z_matrix.shape
    half = shape[1] // 2
    group = shape[0] // quad
    mine = lax.axis_index("col")
    r = lax.broadcasted_iota(jnp.int32, shape, 0)
    q = lax.broadcasted_iota(jnp.int32, shape, 1)
    q = jnp.where(q < half, q, q - half)
    out_cell = ((r // group) ^ mine) * zloc + r % zloc
    in_cell = ((quad * (q // group)) ^ mine) * zloc + q % zloc
    same = (r % group) // zloc == (q % group) // zloc
    gap = jnp.where(same, (in_cell - out_cell + cells_z) % cells_z, -1)
    kind = lax.broadcasted_iota(jnp.int32, (1, shape[1]), 1) < half

    def fill(k, total):
        value = jnp.where(kind, viscosity * z_second[k], -z_first[k])
        return jnp.where(gap == k, value, total)

    z_matrix[...] = lax.fori_loop(0, cells_z, fill, jnp.zeros(shape, jnp.float32), unroll=8)

    u = field[...]
    lead = u[:depth]
    left = jnp.concatenate(
        [u, jnp.concatenate([lead * u[c * depth : (c + 1) * depth] for c in range(comps)], axis=0)], axis=1
    )
    right = jnp.concatenate(
        [viscosity * circulant_rows(x_second[...], length), -circulant_rows(x_first[...], length)], axis=1
    )
    x_part[...] = dot_split(left, right, transposed=True)


def wall_matrix_kernel(rows, zloc, wall_counts, metric_table, metric_index, y_first, y_second, after, matrix):
    cells = y_first.shape[0]
    depth = matrix.shape[0] // 2
    me = lax.axis_index("row")
    plain = functools.partial(
        lax.dot_general, dimension_numbers=(((1,), (0,)), ((), ())), preferred_element_type=jnp.float32
    )
    turned = functools.partial(
        lax.dot_general, dimension_numbers=(((1,), (1,)), ((), ())), preferred_element_type=jnp.float32
    )

    def spots(index):
        start = lax.fori_loop(0, rows, lambda i, acc: acc + jnp.where(i < index, wall_counts[i], 0), 0, unroll=True)
        plane = lax.broadcasted_iota(jnp.int32, (depth, cells), 0) // zloc
        cell = lax.broadcasted_iota(jnp.int32, (depth, cells), 1)
        return ((plane < wall_counts[index]) & (plane + start == cell)).astype(jnp.float32)

    levels = metric_table.shape[1]
    entry = (lax.broadcasted_iota(jnp.int32, (levels, cells), 0) == metric_index[...]).astype(jnp.float32)
    table = jnp.broadcast_to(metric_table[...], (8, levels))
    metric = plain(table, entry, precision=lax.Precision.HIGHEST)[:1]
    ends = jnp.concatenate([spots(me), spots(me ^ 1)], axis=0)
    scale = jnp.sum(ends * metric, axis=1, keepdims=True)
    pick = ends.astype(jnp.bfloat16)
    second = sum(plain(pick, part) for part in halves(viscosity * y_second[...]))
    first = -scale * sum(plain(pick, part) for part in halves(y_first[...]))
    other = jnp.concatenate([spots(me ^ step) for step in range(0, rows, 2)], axis=0).astype(jnp.bfloat16)
    wide = sum(turned(part, other) for part in halves(jnp.concatenate([second, first], axis=0)))
    match = lax.broadcasted_iota(jnp.int32, wide.shape, 0) % zloc == lax.broadcasted_iota(jnp.int32, wide.shape, 1) % zloc
    wide = jnp.where(match, wide, 0.0)
    for b in range(rows // 2):
        for k in range(2):
            matrix[:, (2 * b + k) * depth : (2 * b + k + 1) * depth] = wide[
                2 * k * depth : 2 * (k + 1) * depth, b * depth : (b + 1) * depth
            ]


def wall_kernel(comps, matrix, x_part, z_part, *refs):
    fields, (total, away) = refs[:-2], refs[-2:]
    depth = x_part.shape[0] // comps
    for comp in range(comps):
        at = slice(comp * depth, (comp + 1) * depth)
        stack = []
        for field in fields:
            stack += [field[at], field[depth : 2 * depth] * field[at]]
        result = dot_split(matrix[...], jnp.concatenate(stack, axis=0))
        total[at] = x_part[at] + z_part[at] + result[:depth]
        away[at] = result[depth:]


def sum_kernel(comps, pieces, mask, total, *refs):
    parts, out = refs[:-1], refs[-1]
    depth = mask.shape[0]
    for comp in range(comps):
        at = slice(comp * depth, (comp + 1) * depth)
        value = total[at]
        for part, (_, low, high) in zip(parts, pieces):
            if low <= at.start and at.stop <= high:
                value += part[at.start - low : at.stop - low]
        out[at] = jnp.where(mask[...] > 0, value, 0.0)


def finish_kernel(total, near, out):
    out[...] = total[...] + near[...]


def call(kernel, operands, spaces, results, name, scratch=(), cost=None):
    results = [jax.ShapeDtypeStruct(shape, jnp.float32) for shape in results]
    held = sum(4 * math.prod(array.shape) for array in list(operands) + results)
    return pl.pallas_call(
        kernel,
        out_shape=results,
        in_specs=[pl.BlockSpec(memory_space=space) for space in spaces],
        out_specs=[pl.BlockSpec(memory_space=VMEM)] * len(results),
        scratch_shapes=[pltpu.VMEM(shape, jnp.float32) for shape in scratch],
        compiler_params=pltpu.CompilerParams(vmem_limit_bytes=(4 << 20) + 3 * held),
        cost_estimate=cost,
        name=name,
    )(*operands)


def local(
    velocity,
    wall_counts,
    x_first,
    x_second,
    y_first,
    y_second,
    z_first,
    z_second,
    metric_table,
    metric_index,
):
    rows = lax.axis_size("row")
    cols = lax.axis_size("col")
    comps, slots, zloc, length = velocity.shape
    depth = slots * zloc
    field = velocity.reshape(comps * depth, length)
    group = min(depth, 32)
    sources = cols // quad
    rest = comps * depth
    pieces = [(t, 0, rest) for t in (0, 3, 2)] + [(1, 0, rest - depth), (1, rest - depth, rest)]

    def along(value, step):
        return lax.ppermute(value, "col", [(i, i ^ step) for i in range(cols)])

    def across(value, step):
        return lax.ppermute(value, "row", [(i, i ^ step) for i in range(rows)])

    gathered = [along(field, quad * i) for i in range(1, sources)]
    x_part, z_matrix, mask, held = call(
        functools.partial(stream_kernel, cols, comps, zloc),
        [wall_counts, z_first, z_second, field, x_first.reshape(1, length), x_second.reshape(1, length)],
        [SMEM] * 3 + [VMEM] * 3,
        [field.shape, (quad * group, 2 * sources * group), (depth, length), field.shape],
        "stream",
    )
    far = [across(held, step) for step in range(2, rows, 2)]
    parts = call(
        functools.partial(span_kernel, comps, sources, pieces),
        [z_matrix, field] + gathered,
        [VMEM] * (1 + sources),
        [(high - low, length) for _, low, high in pieces],
        "span",
    )
    returned = [along(part, t) for part, (t, _, _) in zip(parts[1:], pieces[1:])]
    (y_matrix,) = call(
        functools.partial(wall_matrix_kernel, rows, zloc),
        [wall_counts, metric_table.reshape(1, -1), metric_index.reshape(1, -1), y_first, y_second, parts[0]],
        [SMEM] + [VMEM] * 4 + [pl.ANY],
        [(2 * depth, rows * depth)],
        "wall_matrix",
    )
    total, away = call(
        functools.partial(wall_kernel, comps),
        [y_matrix, x_part, parts[0], field] + far,
        [VMEM] * (4 + len(far)),
        [field.shape] * 2,
        "wall",
    )
    near = across(away, 1)
    (summed,) = call(
        functools.partial(sum_kernel, comps, pieces[1:]),
        [mask, total] + returned,
        [VMEM] * (2 + len(returned)),
        [field.shape],
        "sum",
        cost=pl.CostEstimate(flops=1 << 30, bytes_accessed=1 << 22, transcendentals=0),
    )
    (result,) = call(finish_kernel, [summed, near], [VMEM] * 2, [field.shape], "finish")
    return result.reshape(velocity.shape)


def solution(mesh):
    in_specs = (P(None, "row", "col", None), P(), P(), P(), P(), P(), P(), P(), P(), P())
    out_specs = P(None, "row", "col", None)
    return jax.shard_map(local, mesh=mesh, in_specs=in_specs, out_specs=out_specs, check_vma=False)
```

```python
import functools
import math

import jax
import jax.numpy as jnp
from jax import lax
from jax.experimental import pallas as pl
from jax.experimental.pallas import tpu as pltpu
from jax.sharding import PartitionSpec as P

viscosity = 0.4
quad = 4

VMEM = pltpu.VMEM
SMEM = pltpu.SMEM


def halves(value):
    high = value.astype(jnp.bfloat16)
    low = (value - high.astype(jnp.float32)).astype(jnp.bfloat16)
    return high, low


def dot_split(left, right, transposed=False):
    dims = (((1,), (1 if transposed else 0,)), ((), ()))
    mul = functools.partial(lax.dot_general, dimension_numbers=dims, preferred_element_type=jnp.float32)
    lh, ll = halves(left)
    rh, rl = halves(right)
    return mul(lh, rh) + (mul(lh, rl) + mul(ll, rh))


def span_kernel(comps, across, pieces, matrix, *refs):
    fields, parts = refs[:quad], refs[quad:]
    depth, length = fields[0].shape[0] // comps, fields[0].shape[1]
    group = matrix.shape[0] // across
    right = []
    for comp in range(comps):
        for at in range(0, depth, group):
            stack = [field[comp * depth + at : comp * depth + at + group] for field in fields]
            stack += [value * field[2 * depth + at : 2 * depth + at + group] for value, field in zip(stack, fields)]
            right.append(jnp.concatenate(stack, axis=0))
    result = dot_split(matrix[...], jnp.concatenate(right, axis=1))
    for part, (t, low, high) in zip(parts, pieces):
        for at in range(low, high, group):
            i = at // group
            part[at - low : at - low + group] = result[t * group : (t + 1) * group, i * length : (i + 1) * length]


def circulant_rows(row, length):
    return pltpu.roll(jnp.broadcast_to(row, (length, length)), 0, 1, stride=1, stride_axis=0)


def stream_kernel(
    cols, comps, zloc, wall_counts, z_first, z_second, field, x_first, x_second, x_part, z_matrix, mask, held
):
    held[...] = field[...]
    depth = mask.shape[0]
    length = field.shape[1]
    count = wall_counts[lax.axis_index("row")]
    mask[...] = (lax.broadcasted_iota(jnp.int32, mask.shape, 0) // zloc < count).astype(jnp.float32)

    cells_z = cols * zloc
    shape = z_matrix.shape
    half = shape[1] // 2
    group = half // quad
    mine = lax.axis_index("col")
    r = lax.broadcasted_iota(jnp.int32, shape, 0)
    q = lax.broadcasted_iota(jnp.int32, shape, 1)
    q = jnp.where(q < half, q, q - half)
    out_cell = ((quad * (r // group)) ^ mine) * zloc + r % zloc
    in_cell = ((q // group) ^ mine) * zloc + q % zloc
    same = (r % group) // zloc == (q % group) // zloc
    gap = jnp.where(same, (in_cell - out_cell + cells_z) % cells_z, -1)
    kind = lax.broadcasted_iota(jnp.int32, (1, shape[1]), 1) < half

    def fill(k, total):
        value = jnp.where(kind, viscosity * z_second[k], -z_first[k])
        return jnp.where(gap == k, value, total)

    z_matrix[...] = lax.fori_loop(0, cells_z, fill, jnp.zeros(shape, jnp.float32), unroll=8)

    u = field[...]
    lead = u[:depth]
    left = jnp.concatenate(
        [u, jnp.concatenate([lead * u[c * depth : (c + 1) * depth] for c in range(comps)], axis=0)], axis=1
    )
    right = jnp.concatenate(
        [viscosity * circulant_rows(x_second[...], length), -circulant_rows(x_first[...], length)], axis=1
    )
    x_part[...] = dot_split(left, right, transposed=True)


def wall_matrix_kernel(rows, zloc, wall_counts, metric_table, metric_index, y_first, y_second, after, matrix):
    cells = y_first.shape[0]
    depth = matrix.shape[0] // 2
    me = lax.axis_index("row")
    plain = functools.partial(
        lax.dot_general, dimension_numbers=(((1,), (0,)), ((), ())), preferred_element_type=jnp.float32
    )
    turned = functools.partial(
        lax.dot_general, dimension_numbers=(((1,), (1,)), ((), ())), preferred_element_type=jnp.float32
    )

    def spots(index):
        start = lax.fori_loop(0, rows, lambda i, acc: acc + jnp.where(i < index, wall_counts[i], 0), 0, unroll=True)
        plane = lax.broadcasted_iota(jnp.int32, (depth, cells), 0) // zloc
        cell = lax.broadcasted_iota(jnp.int32, (depth, cells), 1)
        return ((plane < wall_counts[index]) & (plane + start == cell)).astype(jnp.float32)

    levels = metric_table.shape[1]
    entry = (lax.broadcasted_iota(jnp.int32, (levels, cells), 0) == metric_index[...]).astype(jnp.float32)
    table = jnp.broadcast_to(metric_table[...], (8, levels))
    metric = plain(table, entry, precision=lax.Precision.HIGHEST)[:1]
    ends = jnp.concatenate([spots(me), spots(me ^ 1)], axis=0)
    scale = jnp.sum(ends * metric, axis=1, keepdims=True)
    pick = ends.astype(jnp.bfloat16)
    second = sum(plain(pick, part) for part in halves(viscosity * y_second[...]))
    first = -scale * sum(plain(pick, part) for part in halves(y_first[...]))
    other = jnp.concatenate([spots(me ^ step) for step in range(0, rows, 2)], axis=0).astype(jnp.bfloat16)
    wide = sum(turned(part, other) for part in halves(jnp.concatenate([second, first], axis=0)))
    match = lax.broadcasted_iota(jnp.int32, wide.shape, 0) % zloc == lax.broadcasted_iota(jnp.int32, wide.shape, 1) % zloc
    wide = jnp.where(match, wide, 0.0)
    for b in range(rows // 2):
        for k in range(2):
            matrix[:, (2 * b + k) * depth : (2 * b + k + 1) * depth] = wide[
                2 * k * depth : 2 * (k + 1) * depth, b * depth : (b + 1) * depth
            ]


def wall_kernel(comps, matrix, x_part, z_part, *refs):
    fields, (total, away) = refs[:-2], refs[-2:]
    depth = x_part.shape[0] // comps
    for comp in range(comps):
        at = slice(comp * depth, (comp + 1) * depth)
        stack = []
        for field in fields:
            stack += [field[at], field[depth : 2 * depth] * field[at]]
        result = dot_split(matrix[...], jnp.concatenate(stack, axis=0))
        total[at] = x_part[at] + z_part[at] + result[:depth]
        away[at] = result[depth:]


def sum_kernel(comps, pieces, mask, total, *refs):
    parts, out = refs[:-1], refs[-1]
    depth = mask.shape[0]
    for comp in range(comps):
        at = slice(comp * depth, (comp + 1) * depth)
        value = total[at]
        for part, (_, low, high) in zip(parts, pieces):
            if low <= at.start and at.stop <= high:
                value += part[at.start - low : at.stop - low]
        out[at] = jnp.where(mask[...] > 0, value, 0.0)


def finish_kernel(total, near, out):
    out[...] = total[...] + near[...]


def call(kernel, operands, spaces, results, name, scratch=(), cost=None):
    results = [jax.ShapeDtypeStruct(shape, jnp.float32) for shape in results]
    held = sum(4 * math.prod(array.shape) for array in list(operands) + results)
    return pl.pallas_call(
        kernel,
        out_shape=results,
        in_specs=[pl.BlockSpec(memory_space=space) for space in spaces],
        out_specs=[pl.BlockSpec(memory_space=VMEM)] * len(results),
        scratch_shapes=[pltpu.VMEM(shape, jnp.float32) for shape in scratch],
        compiler_params=pltpu.CompilerParams(vmem_limit_bytes=(4 << 20) + 3 * held),
        cost_estimate=cost,
        name=name,
    )(*operands)


def local(
    velocity,
    wall_counts,
    x_first,
    x_second,
    y_first,
    y_second,
    z_first,
    z_second,
    metric_table,
    metric_index,
):
    rows = lax.axis_size("row")
    cols = lax.axis_size("col")
    comps, slots, zloc, length = velocity.shape
    depth = slots * zloc
    field = velocity.reshape(comps * depth, length)
    group = min(depth, 32)
    wide = cols // quad
    rest = comps * depth
    pieces = [(0, 0, rest)]
    for t in range(1, wide):
        pieces += [(t, 0, rest - depth), (t, rest - depth, rest)]

    def along(value, step):
        return lax.ppermute(value, "col", [(i, i ^ step) for i in range(cols)])

    def across(value, step):
        return lax.ppermute(value, "row", [(i, i ^ step) for i in range(rows)])

    gathered = [along(field, t) for t in range(1, quad)]
    x_part, z_matrix, mask, held = call(
        functools.partial(stream_kernel, cols, comps, zloc),
        [wall_counts, z_first, z_second, field, x_first.reshape(1, length), x_second.reshape(1, length)],
        [SMEM] * 3 + [VMEM] * 3,
        [field.shape, (wide * group, 2 * quad * group), (depth, length), field.shape],
        "stream",
    )
    far = [across(held, step) for step in range(2, rows, 2)]
    parts = call(
        functools.partial(span_kernel, comps, wide, pieces),
        [z_matrix, field] + gathered,
        [VMEM] * (1 + quad),
        [(high - low, length) for _, low, high in pieces],
        "span",
    )
    returned = [along(part, quad * t) for part, (t, _, _) in zip(parts[1:], pieces[1:])]
    (y_matrix,) = call(
        functools.partial(wall_matrix_kernel, rows, zloc),
        [wall_counts, metric_table.reshape(1, -1), metric_index.reshape(1, -1), y_first, y_second, parts[0]],
        [SMEM] + [VMEM] * 4 + [pl.ANY],
        [(2 * depth, rows * depth)],
        "wall_matrix",
    )
    total, away = call(
        functools.partial(wall_kernel, comps),
        [y_matrix, x_part, parts[0], field] + far,
        [VMEM] * (4 + len(far)),
        [field.shape] * 2,
        "wall",
    )
    near = across(away, 1)
    (summed,) = call(
        functools.partial(sum_kernel, comps, pieces[1:]),
        [mask, total] + returned,
        [VMEM] * (2 + len(returned)),
        [field.shape],
        "sum",
        cost=pl.CostEstimate(flops=1 << 30, bytes_accessed=1 << 22, transcendentals=0),
    )
    (result,) = call(finish_kernel, [summed, near], [VMEM] * 2, [field.shape], "finish")
    return result.reshape(velocity.shape)


def solution(mesh):
    in_specs = (P(None, "row", "col", None), P(), P(), P(), P(), P(), P(), P(), P(), P())
    out_specs = P(None, "row", "col", None)
    return jax.shard_map(local, mesh=mesh, in_specs=in_specs, out_specs=out_specs, check_vma=False)
```

```python
import functools
import math

import jax
import jax.numpy as jnp
from jax import lax
from jax.experimental import pallas as pl
from jax.experimental.pallas import tpu as pltpu
from jax.sharding import PartitionSpec as P

viscosity = 0.4
quad = 4

VMEM = pltpu.VMEM
SMEM = pltpu.SMEM


def halves(value):
    high = value.astype(jnp.bfloat16)
    low = (value - high.astype(jnp.float32)).astype(jnp.bfloat16)
    return high, low


def dot_split(left, right, transposed=False):
    dims = (((1,), (1 if transposed else 0,)), ((), ()))
    mul = functools.partial(lax.dot_general, dimension_numbers=dims, preferred_element_type=jnp.float32)
    lh, ll = halves(left)
    rh, rl = halves(right)
    return mul(lh, rh) + (mul(lh, rl) + mul(ll, rh))


def span_kernel(comps, across, pieces, matrix, *refs):
    fields, parts = refs[:quad], refs[quad:]
    depth, length = fields[0].shape[0] // comps, fields[0].shape[1]
    group = matrix.shape[0] // across
    right = []
    for comp in range(comps):
        for at in range(0, depth, group):
            stack = [field[comp * depth + at : comp * depth + at + group] for field in fields]
            stack += [value * field[2 * depth + at : 2 * depth + at + group] for value, field in zip(stack, fields)]
            right.append(jnp.concatenate(stack, axis=0))
    result = dot_split(matrix[...], jnp.concatenate(right, axis=1))
    for part, (t, low, high) in zip(parts, pieces):
        for at in range(low, high, group):
            i = at // group
            part[at - low : at - low + group] = result[t * group : (t + 1) * group, i * length : (i + 1) * length]


def circulant_rows(row, length):
    return pltpu.roll(jnp.broadcast_to(row, (length, length)), 0, 1, stride=1, stride_axis=0)


def span_matrix_kernel(cols, zloc, wall_counts, z_first, z_second, field, z_matrix, mask, held):
    held[...] = field[...]
    count = wall_counts[lax.axis_index("row")]
    mask[...] = (lax.broadcasted_iota(jnp.int32, mask.shape, 0) // zloc < count).astype(jnp.float32)

    cells_z = cols * zloc
    shape = z_matrix.shape
    half = shape[1] // 2
    group = half // quad
    mine = lax.axis_index("col")
    r = lax.broadcasted_iota(jnp.int32, shape, 0)
    q = lax.broadcasted_iota(jnp.int32, shape, 1)
    q = jnp.where(q < half, q, q - half)
    out_cell = ((quad * (r // group)) ^ mine) * zloc + r % zloc
    in_cell = ((q // group) ^ mine) * zloc + q % zloc
    same = (r % group) // zloc == (q % group) // zloc
    gap = jnp.where(same, (in_cell - out_cell + cells_z) % cells_z, -1)
    kind = lax.broadcasted_iota(jnp.int32, (1, shape[1]), 1) < half

    def fill(k, total):
        value = jnp.where(kind, viscosity * z_second[k], -z_first[k])
        return jnp.where(gap == k, value, total)

    z_matrix[...] = lax.fori_loop(0, cells_z, fill, jnp.zeros(shape, jnp.float32), unroll=8)


def stream_kernel(comps, field, x_first, x_second, after, x_part):
    length = field.shape[1]
    depth = field.shape[0] // comps
    u = field[...]
    lead = u[:depth]
    left = jnp.concatenate(
        [u, jnp.concatenate([lead * u[c * depth : (c + 1) * depth] for c in range(comps)], axis=0)], axis=1
    )
    right = jnp.concatenate(
        [viscosity * circulant_rows(x_second[...], length), -circulant_rows(x_first[...], length)], axis=1
    )
    x_part[...] = dot_split(left, right, transposed=True)


def wall_matrix_kernel(rows, zloc, wall_counts, metric_table, metric_index, y_first, y_second, after, matrix):
    cells = y_first.shape[0]
    depth = matrix.shape[0] // 2
    me = lax.axis_index("row")
    plain = functools.partial(
        lax.dot_general, dimension_numbers=(((1,), (0,)), ((), ())), preferred_element_type=jnp.float32
    )
    turned = functools.partial(
        lax.dot_general, dimension_numbers=(((1,), (1,)), ((), ())), preferred_element_type=jnp.float32
    )

    def spots(index):
        start = lax.fori_loop(0, rows, lambda i, acc: acc + jnp.where(i < index, wall_counts[i], 0), 0, unroll=True)
        plane = lax.broadcasted_iota(jnp.int32, (depth, cells), 0) // zloc
        cell = lax.broadcasted_iota(jnp.int32, (depth, cells), 1)
        return ((plane < wall_counts[index]) & (plane + start == cell)).astype(jnp.float32)

    levels = metric_table.shape[1]
    entry = (lax.broadcasted_iota(jnp.int32, (levels, cells), 0) == metric_index[...]).astype(jnp.float32)
    table = jnp.broadcast_to(metric_table[...], (8, levels))
    metric = plain(table, entry, precision=lax.Precision.HIGHEST)[:1]
    ends = jnp.concatenate([spots(me), spots(me ^ 1)], axis=0)
    scale = jnp.sum(ends * metric, axis=1, keepdims=True)
    pick = ends.astype(jnp.bfloat16)
    second = sum(plain(pick, part) for part in halves(viscosity * y_second[...]))
    first = -scale * sum(plain(pick, part) for part in halves(y_first[...]))
    other = jnp.concatenate([spots(me ^ step) for step in range(0, rows, 2)], axis=0).astype(jnp.bfloat16)
    wide = sum(turned(part, other) for part in halves(jnp.concatenate([second, first], axis=0)))
    match = lax.broadcasted_iota(jnp.int32, wide.shape, 0) % zloc == lax.broadcasted_iota(jnp.int32, wide.shape, 1) % zloc
    wide = jnp.where(match, wide, 0.0)
    for b in range(rows // 2):
        for k in range(2):
            matrix[:, (2 * b + k) * depth : (2 * b + k + 1) * depth] = wide[
                2 * k * depth : 2 * (k + 1) * depth, b * depth : (b + 1) * depth
            ]


def wall_kernel(comps, matrix, x_part, z_part, *refs):
    fields, (total, away) = refs[:-2], refs[-2:]
    depth = x_part.shape[0] // comps
    for comp in range(comps):
        at = slice(comp * depth, (comp + 1) * depth)
        stack = []
        for field in fields:
            stack += [field[at], field[depth : 2 * depth] * field[at]]
        result = dot_split(matrix[...], jnp.concatenate(stack, axis=0))
        total[at] = x_part[at] + z_part[at] + result[:depth]
        away[at] = result[depth:]


def sum_kernel(comps, pieces, mask, total, *refs):
    parts, out = refs[:-1], refs[-1]
    depth = mask.shape[0]
    for comp in range(comps):
        at = slice(comp * depth, (comp + 1) * depth)
        value = total[at]
        for part, (_, low, high) in zip(parts, pieces):
            if low <= at.start and at.stop <= high:
                value += part[at.start - low : at.stop - low]
        out[at] = jnp.where(mask[...] > 0, value, 0.0)


def finish_kernel(total, near, out):
    out[...] = total[...] + near[...]


def call(kernel, operands, spaces, results, name, scratch=(), cost=None):
    results = [jax.ShapeDtypeStruct(shape, jnp.float32) for shape in results]
    held = sum(4 * math.prod(array.shape) for array in list(operands) + results)
    return pl.pallas_call(
        kernel,
        out_shape=results,
        in_specs=[pl.BlockSpec(memory_space=space) for space in spaces],
        out_specs=[pl.BlockSpec(memory_space=VMEM)] * len(results),
        scratch_shapes=[pltpu.VMEM(shape, jnp.float32) for shape in scratch],
        compiler_params=pltpu.CompilerParams(vmem_limit_bytes=(4 << 20) + 3 * held),
        cost_estimate=cost,
        name=name,
    )(*operands)


def local(
    velocity,
    wall_counts,
    x_first,
    x_second,
    y_first,
    y_second,
    z_first,
    z_second,
    metric_table,
    metric_index,
):
    rows = lax.axis_size("row")
    cols = lax.axis_size("col")
    comps, slots, zloc, length = velocity.shape
    depth = slots * zloc
    field = velocity.reshape(comps * depth, length)
    group = min(depth, 32)
    wide = cols // quad
    pieces = [(t, 0, comps * depth) for t in range(wide)]

    def along(value, step):
        return lax.ppermute(value, "col", [(i, i ^ step) for i in range(cols)])

    def across(value, step):
        return lax.ppermute(value, "row", [(i, i ^ step) for i in range(rows)])

    gathered = [along(field, t) for t in range(1, quad)]
    z_matrix, mask, held = call(
        functools.partial(span_matrix_kernel, cols, zloc),
        [wall_counts, z_first, z_second, field],
        [SMEM] * 3 + [VMEM],
        [(wide * group, 2 * quad * group), (depth, length), field.shape],
        "span_matrix",
    )
    far = [across(held, step) for step in range(2, rows, 2)]
    parts = call(
        functools.partial(span_kernel, comps, wide, pieces),
        [z_matrix, field] + gathered,
        [VMEM] * (1 + quad),
        [(high - low, length) for _, low, high in pieces],
        "span",
    )
    returned = [along(part, quad * t) for part, (t, _, _) in zip(parts[1:], pieces[1:])]
    (x_part,) = call(
        functools.partial(stream_kernel, comps),
        [field, x_first.reshape(1, length), x_second.reshape(1, length), parts[0]],
        [VMEM] * 3 + [pl.ANY],
        [field.shape],
        "stream",
    )
    (y_matrix,) = call(
        functools.partial(wall_matrix_kernel, rows, zloc),
        [wall_counts, metric_table.reshape(1, -1), metric_index.reshape(1, -1), y_first, y_second, parts[0]],
        [SMEM] + [VMEM] * 4 + [pl.ANY],
        [(2 * depth, rows * depth)],
        "wall_matrix",
    )
    total, away = call(
        functools.partial(wall_kernel, comps),
        [y_matrix, x_part, parts[0], field] + far,
        [VMEM] * (4 + len(far)),
        [field.shape] * 2,
        "wall",
    )
    near = across(away, 1)
    (summed,) = call(
        functools.partial(sum_kernel, comps, pieces[1:]),
        [mask, total] + returned,
        [VMEM] * (2 + len(returned)),
        [field.shape],
        "sum",
        cost=pl.CostEstimate(flops=1 << 30, bytes_accessed=1 << 22, transcendentals=0),
    )
    (result,) = call(finish_kernel, [summed, near], [VMEM] * 2, [field.shape], "finish")
    return result.reshape(velocity.shape)


def solution(mesh):
    in_specs = (P(None, "row", "col", None), P(), P(), P(), P(), P(), P(), P(), P(), P())
    out_specs = P(None, "row", "col", None)
    return jax.shard_map(local, mesh=mesh, in_specs=in_specs, out_specs=out_specs, check_vma=False)
```

```python
import functools
import math

import jax
import jax.numpy as jnp
from jax import lax
from jax.experimental import pallas as pl
from jax.experimental.pallas import tpu as pltpu
from jax.sharding import PartitionSpec as P

viscosity = 0.4
quad = 4

VMEM = pltpu.VMEM
SMEM = pltpu.SMEM


def halves(value):
    high = value.astype(jnp.bfloat16)
    low = (value - high.astype(jnp.float32)).astype(jnp.bfloat16)
    return high, low


def dot_split(left, right, transposed=False):
    dims = (((1,), (1 if transposed else 0,)), ((), ()))
    mul = functools.partial(lax.dot_general, dimension_numbers=dims, preferred_element_type=jnp.float32)
    lh, ll = halves(left)
    rh, rl = halves(right)
    both = mul(jnp.concatenate([lh, ll], axis=0), rh)
    count = left.shape[0]
    return both[:count] + (mul(lh, rl) + both[count:])


def quad_sums(comps, matrix, fields, chosen):
    depth, length = fields[0].shape[0] // comps, fields[0].shape[1]
    half = matrix.shape[1] // 2
    group = half // quad
    left = jnp.concatenate(
        [matrix[:, start + s * group : start + (s + 1) * group] for start in (0, half) for s in chosen], axis=1
    )
    right = []
    for comp in range(comps):
        for at in range(0, depth, group):
            stack = [field[comp * depth + at : comp * depth + at + group] for field in fields]
            stack += [value * field[2 * depth + at : 2 * depth + at + group] for value, field in zip(stack, fields)]
            right.append(jnp.concatenate(stack, axis=0))
    return dot_split(left, jnp.concatenate(right, axis=1))


def early_kernel(comps, chosen, matrix, *refs):
    refs[-1][...] = quad_sums(comps, matrix, refs[:-1], chosen)


def span_kernel(comps, chosen, matrix, early, *refs):
    fields, parts = refs[: len(chosen)], refs[len(chosen) :]
    result = early[...] + quad_sums(comps, matrix, fields, chosen)
    rows, length = parts[0].shape
    count = len(parts)
    group = result.shape[0] // count
    for t in range(count):
        for i in range(rows // group):
            parts[t][i * group : (i + 1) * group] = result[
                t * group : (t + 1) * group, i * length : (i + 1) * length
            ]


def circulant_rows(row, length):
    return pltpu.roll(jnp.broadcast_to(row, (length, length)), 0, 1, stride=1, stride_axis=0)


def span_matrix_kernel(cols, zloc, wall_counts, z_first, z_second, field, z_matrix, mask, held):
    held[...] = field[...]
    count = wall_counts[lax.axis_index("row")]
    mask[...] = (lax.broadcasted_iota(jnp.int32, mask.shape, 0) // zloc < count).astype(jnp.float32)

    cells_z = cols * zloc
    shape = z_matrix.shape
    half = shape[1] // 2
    group = half // quad
    mine = lax.axis_index("col")
    r = lax.broadcasted_iota(jnp.int32, shape, 0)
    q = lax.broadcasted_iota(jnp.int32, shape, 1)
    q = jnp.where(q < half, q, q - half)
    out_cell = ((quad * (r // group)) ^ mine) * zloc + r % zloc
    in_cell = ((q // group) ^ mine) * zloc + q % zloc
    same = (r % group) // zloc == (q % group) // zloc
    gap = jnp.where(same, (in_cell - out_cell + cells_z) % cells_z, -1)
    kind = lax.broadcasted_iota(jnp.int32, (1, shape[1]), 1) < half

    def fill(k, total):
        value = jnp.where(kind, viscosity * z_second[k], -z_first[k])
        return jnp.where(gap == k, value, total)

    z_matrix[...] = lax.fori_loop(0, cells_z, fill, jnp.zeros(shape, jnp.float32), unroll=8)


def stream_kernel(comps, field, x_first, x_second, after, x_part):
    length = field.shape[1]
    depth = field.shape[0] // comps
    u = field[...]
    lead = u[:depth]
    left = jnp.concatenate(
        [u, jnp.concatenate([lead * u[c * depth : (c + 1) * depth] for c in range(comps)], axis=0)], axis=1
    )
    right = jnp.concatenate(
        [viscosity * circulant_rows(x_second[...], length), -circulant_rows(x_first[...], length)], axis=1
    )
    x_part[...] = dot_split(left, right, transposed=True)


def wall_matrix_kernel(rows, zloc, wall_counts, metric_table, metric_index, y_first, y_second, after, matrix):
    cells = y_first.shape[0]
    depth = matrix.shape[0] // 2
    me = lax.axis_index("row")
    plain = functools.partial(
        lax.dot_general, dimension_numbers=(((1,), (0,)), ((), ())), preferred_element_type=jnp.float32
    )
    turned = functools.partial(
        lax.dot_general, dimension_numbers=(((1,), (1,)), ((), ())), preferred_element_type=jnp.float32
    )

    def spots(index):
        start = lax.fori_loop(0, rows, lambda i, acc: acc + jnp.where(i < index, wall_counts[i], 0), 0, unroll=True)
        plane = lax.broadcasted_iota(jnp.int32, (depth, cells), 0) // zloc
        cell = lax.broadcasted_iota(jnp.int32, (depth, cells), 1)
        return ((plane < wall_counts[index]) & (plane + start == cell)).astype(jnp.float32)

    levels = metric_table.shape[1]
    entry = (lax.broadcasted_iota(jnp.int32, (levels, cells), 0) == metric_index[...]).astype(jnp.float32)
    table = jnp.broadcast_to(metric_table[...], (8, levels))
    metric = plain(table, entry, precision=lax.Precision.HIGHEST)[:1]
    ends = jnp.concatenate([spots(me), spots(me ^ 1)], axis=0)
    scale = jnp.sum(ends * metric, axis=1, keepdims=True)
    pick = ends.astype(jnp.bfloat16)
    second = sum(plain(pick, part) for part in halves(viscosity * y_second[...]))
    first = -scale * sum(plain(pick, part) for part in halves(y_first[...]))
    other = jnp.concatenate([spots(me ^ step) for step in range(0, rows, 2)], axis=0).astype(jnp.bfloat16)
    wide = sum(turned(part, other) for part in halves(jnp.concatenate([second, first], axis=0)))
    match = lax.broadcasted_iota(jnp.int32, wide.shape, 0) % zloc == lax.broadcasted_iota(jnp.int32, wide.shape, 1) % zloc
    wide = jnp.where(match, wide, 0.0)
    for b in range(rows // 2):
        for k in range(2):
            matrix[:, (2 * b + k) * depth : (2 * b + k + 1) * depth] = wide[
                2 * k * depth : 2 * (k + 1) * depth, b * depth : (b + 1) * depth
            ]


def wall_kernel(comps, matrix, x_part, z_part, *refs):
    fields, (total, away) = refs[:-2], refs[-2:]
    depth = x_part.shape[0] // comps
    for comp in range(comps):
        at = slice(comp * depth, (comp + 1) * depth)
        stack = []
        for field in fields:
            stack += [field[at], field[depth : 2 * depth] * field[at]]
        result = dot_split(matrix[...], jnp.concatenate(stack, axis=0))
        total[at] = x_part[at] + z_part[at] + result[:depth]
        away[at] = result[depth:]


def sum_kernel(comps, mask, *refs):
    parts, out = refs[:-1], refs[-1]
    depth = mask.shape[0]
    for comp in range(comps):
        at = slice(comp * depth, (comp + 1) * depth)
        out[at] = jnp.where(mask[...] > 0, sum(part[at] for part in parts[1:]) + parts[0][at], 0.0)


def finish_kernel(total, near, out):
    out[...] = total[...] + near[...]


def call(kernel, operands, spaces, results, name, scratch=(), cost=None):
    results = [jax.ShapeDtypeStruct(shape, jnp.float32) for shape in results]
    held = sum(4 * math.prod(array.shape) for array in list(operands) + results)
    return pl.pallas_call(
        kernel,
        out_shape=results,
        in_specs=[pl.BlockSpec(memory_space=space) for space in spaces],
        out_specs=[pl.BlockSpec(memory_space=VMEM)] * len(results),
        scratch_shapes=[pltpu.VMEM(shape, jnp.float32) for shape in scratch],
        compiler_params=pltpu.CompilerParams(vmem_limit_bytes=(4 << 20) + 3 * held),
        cost_estimate=cost,
        name=name,
    )(*operands)


def local(
    velocity,
    wall_counts,
    x_first,
    x_second,
    y_first,
    y_second,
    z_first,
    z_second,
    metric_table,
    metric_index,
):
    rows = lax.axis_size("row")
    cols = lax.axis_size("col")
    comps, slots, zloc, length = velocity.shape
    depth = slots * zloc
    field = velocity.reshape(comps * depth, length)
    group = min(depth, 32)
    wide = cols // quad

    def along(value, step):
        return lax.ppermute(value, "col", [(i, i ^ step) for i in range(cols)])

    def across(value, step):
        return lax.ppermute(value, "row", [(i, i ^ step) for i in range(rows)])

    gathered = [along(field, t) for t in range(1, quad)]
    z_matrix, mask, held = call(
        functools.partial(span_matrix_kernel, cols, zloc),
        [wall_counts, z_first, z_second, field],
        [SMEM] * 3 + [VMEM],
        [(wide * group, 2 * quad * group), (depth, length), field.shape],
        "span_matrix",
    )
    far = [across(held, step) for step in range(2, rows, 2)]
    (early,) = call(
        functools.partial(early_kernel, comps, (0, quad - 1)),
        [z_matrix, field, gathered[-1]],
        [VMEM] * 3,
        [(wide * group, comps * (depth // group) * length)],
        "early",
    )
    parts = call(
        functools.partial(span_kernel, comps, tuple(range(1, quad - 1))),
        [z_matrix, early] + gathered[:-1],
        [VMEM] * quad,
        [field.shape] * wide,
        "span",
    )
    returned = [along(parts[t], quad * t) for t in range(1, wide)]
    (x_part,) = call(
        functools.partial(stream_kernel, comps),
        [field, x_first.reshape(1, length), x_second.reshape(1, length), parts[0]],
        [VMEM] * 3 + [pl.ANY],
        [field.shape],
        "stream",
    )
    (y_matrix,) = call(
        functools.partial(wall_matrix_kernel, rows, zloc),
        [wall_counts, metric_table.reshape(1, -1), metric_index.reshape(1, -1), y_first, y_second, parts[0]],
        [SMEM] + [VMEM] * 4 + [pl.ANY],
        [(2 * depth, rows * depth)],
        "wall_matrix",
    )
    total, away = call(
        functools.partial(wall_kernel, comps),
        [y_matrix, x_part, parts[0], field] + far,
        [VMEM] * (4 + len(far)),
        [field.shape] * 2,
        "wall",
    )
    near = across(away, 1)
    (summed,) = call(
        functools.partial(sum_kernel, comps),
        [mask, total] + returned,
        [VMEM] * (2 + len(returned)),
        [field.shape],
        "sum",
        cost=pl.CostEstimate(flops=1 << 30, bytes_accessed=1 << 22, transcendentals=0),
    )
    (result,) = call(finish_kernel, [summed, near], [VMEM] * 2, [field.shape], "finish")
    return result.reshape(velocity.shape)


def solution(mesh):
    in_specs = (P(None, "row", "col", None), P(), P(), P(), P(), P(), P(), P(), P(), P())
    out_specs = P(None, "row", "col", None)
    return jax.shard_map(local, mesh=mesh, in_specs=in_specs, out_specs=out_specs, check_vma=False)
```

```python
import functools
import math

import jax
import jax.numpy as jnp
from jax import lax
from jax.experimental import pallas as pl
from jax.experimental.pallas import tpu as pltpu
from jax.sharding import PartitionSpec as P

viscosity = 0.4
quad = 4

VMEM = pltpu.VMEM
SMEM = pltpu.SMEM


def halves(value):
    high = value.astype(jnp.bfloat16)
    low = (value - high.astype(jnp.float32)).astype(jnp.bfloat16)
    return high, low


def dot_split(left, right, transposed=False):
    dims = (((1,), (1 if transposed else 0,)), ((), ()))
    mul = functools.partial(lax.dot_general, dimension_numbers=dims, preferred_element_type=jnp.float32)
    lh, ll = halves(left)
    rh, rl = halves(right)
    both = mul(jnp.concatenate([lh, ll], axis=0), rh)
    count = left.shape[0]
    return both[:count] + (mul(lh, rl) + both[count:])


def quad_sums(comps, matrix, fields, chosen):
    depth, length = fields[0].shape[0] // comps, fields[0].shape[1]
    half = matrix.shape[1] // 2
    group = half // quad
    left = jnp.concatenate(
        [matrix[:, start + s * group : start + (s + 1) * group] for start in (0, half) for s in chosen], axis=1
    )
    right = []
    for comp in range(comps):
        for at in range(0, depth, group):
            stack = [field[comp * depth + at : comp * depth + at + group] for field in fields]
            stack += [value * field[2 * depth + at : 2 * depth + at + group] for value, field in zip(stack, fields)]
            right.append(jnp.concatenate(stack, axis=0))
    return dot_split(left, jnp.concatenate(right, axis=1))


def early_kernel(comps, chosen, matrix, *refs):
    refs[-1][...] = quad_sums(comps, matrix, refs[:-1], chosen)


def span_kernel(comps, chosen, matrix, early, *refs):
    fields, parts = refs[: len(chosen)], refs[len(chosen) :]
    result = early[...] + quad_sums(comps, matrix, fields, chosen)
    rows, length = parts[0].shape
    count = len(parts)
    group = result.shape[0] // count
    for t in range(count):
        for i in range(rows // group):
            parts[t][i * group : (i + 1) * group] = result[
                t * group : (t + 1) * group, i * length : (i + 1) * length
            ]


def circulant_rows(row, length):
    return pltpu.roll(jnp.broadcast_to(row, (length, length)), 0, 1, stride=1, stride_axis=0)


def span_matrix_kernel(cols, zloc, wall_counts, z_first, z_second, field, z_matrix, mask, held):
    held[...] = field[...]
    count = wall_counts[lax.axis_index("row")]
    mask[...] = (lax.broadcasted_iota(jnp.int32, mask.shape, 0) // zloc < count).astype(jnp.float32)

    cells_z = cols * zloc
    shape = z_matrix.shape
    half = shape[1] // 2
    group = half // quad
    mine = lax.axis_index("col")
    r = lax.broadcasted_iota(jnp.int32, shape, 0)
    q = lax.broadcasted_iota(jnp.int32, shape, 1)
    q = jnp.where(q < half, q, q - half)
    out_cell = ((quad * (r // group)) ^ mine) * zloc + r % zloc
    in_cell = ((q // group) ^ mine) * zloc + q % zloc
    same = (r % group) // zloc == (q % group) // zloc
    gap = jnp.where(same, (in_cell - out_cell + cells_z) % cells_z, -1)
    kind = lax.broadcasted_iota(jnp.int32, (1, shape[1]), 1) < half

    def fill(k, total):
        value = jnp.where(kind, viscosity * z_second[k], -z_first[k])
        return jnp.where(gap == k, value, total)

    z_matrix[...] = lax.fori_loop(0, cells_z, fill, jnp.zeros(shape, jnp.float32), unroll=8)


def stream_kernel(comps, field, x_first, x_second, after, x_part):
    length = field.shape[1]
    depth = field.shape[0] // comps
    u = field[...]
    lead = u[:depth]
    left = jnp.concatenate(
        [u, jnp.concatenate([lead * u[c * depth : (c + 1) * depth] for c in range(comps)], axis=0)], axis=1
    )
    right = jnp.concatenate(
        [viscosity * circulant_rows(x_second[...], length), -circulant_rows(x_first[...], length)], axis=1
    )
    x_part[...] = dot_split(left, right, transposed=True)


def wall_matrix_kernel(rows, zloc, wall_counts, metric_table, metric_index, y_first, y_second, after, matrix):
    cells = y_first.shape[0]
    depth = matrix.shape[0] // 2
    me = lax.axis_index("row")
    plain = functools.partial(
        lax.dot_general, dimension_numbers=(((1,), (0,)), ((), ())), preferred_element_type=jnp.float32
    )
    turned = functools.partial(
        lax.dot_general, dimension_numbers=(((1,), (1,)), ((), ())), preferred_element_type=jnp.float32
    )

    def spots(index):
        start = lax.fori_loop(0, rows, lambda i, acc: acc + jnp.where(i < index, wall_counts[i], 0), 0, unroll=True)
        plane = lax.broadcasted_iota(jnp.int32, (depth, cells), 0) // zloc
        cell = lax.broadcasted_iota(jnp.int32, (depth, cells), 1)
        return ((plane < wall_counts[index]) & (plane + start == cell)).astype(jnp.float32)

    levels = metric_table.shape[1]
    entry = (lax.broadcasted_iota(jnp.int32, (levels, cells), 0) == metric_index[...]).astype(jnp.float32)
    table = jnp.broadcast_to(metric_table[...], (8, levels))
    metric = plain(table, entry, precision=lax.Precision.HIGHEST)[:1]
    ends = jnp.concatenate([spots(me), spots(me ^ 1)], axis=0)
    scale = jnp.sum(ends * metric, axis=1, keepdims=True)
    pick = ends.astype(jnp.bfloat16)
    second = sum(plain(pick, part) for part in halves(viscosity * y_second[...]))
    first = -scale * sum(plain(pick, part) for part in halves(y_first[...]))
    other = jnp.concatenate([spots(me ^ step) for step in range(0, rows, 2)], axis=0).astype(jnp.bfloat16)
    wide = sum(turned(part, other) for part in halves(jnp.concatenate([second, first], axis=0)))
    match = lax.broadcasted_iota(jnp.int32, wide.shape, 0) % zloc == lax.broadcasted_iota(jnp.int32, wide.shape, 1) % zloc
    wide = jnp.where(match, wide, 0.0)
    for b in range(rows // 2):
        for k in range(2):
            matrix[:, (2 * b + k) * depth : (2 * b + k + 1) * depth] = wide[
                2 * k * depth : 2 * (k + 1) * depth, b * depth : (b + 1) * depth
            ]


def wall_kernel(comps, matrix, x_part, z_part, *refs):
    fields, (total, away) = refs[:-2], refs[-2:]
    depth = x_part.shape[0] // comps
    for comp in range(comps):
        at = slice(comp * depth, (comp + 1) * depth)
        stack = []
        for field in fields:
            stack += [field[at], field[depth : 2 * depth] * field[at]]
        result = dot_split(matrix[...], jnp.concatenate(stack, axis=0))
        total[at] = x_part[at] + z_part[at] + result[:depth]
        away[at] = result[depth:]


def sum_kernel(comps, mask, *refs):
    parts, out = refs[:-1], refs[-1]
    depth = mask.shape[0]
    for comp in range(comps):
        at = slice(comp * depth, (comp + 1) * depth)
        out[at] = jnp.where(mask[...] > 0, sum(part[at] for part in parts[1:]) + parts[0][at], 0.0)


def finish_kernel(total, near, out):
    out[...] = total[...] + near[...]


def call(kernel, operands, spaces, results, name, scratch=(), cost=None):
    results = [jax.ShapeDtypeStruct(shape, jnp.float32) for shape in results]
    held = sum(4 * math.prod(array.shape) for array in list(operands) + results)
    return pl.pallas_call(
        kernel,
        out_shape=results,
        in_specs=[pl.BlockSpec(memory_space=space) for space in spaces],
        out_specs=[pl.BlockSpec(memory_space=VMEM)] * len(results),
        scratch_shapes=[pltpu.VMEM(shape, jnp.float32) for shape in scratch],
        compiler_params=pltpu.CompilerParams(vmem_limit_bytes=(4 << 20) + 3 * held),
        cost_estimate=cost,
        name=name,
    )(*operands)


def local(
    velocity,
    wall_counts,
    x_first,
    x_second,
    y_first,
    y_second,
    z_first,
    z_second,
    metric_table,
    metric_index,
):
    rows = lax.axis_size("row")
    cols = lax.axis_size("col")
    comps, slots, zloc, length = velocity.shape
    depth = slots * zloc
    field = velocity.reshape(comps * depth, length)
    group = min(depth, 32)
    wide = cols // quad

    def along(value, step):
        return lax.ppermute(value, "col", [(i, i ^ step) for i in range(cols)])

    def across(value, step):
        return lax.ppermute(value, "row", [(i, i ^ step) for i in range(rows)])

    gathered = [along(field, t) for t in range(1, quad)]
    z_matrix, mask, held = call(
        functools.partial(span_matrix_kernel, cols, zloc),
        [wall_counts, z_first, z_second, field],
        [SMEM] * 3 + [VMEM],
        [(wide * group, 2 * quad * group), (depth, length), field.shape],
        "span_matrix",
    )
    far = [across(held, step) for step in range(2, rows, 2)]
    (early,) = call(
        functools.partial(early_kernel, comps, (0, quad - 1)),
        [z_matrix, field, gathered[-1]],
        [VMEM] * 3,
        [(wide * group, comps * (depth // group) * length)],
        "early",
    )
    parts = call(
        functools.partial(span_kernel, comps, tuple(range(quad - 2, 0, -1))),
        [z_matrix, early] + gathered[-2::-1],
        [VMEM] * quad,
        [field.shape] * wide,
        "span",
    )
    returned = [along(parts[t], quad * t) for t in range(1, wide)]
    (x_part,) = call(
        functools.partial(stream_kernel, comps),
        [field, x_first.reshape(1, length), x_second.reshape(1, length), parts[0]],
        [VMEM] * 3 + [pl.ANY],
        [field.shape],
        "stream",
    )
    (y_matrix,) = call(
        functools.partial(wall_matrix_kernel, rows, zloc),
        [wall_counts, metric_table.reshape(1, -1), metric_index.reshape(1, -1), y_first, y_second, parts[0]],
        [SMEM] + [VMEM] * 4 + [pl.ANY],
        [(2 * depth, rows * depth)],
        "wall_matrix",
    )
    total, away = call(
        functools.partial(wall_kernel, comps),
        [y_matrix, x_part, parts[0], field] + far,
        [VMEM] * (4 + len(far)),
        [field.shape] * 2,
        "wall",
    )
    near = across(away, 1)
    (summed,) = call(
        functools.partial(sum_kernel, comps),
        [mask, total] + returned,
        [VMEM] * (2 + len(returned)),
        [field.shape],
        "sum",
        cost=pl.CostEstimate(flops=1 << 30, bytes_accessed=1 << 22, transcendentals=0),
    )
    (result,) = call(finish_kernel, [summed, near], [VMEM] * 2, [field.shape], "finish")
    return result.reshape(velocity.shape)


def solution(mesh):
    in_specs = (P(None, "row", "col", None), P(), P(), P(), P(), P(), P(), P(), P(), P())
    out_specs = P(None, "row", "col", None)
    return jax.shard_map(local, mesh=mesh, in_specs=in_specs, out_specs=out_specs, check_vma=False)
```

```python
import functools
import math

import jax
import jax.numpy as jnp
from jax import lax
from jax.experimental import pallas as pl
from jax.experimental.pallas import tpu as pltpu
from jax.sharding import PartitionSpec as P

viscosity = 0.4
quad = 4

VMEM = pltpu.VMEM
SMEM = pltpu.SMEM


def halves(value):
    high = value.astype(jnp.bfloat16)
    low = (value - high.astype(jnp.float32)).astype(jnp.bfloat16)
    return high, low


def dot_split(left, right, transposed=False):
    dims = (((1,), (1 if transposed else 0,)), ((), ()))
    mul = functools.partial(lax.dot_general, dimension_numbers=dims, preferred_element_type=jnp.float32)
    lh, ll = halves(left)
    rh, rl = halves(right)
    both = mul(jnp.concatenate([lh, ll], axis=0), rh)
    count = left.shape[0]
    return both[:count] + (mul(lh, rl) + both[count:])


def over(t):
    return quad * t + 2 * (t != 0)


def quad_sums(comps, matrix, fields, chosen):
    depth, length = fields[0].shape[0] // comps, fields[0].shape[1]
    half = matrix.shape[1] // 2
    group = half // quad
    left = jnp.concatenate(
        [matrix[:, start + s * group : start + (s + 1) * group] for start in (0, half) for s in chosen], axis=1
    )
    right = []
    for comp in range(comps):
        for at in range(0, depth, group):
            stack = [field[comp * depth + at : comp * depth + at + group] for field in fields]
            stack += [value * field[2 * depth + at : 2 * depth + at + group] for value, field in zip(stack, fields)]
            right.append(jnp.concatenate(stack, axis=0))
    return dot_split(left, jnp.concatenate(right, axis=1))


def early_kernel(comps, chosen, matrix, *refs):
    refs[-1][...] = quad_sums(comps, matrix, refs[:-1], chosen)


def span_kernel(comps, chosen, matrix, early, *refs):
    fields, parts = refs[: len(chosen)], refs[len(chosen) :]
    result = early[...] + quad_sums(comps, matrix, fields, chosen)
    rows, length = parts[0].shape
    count = len(parts)
    group = result.shape[0] // count
    for t in range(count):
        for i in range(rows // group):
            parts[t][i * group : (i + 1) * group] = result[
                t * group : (t + 1) * group, i * length : (i + 1) * length
            ]


def circulant_rows(row, length):
    return pltpu.roll(jnp.broadcast_to(row, (length, length)), 0, 1, stride=1, stride_axis=0)


def span_matrix_kernel(cols, zloc, wall_counts, z_first, z_second, field, z_matrix, mask, held):
    held[...] = field[...]
    count = wall_counts[lax.axis_index("row")]
    mask[...] = (lax.broadcasted_iota(jnp.int32, mask.shape, 0) // zloc < count).astype(jnp.float32)

    cells_z = cols * zloc
    shape = z_matrix.shape
    half = shape[1] // 2
    group = half // quad
    mine = lax.axis_index("col")
    r = lax.broadcasted_iota(jnp.int32, shape, 0)
    q = lax.broadcasted_iota(jnp.int32, shape, 1)
    q = jnp.where(q < half, q, q - half)
    out_cell = (over(r // group) ^ mine) * zloc + r % zloc
    in_cell = ((q // group) ^ mine) * zloc + q % zloc
    same = (r % group) // zloc == (q % group) // zloc
    gap = jnp.where(same, (in_cell - out_cell + cells_z) % cells_z, -1)
    kind = lax.broadcasted_iota(jnp.int32, (1, shape[1]), 1) < half

    def fill(k, total):
        value = jnp.where(kind, viscosity * z_second[k], -z_first[k])
        return jnp.where(gap == k, value, total)

    z_matrix[...] = lax.fori_loop(0, cells_z, fill, jnp.zeros(shape, jnp.float32), unroll=8)


def stream_kernel(comps, field, x_first, x_second, after, x_part):
    length = field.shape[1]
    depth = field.shape[0] // comps
    u = field[...]
    lead = u[:depth]
    left = jnp.concatenate(
        [u, jnp.concatenate([lead * u[c * depth : (c + 1) * depth] for c in range(comps)], axis=0)], axis=1
    )
    right = jnp.concatenate(
        [viscosity * circulant_rows(x_second[...], length), -circulant_rows(x_first[...], length)], axis=1
    )
    x_part[...] = dot_split(left, right, transposed=True)


def wall_matrix_kernel(rows, zloc, wall_counts, metric_table, metric_index, y_first, y_second, after, matrix):
    cells = y_first.shape[0]
    depth = matrix.shape[0] // 2
    me = lax.axis_index("row")
    plain = functools.partial(
        lax.dot_general, dimension_numbers=(((1,), (0,)), ((), ())), preferred_element_type=jnp.float32
    )
    turned = functools.partial(
        lax.dot_general, dimension_numbers=(((1,), (1,)), ((), ())), preferred_element_type=jnp.float32
    )

    def spots(index):
        start = lax.fori_loop(0, rows, lambda i, acc: acc + jnp.where(i < index, wall_counts[i], 0), 0, unroll=True)
        plane = lax.broadcasted_iota(jnp.int32, (depth, cells), 0) // zloc
        cell = lax.broadcasted_iota(jnp.int32, (depth, cells), 1)
        return ((plane < wall_counts[index]) & (plane + start == cell)).astype(jnp.float32)

    levels = metric_table.shape[1]
    entry = (lax.broadcasted_iota(jnp.int32, (levels, cells), 0) == metric_index[...]).astype(jnp.float32)
    table = jnp.broadcast_to(metric_table[...], (8, levels))
    metric = plain(table, entry, precision=lax.Precision.HIGHEST)[:1]
    ends = jnp.concatenate([spots(me), spots(me ^ 1)], axis=0)
    scale = jnp.sum(ends * metric, axis=1, keepdims=True)
    pick = ends.astype(jnp.bfloat16)
    second = sum(plain(pick, part) for part in halves(viscosity * y_second[...]))
    first = -scale * sum(plain(pick, part) for part in halves(y_first[...]))
    other = jnp.concatenate([spots(me ^ step) for step in range(0, rows, 2)], axis=0).astype(jnp.bfloat16)
    wide = sum(turned(part, other) for part in halves(jnp.concatenate([second, first], axis=0)))
    match = lax.broadcasted_iota(jnp.int32, wide.shape, 0) % zloc == lax.broadcasted_iota(jnp.int32, wide.shape, 1) % zloc
    wide = jnp.where(match, wide, 0.0)
    for b in range(rows // 2):
        for k in range(2):
            matrix[:, (2 * b + k) * depth : (2 * b + k + 1) * depth] = wide[
                2 * k * depth : 2 * (k + 1) * depth, b * depth : (b + 1) * depth
            ]


def wall_kernel(comps, matrix, x_part, z_part, *refs):
    fields, (total, away) = refs[:-2], refs[-2:]
    depth = x_part.shape[0] // comps
    for comp in range(comps):
        at = slice(comp * depth, (comp + 1) * depth)
        stack = []
        for field in fields:
            stack += [field[at], field[depth : 2 * depth] * field[at]]
        result = dot_split(matrix[...], jnp.concatenate(stack, axis=0))
        total[at] = x_part[at] + z_part[at] + result[:depth]
        away[at] = result[depth:]


def sum_kernel(comps, mask, *refs):
    parts, out = refs[:-1], refs[-1]
    depth = mask.shape[0]
    for comp in range(comps):
        at = slice(comp * depth, (comp + 1) * depth)
        out[at] = jnp.where(mask[...] > 0, sum(part[at] for part in parts[1:]) + parts[0][at], 0.0)


def finish_kernel(total, near, out):
    out[...] = total[...] + near[...]


def call(kernel, operands, spaces, results, name, scratch=(), cost=None):
    results = [jax.ShapeDtypeStruct(shape, jnp.float32) for shape in results]
    held = sum(4 * math.prod(array.shape) for array in list(operands) + results)
    return pl.pallas_call(
        kernel,
        out_shape=results,
        in_specs=[pl.BlockSpec(memory_space=space) for space in spaces],
        out_specs=[pl.BlockSpec(memory_space=VMEM)] * len(results),
        scratch_shapes=[pltpu.VMEM(shape, jnp.float32) for shape in scratch],
        compiler_params=pltpu.CompilerParams(vmem_limit_bytes=(4 << 20) + 3 * held),
        cost_estimate=cost,
        name=name,
    )(*operands)


def local(
    velocity,
    wall_counts,
    x_first,
    x_second,
    y_first,
    y_second,
    z_first,
    z_second,
    metric_table,
    metric_index,
):
    rows = lax.axis_size("row")
    cols = lax.axis_size("col")
    comps, slots, zloc, length = velocity.shape
    depth = slots * zloc
    field = velocity.reshape(comps * depth, length)
    group = min(depth, 32)
    wide = cols // quad

    def along(value, step):
        return lax.ppermute(value, "col", [(i, i ^ step) for i in range(cols)])

    def across(value, step):
        return lax.ppermute(value, "row", [(i, i ^ step) for i in range(rows)])

    gathered = [along(field, t) for t in range(1, quad)]
    z_matrix, mask, held = call(
        functools.partial(span_matrix_kernel, cols, zloc),
        [wall_counts, z_first, z_second, field],
        [SMEM] * 3 + [VMEM],
        [(wide * group, 2 * quad * group), (depth, length), field.shape],
        "span_matrix",
    )
    far = [across(held, step) for step in range(2, rows, 2)]
    (early,) = call(
        functools.partial(early_kernel, comps, (0, quad - 1)),
        [z_matrix, field, gathered[-1]],
        [VMEM] * 3,
        [(wide * group, comps * (depth // group) * length)],
        "early",
    )
    parts = call(
        functools.partial(span_kernel, comps, tuple(range(1, quad - 1))),
        [z_matrix, early] + gathered[:-1],
        [VMEM] * quad,
        [field.shape] * wide,
        "span",
    )
    returned = [along(parts[t], over(t)) for t in range(1, wide)]
    (x_part,) = call(
        functools.partial(stream_kernel, comps),
        [field, x_first.reshape(1, length), x_second.reshape(1, length), parts[0]],
        [VMEM] * 3 + [pl.ANY],
        [field.shape],
        "stream",
    )
    (y_matrix,) = call(
        functools.partial(wall_matrix_kernel, rows, zloc),
        [wall_counts, metric_table.reshape(1, -1), metric_index.reshape(1, -1), y_first, y_second, parts[0]],
        [SMEM] + [VMEM] * 4 + [pl.ANY],
        [(2 * depth, rows * depth)],
        "wall_matrix",
    )
    total, away = call(
        functools.partial(wall_kernel, comps),
        [y_matrix, x_part, parts[0], field] + far,
        [VMEM] * (4 + len(far)),
        [field.shape] * 2,
        "wall",
    )
    near = across(away, 1)
    (summed,) = call(
        functools.partial(sum_kernel, comps),
        [mask, total] + returned,
        [VMEM] * (2 + len(returned)),
        [field.shape],
        "sum",
        cost=pl.CostEstimate(flops=1 << 30, bytes_accessed=1 << 22, transcendentals=0),
    )
    (result,) = call(finish_kernel, [summed, near], [VMEM] * 2, [field.shape], "finish")
    return result.reshape(velocity.shape)


def solution(mesh):
    in_specs = (P(None, "row", "col", None), P(), P(), P(), P(), P(), P(), P(), P(), P())
    out_specs = P(None, "row", "col", None)
    return jax.shard_map(local, mesh=mesh, in_specs=in_specs, out_specs=out_specs, check_vma=False)
```

```python
import functools
import math

import jax
import jax.numpy as jnp
from jax import lax
from jax.experimental import pallas as pl
from jax.experimental.pallas import tpu as pltpu
from jax.sharding import PartitionSpec as P

viscosity = 0.4
quad = 4

VMEM = pltpu.VMEM
SMEM = pltpu.SMEM


def halves(value):
    high = value.astype(jnp.bfloat16)
    low = (value - high.astype(jnp.float32)).astype(jnp.bfloat16)
    return high, low


def dot_split(left, right, transposed=False):
    dims = (((1,), (1 if transposed else 0,)), ((), ()))
    mul = functools.partial(lax.dot_general, dimension_numbers=dims, preferred_element_type=jnp.float32)
    lh, ll = halves(left)
    rh, rl = halves(right)
    both = mul(jnp.concatenate([lh, ll], axis=0), rh)
    count = left.shape[0]
    return both[:count] + (mul(lh, rl) + both[count:])


def over(t):
    return quad * t + 2 * (t != 0)


def quad_sums(comps, matrix, fields, chosen):
    depth, length = fields[0].shape[0] // comps, fields[0].shape[1]
    half = matrix.shape[1] // 2
    group = half // quad
    left = jnp.concatenate(
        [matrix[:, start + s * group : start + (s + 1) * group] for start in (0, half) for s in chosen], axis=1
    )
    right = []
    for comp in range(comps):
        for at in range(0, depth, group):
            stack = [field[comp * depth + at : comp * depth + at + group] for field in fields]
            stack += [value * field[2 * depth + at : 2 * depth + at + group] for value, field in zip(stack, fields)]
            right.append(jnp.concatenate(stack, axis=0))
    return dot_split(left, jnp.concatenate(right, axis=1))


def early_kernel(comps, chosen, matrix, *refs):
    refs[-1][...] = quad_sums(comps, matrix, refs[:-1], chosen)


def span_kernel(comps, chosen, matrix, early, *refs):
    fields, parts = refs[: len(chosen)], refs[len(chosen) :]
    result = early[...] + quad_sums(comps, matrix, fields, chosen)
    rows, length = parts[0].shape
    count = len(parts)
    group = result.shape[0] // count
    for t in range(count):
        for i in range(rows // group):
            parts[t][i * group : (i + 1) * group] = result[
                t * group : (t + 1) * group, i * length : (i + 1) * length
            ]


def circulant_rows(row, length):
    return pltpu.roll(jnp.broadcast_to(row, (length, length)), 0, 1, stride=1, stride_axis=0)


def span_matrix_kernel(cols, zloc, wall_counts, z_first, z_second, field, z_matrix, mask, held):
    held[...] = field[...]
    count = wall_counts[lax.axis_index("row")]
    mask[...] = (lax.broadcasted_iota(jnp.int32, mask.shape, 0) // zloc < count).astype(jnp.float32)

    cells_z = cols * zloc
    shape = z_matrix.shape
    half = shape[1] // 2
    group = half // quad
    mine = lax.axis_index("col")
    r = lax.broadcasted_iota(jnp.int32, shape, 0)
    q = lax.broadcasted_iota(jnp.int32, shape, 1)
    q = jnp.where(q < half, q, q - half)
    out_cell = (over(r // group) ^ mine) * zloc + r % zloc
    in_cell = ((q // group) ^ mine) * zloc + q % zloc
    same = (r % group) // zloc == (q % group) // zloc
    gap = jnp.where(same, (in_cell - out_cell + cells_z) % cells_z, -1)
    kind = lax.broadcasted_iota(jnp.int32, (1, shape[1]), 1) < half

    def fill(k, total):
        value = jnp.where(kind, viscosity * z_second[k], -z_first[k])
        return jnp.where(gap == k, value, total)

    z_matrix[...] = lax.fori_loop(0, cells_z, fill, jnp.zeros(shape, jnp.float32), unroll=8)


def stream_kernel(comps, field, x_first, x_second, after, x_part):
    length = field.shape[1]
    depth = field.shape[0] // comps
    u = field[...]
    lead = u[:depth]
    left = jnp.concatenate(
        [u, jnp.concatenate([lead * u[c * depth : (c + 1) * depth] for c in range(comps)], axis=0)], axis=1
    )
    right = jnp.concatenate(
        [viscosity * circulant_rows(x_second[...], length), -circulant_rows(x_first[...], length)], axis=1
    )
    x_part[...] = dot_split(left, right, transposed=True)


def wall_matrix_kernel(rows, zloc, wall_counts, metric_table, metric_index, y_first, y_second, after, matrix):
    cells = y_first.shape[0]
    depth = matrix.shape[0] // 2
    me = lax.axis_index("row")
    plain = functools.partial(
        lax.dot_general, dimension_numbers=(((1,), (0,)), ((), ())), preferred_element_type=jnp.float32
    )
    turned = functools.partial(
        lax.dot_general, dimension_numbers=(((1,), (1,)), ((), ())), preferred_element_type=jnp.float32
    )

    def spots(index):
        start = lax.fori_loop(0, rows, lambda i, acc: acc + jnp.where(i < index, wall_counts[i], 0), 0, unroll=True)
        plane = lax.broadcasted_iota(jnp.int32, (depth, cells), 0) // zloc
        cell = lax.broadcasted_iota(jnp.int32, (depth, cells), 1)
        return ((plane < wall_counts[index]) & (plane + start == cell)).astype(jnp.float32)

    levels = metric_table.shape[1]
    entry = (lax.broadcasted_iota(jnp.int32, (levels, cells), 0) == metric_index[...]).astype(jnp.bfloat16)
    high, low = halves(metric_table[...])
    rest = (metric_table[...] - high.astype(jnp.float32) - low.astype(jnp.float32)).astype(jnp.bfloat16)
    table = jnp.concatenate([jnp.broadcast_to(part, (16, levels)) for part in (high, low, rest)], axis=0)
    metric = plain(table, entry)
    metric = metric[:1] + metric[16:17] + metric[32:33]
    ends = jnp.concatenate([spots(me), spots(me ^ 1)], axis=0)
    scale = jnp.sum(ends * metric, axis=1, keepdims=True)
    both = halves(jnp.concatenate([viscosity * y_second[...], y_first[...]], axis=1))
    picked = plain(ends.astype(jnp.bfloat16), jnp.concatenate(both, axis=1))
    picked = picked[:, : 2 * cells] + picked[:, 2 * cells :]
    second, first = picked[:, :cells], -scale * picked[:, cells:]
    other = jnp.concatenate([spots(me ^ step) for step in range(0, rows, 2)], axis=0).astype(jnp.bfloat16)
    wide = turned(jnp.concatenate(halves(jnp.concatenate([second, first], axis=0)), axis=0), other)
    wide = wide[: 4 * depth] + wide[4 * depth :]
    match = lax.broadcasted_iota(jnp.int32, wide.shape, 0) % zloc == lax.broadcasted_iota(jnp.int32, wide.shape, 1) % zloc
    wide = jnp.where(match, wide, 0.0)
    for b in range(rows // 2):
        for k in range(2):
            matrix[:, (2 * b + k) * depth : (2 * b + k + 1) * depth] = wide[
                2 * k * depth : 2 * (k + 1) * depth, b * depth : (b + 1) * depth
            ]


def wall_kernel(comps, matrix, z_part, *refs):
    fields, (total, away) = refs[:-2], refs[-2:]
    depth = z_part.shape[0] // comps
    for comp in range(comps):
        at = slice(comp * depth, (comp + 1) * depth)
        stack = []
        for field in fields:
            stack += [field[at], field[depth : 2 * depth] * field[at]]
        result = dot_split(matrix[...], jnp.concatenate(stack, axis=0))
        total[at] = z_part[at] + result[:depth]
        away[at] = result[depth:]


def sum_kernel(comps, mask, *refs):
    parts, out = refs[:-1], refs[-1]
    depth = mask.shape[0]
    for comp in range(comps):
        at = slice(comp * depth, (comp + 1) * depth)
        out[at] = jnp.where(mask[...] > 0, sum(part[at] for part in parts[1:]) + parts[0][at], 0.0)


def finish_kernel(total, near, out):
    out[...] = total[...] + near[...]


def call(kernel, operands, spaces, results, name, scratch=(), cost=None):
    results = [jax.ShapeDtypeStruct(shape, jnp.float32) for shape in results]
    held = sum(4 * math.prod(array.shape) for array in list(operands) + results)
    return pl.pallas_call(
        kernel,
        out_shape=results,
        in_specs=[pl.BlockSpec(memory_space=space) for space in spaces],
        out_specs=[pl.BlockSpec(memory_space=VMEM)] * len(results),
        scratch_shapes=[pltpu.VMEM(shape, jnp.float32) for shape in scratch],
        compiler_params=pltpu.CompilerParams(vmem_limit_bytes=(4 << 20) + 3 * held),
        cost_estimate=cost,
        name=name,
    )(*operands)


def local(
    velocity,
    wall_counts,
    x_first,
    x_second,
    y_first,
    y_second,
    z_first,
    z_second,
    metric_table,
    metric_index,
):
    rows = lax.axis_size("row")
    cols = lax.axis_size("col")
    comps, slots, zloc, length = velocity.shape
    depth = slots * zloc
    field = velocity.reshape(comps * depth, length)
    group = min(depth, 32)
    wide = cols // quad

    def along(value, step):
        return lax.ppermute(value, "col", [(i, i ^ step) for i in range(cols)])

    def across(value, step):
        return lax.ppermute(value, "row", [(i, i ^ step) for i in range(rows)])

    gathered = [along(field, t) for t in range(1, quad)]
    z_matrix, mask, held = call(
        functools.partial(span_matrix_kernel, cols, zloc),
        [wall_counts, z_first, z_second, field],
        [SMEM] * 3 + [VMEM],
        [(wide * group, 2 * quad * group), (depth, length), field.shape],
        "span_matrix",
    )
    far = [across(held, step) for step in range(2, rows, 2)]
    (early,) = call(
        functools.partial(early_kernel, comps, (0, quad - 1)),
        [z_matrix, field, gathered[-1]],
        [VMEM] * 3,
        [(wide * group, comps * (depth // group) * length)],
        "early",
    )
    parts = call(
        functools.partial(span_kernel, comps, tuple(range(1, quad - 1))),
        [z_matrix, early] + gathered[:-1],
        [VMEM] * quad,
        [field.shape] * wide,
        "span",
    )
    returned = [along(parts[t], over(t)) for t in range(1, wide)]
    (y_matrix,) = call(
        functools.partial(wall_matrix_kernel, rows, zloc),
        [wall_counts, metric_table.reshape(1, -1), metric_index.reshape(1, -1), y_first, y_second, parts[0]],
        [SMEM] + [VMEM] * 4 + [pl.ANY],
        [(2 * depth, rows * depth)],
        "wall_matrix",
    )
    total, away = call(
        functools.partial(wall_kernel, comps),
        [y_matrix, parts[0], field] + far,
        [VMEM] * (3 + len(far)),
        [field.shape] * 2,
        "wall",
    )
    near = across(away, 1)
    (x_part,) = call(
        functools.partial(stream_kernel, comps),
        [field, x_first.reshape(1, length), x_second.reshape(1, length), away],
        [VMEM] * 3 + [pl.ANY],
        [field.shape],
        "stream",
    )
    (summed,) = call(
        functools.partial(sum_kernel, comps),
        [mask, total, x_part] + returned,
        [VMEM] * (3 + len(returned)),
        [field.shape],
        "sum",
        cost=pl.CostEstimate(flops=1 << 30, bytes_accessed=1 << 22, transcendentals=0),
    )
    (result,) = call(finish_kernel, [summed, near], [VMEM] * 2, [field.shape], "finish")
    return result.reshape(velocity.shape)


def solution(mesh):
    in_specs = (P(None, "row", "col", None), P(), P(), P(), P(), P(), P(), P(), P(), P())
    out_specs = P(None, "row", "col", None)
    return jax.shard_map(local, mesh=mesh, in_specs=in_specs, out_specs=out_specs, check_vma=False)
```

```python
import functools
import math

import jax
import jax.numpy as jnp
from jax import lax
from jax.experimental import pallas as pl
from jax.experimental.pallas import tpu as pltpu
from jax.sharding import PartitionSpec as P

viscosity = 0.4
quad = 4

VMEM = pltpu.VMEM
SMEM = pltpu.SMEM


def halves(value):
    high = value.astype(jnp.bfloat16)
    low = (value - high.astype(jnp.float32)).astype(jnp.bfloat16)
    return high, low


def dot_split(left, right, transposed=False):
    dims = (((1,), (1 if transposed else 0,)), ((), ()))
    mul = functools.partial(lax.dot_general, dimension_numbers=dims, preferred_element_type=jnp.float32)
    lh, ll = halves(left)
    rh, rl = halves(right)
    both = mul(jnp.concatenate([lh, ll], axis=0), rh)
    count = left.shape[0]
    return both[:count] + (mul(lh, rl) + both[count:])


def over(t):
    return quad * t + 2 * (t != 0)


def quad_sums(comps, matrix, fields, chosen):
    depth, length = fields[0].shape[0] // comps, fields[0].shape[1]
    half = matrix.shape[1] // 2
    group = half // quad
    left = jnp.concatenate(
        [matrix[:, start + s * group : start + (s + 1) * group] for start in (0, half) for s in chosen], axis=1
    )
    right = []
    for comp in range(comps):
        for at in range(0, depth, group):
            stack = [field[comp * depth + at : comp * depth + at + group] for field in fields]
            stack += [value * field[2 * depth + at : 2 * depth + at + group] for value, field in zip(stack, fields)]
            right.append(jnp.concatenate(stack, axis=0))
    return dot_split(left, jnp.concatenate(right, axis=1))


def early_kernel(comps, chosen, matrix, *refs):
    refs[-1][...] = quad_sums(comps, matrix, refs[:-1], chosen)


def span_kernel(comps, chosen, matrix, early, *refs):
    fields, parts = refs[: len(chosen)], refs[len(chosen) :]
    result = early[...] + quad_sums(comps, matrix, fields, chosen)
    rows, length = parts[0].shape
    count = len(parts)
    group = result.shape[0] // count
    for t in range(count):
        for i in range(rows // group):
            parts[t][i * group : (i + 1) * group] = result[
                t * group : (t + 1) * group, i * length : (i + 1) * length
            ]


def circulant_rows(row, length):
    return pltpu.roll(jnp.broadcast_to(row, (length, length)), 0, 1, stride=1, stride_axis=0)


def span_matrix_kernel(
    rows, cols, zloc, wall_counts, z_first, z_second, field, z_matrix, mask, held, ends, others
):
    held[...] = field[...]
    me = lax.axis_index("row")
    mask[...] = (lax.broadcasted_iota(jnp.int32, mask.shape, 0) // zloc < wall_counts[me]).astype(jnp.float32)
    depth = mask.shape[0]
    plane = lax.broadcasted_iota(jnp.int32, (depth, ends.shape[1]), 0) // zloc
    cell = lax.broadcasted_iota(jnp.int32, (depth, ends.shape[1]), 1)

    def spots(index):
        start = lax.fori_loop(0, rows, lambda i, acc: acc + jnp.where(i < index, wall_counts[i], 0), 0, unroll=True)
        return ((plane < wall_counts[index]) & (plane + start == cell)).astype(jnp.float32)

    for i in range(2):
        ends[i * depth : (i + 1) * depth] = spots(me ^ i)
    for i in range(rows // 2):
        others[i * depth : (i + 1) * depth] = spots(me ^ (2 * i))

    cells_z = cols * zloc
    shape = z_matrix.shape
    half = shape[1] // 2
    group = half // quad
    mine = lax.axis_index("col")
    r = lax.broadcasted_iota(jnp.int32, shape, 0)
    q = lax.broadcasted_iota(jnp.int32, shape, 1)
    q = jnp.where(q < half, q, q - half)
    out_cell = (over(r // group) ^ mine) * zloc + r % zloc
    in_cell = ((q // group) ^ mine) * zloc + q % zloc
    same = (r % group) // zloc == (q % group) // zloc
    gap = jnp.where(same, (in_cell - out_cell + cells_z) % cells_z, -1)
    kind = lax.broadcasted_iota(jnp.int32, (1, shape[1]), 1) < half

    def fill(k, total):
        value = jnp.where(kind, viscosity * z_second[k], -z_first[k])
        return jnp.where(gap == k, value, total)

    z_matrix[...] = lax.fori_loop(0, cells_z, fill, jnp.zeros(shape, jnp.float32), unroll=8)


def stream_kernel(comps, field, x_first, x_second, after, x_part):
    length = field.shape[1]
    depth = field.shape[0] // comps
    u = field[...]
    lead = u[:depth]
    left = jnp.concatenate(
        [u, jnp.concatenate([lead * u[c * depth : (c + 1) * depth] for c in range(comps)], axis=0)], axis=1
    )
    right = jnp.concatenate(
        [viscosity * circulant_rows(x_second[...], length), -circulant_rows(x_first[...], length)], axis=1
    )
    x_part[...] = dot_split(left, right, transposed=True)


def wall_matrix_kernel(zloc, ends, others, metric_table, metric_index, y_first, y_second, after, matrix):
    cells = y_first.shape[0]
    depth = matrix.shape[0] // 2
    plain = functools.partial(
        lax.dot_general, dimension_numbers=(((1,), (0,)), ((), ())), preferred_element_type=jnp.float32
    )
    turned = functools.partial(
        lax.dot_general, dimension_numbers=(((1,), (1,)), ((), ())), preferred_element_type=jnp.float32
    )
    levels = metric_table.shape[1]
    entry = (lax.broadcasted_iota(jnp.int32, (levels, cells), 0) == metric_index[...]).astype(jnp.float32)
    table = jnp.broadcast_to(metric_table[...], (8, levels))
    metric = plain(table, entry, precision=lax.Precision.HIGHEST)[:1]
    scale = jnp.sum(ends[...] * metric, axis=1, keepdims=True)
    pick = ends[...].astype(jnp.bfloat16)
    second = sum(plain(pick, part) for part in halves(viscosity * y_second[...]))
    first = -scale * sum(plain(pick, part) for part in halves(y_first[...]))
    other = others[...].astype(jnp.bfloat16)
    wide = sum(turned(part, other) for part in halves(jnp.concatenate([second, first], axis=0)))
    match = lax.broadcasted_iota(jnp.int32, wide.shape, 0) % zloc == lax.broadcasted_iota(jnp.int32, wide.shape, 1) % zloc
    wide = jnp.where(match, wide, 0.0)
    for b in range(others.shape[0] // depth):
        for k in range(2):
            matrix[:, (2 * b + k) * depth : (2 * b + k + 1) * depth] = wide[
                2 * k * depth : 2 * (k + 1) * depth, b * depth : (b + 1) * depth
            ]


def wall_kernel(comps, matrix, z_part, *refs):
    fields, (total, away) = refs[:-2], refs[-2:]
    depth = z_part.shape[0] // comps
    for comp in range(comps):
        at = slice(comp * depth, (comp + 1) * depth)
        stack = []
        for field in fields:
            stack += [field[at], field[depth : 2 * depth] * field[at]]
        result = dot_split(matrix[...], jnp.concatenate(stack, axis=0))
        total[at] = z_part[at] + result[:depth]
        away[at] = result[depth:]


def sum_kernel(comps, mask, *refs):
    parts, out = refs[:-1], refs[-1]
    depth = mask.shape[0]
    for comp in range(comps):
        at = slice(comp * depth, (comp + 1) * depth)
        out[at] = jnp.where(mask[...] > 0, sum(part[at] for part in parts[1:]) + parts[0][at], 0.0)


def finish_kernel(total, near, out):
    out[...] = total[...] + near[...]


def call(kernel, operands, spaces, results, name, scratch=(), cost=None):
    results = [jax.ShapeDtypeStruct(shape, jnp.float32) for shape in results]
    held = sum(4 * math.prod(array.shape) for array in list(operands) + results)
    return pl.pallas_call(
        kernel,
        out_shape=results,
        in_specs=[pl.BlockSpec(memory_space=space) for space in spaces],
        out_specs=[pl.BlockSpec(memory_space=VMEM)] * len(results),
        scratch_shapes=[pltpu.VMEM(shape, jnp.float32) for shape in scratch],
        compiler_params=pltpu.CompilerParams(vmem_limit_bytes=(4 << 20) + 3 * held),
        cost_estimate=cost,
        name=name,
    )(*operands)


def local(
    velocity,
    wall_counts,
    x_first,
    x_second,
    y_first,
    y_second,
    z_first,
    z_second,
    metric_table,
    metric_index,
):
    rows = lax.axis_size("row")
    cols = lax.axis_size("col")
    comps, slots, zloc, length = velocity.shape
    depth = slots * zloc
    field = velocity.reshape(comps * depth, length)
    group = min(depth, 32)
    wide = cols // quad

    def along(value, step):
        return lax.ppermute(value, "col", [(i, i ^ step) for i in range(cols)])

    def across(value, step):
        return lax.ppermute(value, "row", [(i, i ^ step) for i in range(rows)])

    gathered = [along(field, t) for t in range(1, quad)]
    cells = metric_index.shape[0]
    z_matrix, mask, held, ends, others = call(
        functools.partial(span_matrix_kernel, rows, cols, zloc),
        [wall_counts, z_first, z_second, field],
        [SMEM] * 3 + [VMEM],
        [
            (wide * group, 2 * quad * group),
            (depth, length),
            field.shape,
            (2 * depth, cells),
            (rows // 2 * depth, cells),
        ],
        "span_matrix",
    )
    far = [across(held, step) for step in range(2, rows, 2)]
    (early,) = call(
        functools.partial(early_kernel, comps, (0, quad - 1)),
        [z_matrix, field, gathered[-1]],
        [VMEM] * 3,
        [(wide * group, comps * (depth // group) * length)],
        "early",
    )
    parts = call(
        functools.partial(span_kernel, comps, tuple(range(1, quad - 1))),
        [z_matrix, early] + gathered[:-1],
        [VMEM] * quad,
        [field.shape] * wide,
        "span",
    )
    returned = [along(parts[t], over(t)) for t in range(1, wide)]
    (y_matrix,) = call(
        functools.partial(wall_matrix_kernel, zloc),
        [ends, others, metric_table.reshape(1, -1), metric_index.reshape(1, -1), y_first, y_second, parts[0]],
        [VMEM] * 6 + [pl.ANY],
        [(2 * depth, rows * depth)],
        "wall_matrix",
    )
    total, away = call(
        functools.partial(wall_kernel, comps),
        [y_matrix, parts[0], field] + far,
        [VMEM] * (3 + len(far)),
        [field.shape] * 2,
        "wall",
    )
    near = across(away, 1)
    (x_part,) = call(
        functools.partial(stream_kernel, comps),
        [field, x_first.reshape(1, length), x_second.reshape(1, length), away],
        [VMEM] * 3 + [pl.ANY],
        [field.shape],
        "stream",
    )
    (summed,) = call(
        functools.partial(sum_kernel, comps),
        [mask, total, x_part] + returned,
        [VMEM] * (3 + len(returned)),
        [field.shape],
        "sum",
        cost=pl.CostEstimate(flops=1 << 30, bytes_accessed=1 << 22, transcendentals=0),
    )
    (result,) = call(finish_kernel, [summed, near], [VMEM] * 2, [field.shape], "finish")
    return result.reshape(velocity.shape)


def solution(mesh):
    in_specs = (P(None, "row", "col", None), P(), P(), P(), P(), P(), P(), P(), P(), P())
    out_specs = P(None, "row", "col", None)
    return jax.shard_map(local, mesh=mesh, in_specs=in_specs, out_specs=out_specs, check_vma=False)
```

```python
import functools
import math

import jax
import jax.numpy as jnp
from jax import lax
from jax.experimental import pallas as pl
from jax.experimental.pallas import tpu as pltpu
from jax.sharding import PartitionSpec as P

viscosity = 0.4
quad = 4

VMEM = pltpu.VMEM
SMEM = pltpu.SMEM


def halves(value):
    high = value.astype(jnp.bfloat16)
    low = (value - high.astype(jnp.float32)).astype(jnp.bfloat16)
    return high, low


def dot_split(left, right, transposed=False):
    dims = (((1,), (1 if transposed else 0,)), ((), ()))
    mul = functools.partial(lax.dot_general, dimension_numbers=dims, preferred_element_type=jnp.float32)
    lh, ll = halves(left)
    rh, rl = halves(right)
    both = mul(jnp.concatenate([lh, ll], axis=0), rh)
    count = left.shape[0]
    return both[:count] + (mul(lh, rl) + both[count:])


def over(t):
    return quad * t + 2 * (t != 0)


def quad_sums(comps, matrix, fields, chosen):
    depth, length = fields[0].shape[0] // comps, fields[0].shape[1]
    half = matrix.shape[1] // 2
    group = half // quad
    left = jnp.concatenate(
        [matrix[:, start + s * group : start + (s + 1) * group] for start in (0, half) for s in chosen], axis=1
    )
    right = []
    for comp in range(comps):
        for at in range(0, depth, group):
            stack = [field[comp * depth + at : comp * depth + at + group] for field in fields]
            stack += [value * field[2 * depth + at : 2 * depth + at + group] for value, field in zip(stack, fields)]
            right.append(jnp.concatenate(stack, axis=0))
    return dot_split(left, jnp.concatenate(right, axis=1))


def early_kernel(comps, chosen, matrix, *refs):
    refs[-1][...] = quad_sums(comps, matrix, refs[:-1], chosen)


def span_kernel(comps, chosen, matrix, early, *refs):
    fields, parts = refs[: len(chosen)], refs[len(chosen) :]
    result = early[...] + quad_sums(comps, matrix, fields, chosen)
    rows, length = parts[0].shape
    count = len(parts)
    group = result.shape[0] // count
    for t in range(count):
        for i in range(rows // group):
            parts[t][i * group : (i + 1) * group] = result[
                t * group : (t + 1) * group, i * length : (i + 1) * length
            ]


def circulant_rows(row, length):
    return pltpu.roll(jnp.broadcast_to(row, (length, length)), 0, 1, stride=1, stride_axis=0)


def span_matrix_kernel(
    rows, cols, zloc, wall_counts, z_first, z_second, field, z_matrix, mask, held, ends, others
):
    held[...] = field[...]
    me = lax.axis_index("row")
    mask[...] = (lax.broadcasted_iota(jnp.int32, mask.shape, 0) // zloc < wall_counts[me]).astype(jnp.float32)
    depth = mask.shape[0]
    plane = lax.broadcasted_iota(jnp.int32, (depth, ends.shape[1]), 0) // zloc
    cell = lax.broadcasted_iota(jnp.int32, (depth, ends.shape[1]), 1)

    def spots(index):
        start = lax.fori_loop(0, rows, lambda i, acc: acc + jnp.where(i < index, wall_counts[i], 0), 0, unroll=True)
        return ((plane < wall_counts[index]) & (plane + start == cell)).astype(jnp.float32)

    for i in range(2):
        ends[i * depth : (i + 1) * depth] = spots(me ^ i)
    for i in range(rows // 2):
        others[i * depth : (i + 1) * depth] = spots(me ^ (2 * i))

    cells_z = cols * zloc
    shape = z_matrix.shape
    half = shape[1] // 2
    group = half // quad
    mine = lax.axis_index("col")
    r = lax.broadcasted_iota(jnp.int32, shape, 0)
    q = lax.broadcasted_iota(jnp.int32, shape, 1)
    q = jnp.where(q < half, q, q - half)
    out_cell = (over(r // group) ^ mine) * zloc + r % zloc
    in_cell = ((q // group) ^ mine) * zloc + q % zloc
    same = (r % group) // zloc == (q % group) // zloc
    gap = jnp.where(same, (in_cell - out_cell + cells_z) % cells_z, -1)
    kind = lax.broadcasted_iota(jnp.int32, (1, shape[1]), 1) < half

    def fill(k, total):
        value = jnp.where(kind, viscosity * z_second[k], -z_first[k])
        return jnp.where(gap == k, value, total)

    z_matrix[...] = lax.fori_loop(0, cells_z, fill, jnp.zeros(shape, jnp.float32), unroll=8)


def stream_kernel(comps, field, x_first, x_second, after, x_part):
    length = field.shape[1]
    depth = field.shape[0] // comps
    u = field[...]
    lead = u[:depth]
    left = jnp.concatenate(
        [u, jnp.concatenate([lead * u[c * depth : (c + 1) * depth] for c in range(comps)], axis=0)], axis=1
    )
    right = jnp.concatenate(
        [viscosity * circulant_rows(x_second[...], length), -circulant_rows(x_first[...], length)], axis=1
    )
    x_part[...] = dot_split(left, right, transposed=True)


def wall_matrix_kernel(zloc, ends, others, metric_table, metric_index, y_first, y_second, after, matrix):
    cells = y_first.shape[0]
    depth = matrix.shape[0] // 2
    plain = functools.partial(
        lax.dot_general, dimension_numbers=(((1,), (0,)), ((), ())), preferred_element_type=jnp.float32
    )
    turned = functools.partial(
        lax.dot_general, dimension_numbers=(((1,), (1,)), ((), ())), preferred_element_type=jnp.float32
    )
    levels = metric_table.shape[1]
    entry = (lax.broadcasted_iota(jnp.int32, (levels, cells), 0) == metric_index[...]).astype(jnp.float32)
    table = jnp.broadcast_to(metric_table[...], (8, levels))
    metric = plain(table, entry, precision=lax.Precision.HIGHEST)[:1]
    scale = jnp.sum(ends[...] * metric, axis=1, keepdims=True)
    pick = ends[...].astype(jnp.bfloat16)
    second = sum(plain(pick, part) for part in halves(viscosity * y_second[...]))
    first = -scale * sum(plain(pick, part) for part in halves(y_first[...]))
    other = others[...].astype(jnp.bfloat16)
    wide = sum(turned(part, other) for part in halves(jnp.concatenate([second, first], axis=0)))
    match = lax.broadcasted_iota(jnp.int32, wide.shape, 0) % zloc == lax.broadcasted_iota(jnp.int32, wide.shape, 1) % zloc
    wide = jnp.where(match, wide, 0.0)
    for b in range(others.shape[0] // depth):
        for k in range(2):
            matrix[:, (2 * b + k) * depth : (2 * b + k + 1) * depth] = wide[
                2 * k * depth : 2 * (k + 1) * depth, b * depth : (b + 1) * depth
            ]


def wall_kernel(comps, matrix, z_part, *refs):
    fields, (total, away) = refs[:-2], refs[-2:]
    depth = z_part.shape[0] // comps
    for comp in range(comps):
        at = slice(comp * depth, (comp + 1) * depth)
        stack = []
        for field in fields:
            stack += [field[at], field[depth : 2 * depth] * field[at]]
        result = dot_split(matrix[...], jnp.concatenate(stack, axis=0))
        total[at] = z_part[at] + result[:depth]
        away[at] = result[depth:]


def sum_kernel(comps, mask, *refs):
    parts, out = refs[:-1], refs[-1]
    depth = mask.shape[0]
    for comp in range(comps):
        at = slice(comp * depth, (comp + 1) * depth)
        out[at] = jnp.where(mask[...] > 0, sum(part[at] for part in parts[1:]) + parts[0][at], 0.0)


def finish_kernel(total, near, out):
    out[...] = total[...] + near[...]


def call(kernel, operands, spaces, results, name, scratch=(), cost=None):
    results = [jax.ShapeDtypeStruct(shape, jnp.float32) for shape in results]
    held = sum(4 * math.prod(array.shape) for array in list(operands) + results)
    return pl.pallas_call(
        kernel,
        out_shape=results,
        in_specs=[pl.BlockSpec(memory_space=space) for space in spaces],
        out_specs=[pl.BlockSpec(memory_space=VMEM)] * len(results),
        scratch_shapes=[pltpu.VMEM(shape, jnp.float32) for shape in scratch],
        compiler_params=pltpu.CompilerParams(vmem_limit_bytes=(4 << 20) + 3 * held),
        cost_estimate=cost,
        name=name,
    )(*operands)


def local(
    velocity,
    wall_counts,
    x_first,
    x_second,
    y_first,
    y_second,
    z_first,
    z_second,
    metric_table,
    metric_index,
):
    rows = lax.axis_size("row")
    cols = lax.axis_size("col")
    comps, slots, zloc, length = velocity.shape
    depth = slots * zloc
    field = velocity.reshape(comps * depth, length)
    group = min(depth, 32)
    wide = cols // quad

    def along(value, step):
        return lax.ppermute(value, "col", [(i, i ^ step) for i in range(cols)])

    def across(value, step):
        return lax.ppermute(value, "row", [(i, i ^ step) for i in range(rows)])

    gathered = [along(field, t) for t in range(1, quad)]
    cells = metric_index.shape[0]
    z_matrix, mask, held, ends, others = call(
        functools.partial(span_matrix_kernel, rows, cols, zloc),
        [wall_counts, z_first, z_second, field],
        [SMEM] * 3 + [VMEM],
        [
            (wide * group, 2 * quad * group),
            (depth, length),
            field.shape,
            (2 * depth, cells),
            (rows // 2 * depth, cells),
        ],
        "span_matrix",
    )
    far = [across(held, step) for step in range(2, rows, 2)]
    first, last = 2, (1, 3)
    (early,) = call(
        functools.partial(early_kernel, comps, (0, first)),
        [z_matrix, field, gathered[first - 1]],
        [VMEM] * 3,
        [(wide * group, comps * (depth // group) * length)],
        "early",
    )
    parts = call(
        functools.partial(span_kernel, comps, last),
        [z_matrix, early] + [gathered[s - 1] for s in last],
        [VMEM] * (2 + len(last)),
        [field.shape] * wide,
        "span",
    )
    returned = [along(parts[t], over(t)) for t in range(1, wide)]
    (y_matrix,) = call(
        functools.partial(wall_matrix_kernel, zloc),
        [ends, others, metric_table.reshape(1, -1), metric_index.reshape(1, -1), y_first, y_second, parts[0]],
        [VMEM] * 6 + [pl.ANY],
        [(2 * depth, rows * depth)],
        "wall_matrix",
    )
    total, away = call(
        functools.partial(wall_kernel, comps),
        [y_matrix, parts[0], field] + far,
        [VMEM] * (3 + len(far)),
        [field.shape] * 2,
        "wall",
    )
    near = across(away, 1)
    (x_part,) = call(
        functools.partial(stream_kernel, comps),
        [field, x_first.reshape(1, length), x_second.reshape(1, length), away],
        [VMEM] * 3 + [pl.ANY],
        [field.shape],
        "stream",
    )
    (summed,) = call(
        functools.partial(sum_kernel, comps),
        [mask, total, x_part] + returned,
        [VMEM] * (3 + len(returned)),
        [field.shape],
        "sum",
        cost=pl.CostEstimate(flops=1 << 30, bytes_accessed=1 << 22, transcendentals=0),
    )
    (result,) = call(finish_kernel, [summed, near], [VMEM] * 2, [field.shape], "finish")
    return result.reshape(velocity.shape)


def solution(mesh):
    in_specs = (P(None, "row", "col", None), P(), P(), P(), P(), P(), P(), P(), P(), P())
    out_specs = P(None, "row", "col", None)
    return jax.shard_map(local, mesh=mesh, in_specs=in_specs, out_specs=out_specs, check_vma=False)
```

```python
import functools
import math

import jax
import jax.numpy as jnp
from jax import lax
from jax.experimental import pallas as pl
from jax.experimental.pallas import tpu as pltpu
from jax.sharding import PartitionSpec as P

viscosity = 0.4
quad = 4

VMEM = pltpu.VMEM
SMEM = pltpu.SMEM


def halves(value):
    high = value.astype(jnp.bfloat16)
    low = (value - high.astype(jnp.float32)).astype(jnp.bfloat16)
    return high, low


def dot_split(left, right, transposed=False):
    dims = (((1,), (1 if transposed else 0,)), ((), ()))
    mul = functools.partial(lax.dot_general, dimension_numbers=dims, preferred_element_type=jnp.float32)
    lh, ll = halves(left)
    rh, rl = halves(right)
    both = mul(jnp.concatenate([lh, ll], axis=0), rh)
    count = left.shape[0]
    return both[:count] + (mul(lh, rl) + both[count:])


def over(t):
    return quad * t + 2 * (t != 0)


def span_kernel(comps, sources, matrix, *refs):
    fields, parts = refs[:sources], refs[sources:]
    depth, length = fields[0].shape[0] // comps, fields[0].shape[1]
    group = matrix.shape[0] // quad
    right = []
    for comp in range(comps):
        for at in range(0, depth, group):
            stack = [field[comp * depth + at : comp * depth + at + group] for field in fields]
            stack += [value * field[2 * depth + at : 2 * depth + at + group] for value, field in zip(stack, fields)]
            right.append(jnp.concatenate(stack, axis=0))
    result = dot_split(matrix[...], jnp.concatenate(right, axis=1))
    for t in range(quad):
        for i in range(len(right)):
            parts[t][i * group : (i + 1) * group] = result[
                t * group : (t + 1) * group, i * length : (i + 1) * length
            ]


def circulant_rows(row, length):
    return pltpu.roll(jnp.broadcast_to(row, (length, length)), 0, 1, stride=1, stride_axis=0)


def span_matrix_kernel(
    rows, cols, zloc, wall_counts, z_first, z_second, field, z_matrix, mask, held, ends, others
):
    held[...] = field[...]
    me = lax.axis_index("row")
    mask[...] = (lax.broadcasted_iota(jnp.int32, mask.shape, 0) // zloc < wall_counts[me]).astype(jnp.float32)
    depth = mask.shape[0]
    plane = lax.broadcasted_iota(jnp.int32, (depth, ends.shape[1]), 0) // zloc
    cell = lax.broadcasted_iota(jnp.int32, (depth, ends.shape[1]), 1)

    def spots(index):
        start = lax.fori_loop(0, rows, lambda i, acc: acc + jnp.where(i < index, wall_counts[i], 0), 0, unroll=True)
        return ((plane < wall_counts[index]) & (plane + start == cell)).astype(jnp.float32)

    for i in range(2):
        ends[i * depth : (i + 1) * depth] = spots(me ^ i)
    for i in range(rows // 2):
        others[i * depth : (i + 1) * depth] = spots(me ^ (2 * i))

    cells_z = cols * zloc
    shape = z_matrix.shape
    half = shape[1] // 2
    group = shape[0] // quad
    mine = lax.axis_index("col")
    r = lax.broadcasted_iota(jnp.int32, shape, 0)
    q = lax.broadcasted_iota(jnp.int32, shape, 1)
    q = jnp.where(q < half, q, q - half)
    out_cell = ((r // group) ^ mine) * zloc + r % zloc
    in_cell = (over(q // group) ^ mine) * zloc + q % zloc
    same = (r % group) // zloc == (q % group) // zloc
    gap = jnp.where(same, (in_cell - out_cell + cells_z) % cells_z, -1)
    kind = lax.broadcasted_iota(jnp.int32, (1, shape[1]), 1) < half

    def fill(k, total):
        value = jnp.where(kind, viscosity * z_second[k], -z_first[k])
        return jnp.where(gap == k, value, total)

    z_matrix[...] = lax.fori_loop(0, cells_z, fill, jnp.zeros(shape, jnp.float32), unroll=8)


def stream_kernel(comps, field, x_first, x_second, after, x_part):
    length = field.shape[1]
    depth = field.shape[0] // comps
    u = field[...]
    lead = u[:depth]
    left = jnp.concatenate(
        [u, jnp.concatenate([lead * u[c * depth : (c + 1) * depth] for c in range(comps)], axis=0)], axis=1
    )
    right = jnp.concatenate(
        [viscosity * circulant_rows(x_second[...], length), -circulant_rows(x_first[...], length)], axis=1
    )
    x_part[...] = dot_split(left, right, transposed=True)


def wall_matrix_kernel(zloc, ends, others, metric_table, metric_index, y_first, y_second, after, matrix):
    cells = y_first.shape[0]
    depth = matrix.shape[0] // 2
    plain = functools.partial(
        lax.dot_general, dimension_numbers=(((1,), (0,)), ((), ())), preferred_element_type=jnp.float32
    )
    turned = functools.partial(
        lax.dot_general, dimension_numbers=(((1,), (1,)), ((), ())), preferred_element_type=jnp.float32
    )
    levels = metric_table.shape[1]
    entry = (lax.broadcasted_iota(jnp.int32, (levels, cells), 0) == metric_index[...]).astype(jnp.float32)
    table = jnp.broadcast_to(metric_table[...], (8, levels))
    metric = plain(table, entry, precision=lax.Precision.HIGHEST)[:1]
    scale = jnp.sum(ends[...] * metric, axis=1, keepdims=True)
    pick = ends[...].astype(jnp.bfloat16)
    second = sum(plain(pick, part) for part in halves(viscosity * y_second[...]))
    first = -scale * sum(plain(pick, part) for part in halves(y_first[...]))
    other = others[...].astype(jnp.bfloat16)
    wide = sum(turned(part, other) for part in halves(jnp.concatenate([second, first], axis=0)))
    match = lax.broadcasted_iota(jnp.int32, wide.shape, 0) % zloc == lax.broadcasted_iota(jnp.int32, wide.shape, 1) % zloc
    wide = jnp.where(match, wide, 0.0)
    for b in range(others.shape[0] // depth):
        for k in range(2):
            matrix[:, (2 * b + k) * depth : (2 * b + k + 1) * depth] = wide[
                2 * k * depth : 2 * (k + 1) * depth, b * depth : (b + 1) * depth
            ]


def wall_kernel(comps, matrix, z_part, *refs):
    fields, (total, away) = refs[:-2], refs[-2:]
    depth = z_part.shape[0] // comps
    for comp in range(comps):
        at = slice(comp * depth, (comp + 1) * depth)
        stack = []
        for field in fields:
            stack += [field[at], field[depth : 2 * depth] * field[at]]
        result = dot_split(matrix[...], jnp.concatenate(stack, axis=0))
        total[at] = z_part[at] + result[:depth]
        away[at] = result[depth:]


def sum_kernel(comps, mask, *refs):
    parts, out = refs[:-1], refs[-1]
    depth = mask.shape[0]
    for comp in range(comps):
        at = slice(comp * depth, (comp + 1) * depth)
        out[at] = jnp.where(mask[...] > 0, sum(part[at] for part in parts[1:]) + parts[0][at], 0.0)


def finish_kernel(total, near, out):
    out[...] = total[...] + near[...]


def call(kernel, operands, spaces, results, name, scratch=(), cost=None):
    results = [jax.ShapeDtypeStruct(shape, jnp.float32) for shape in results]
    held = sum(4 * math.prod(array.shape) for array in list(operands) + results)
    return pl.pallas_call(
        kernel,
        out_shape=results,
        in_specs=[pl.BlockSpec(memory_space=space) for space in spaces],
        out_specs=[pl.BlockSpec(memory_space=VMEM)] * len(results),
        scratch_shapes=[pltpu.VMEM(shape, jnp.float32) for shape in scratch],
        compiler_params=pltpu.CompilerParams(vmem_limit_bytes=(4 << 20) + 3 * held),
        cost_estimate=cost,
        name=name,
    )(*operands)


def local(
    velocity,
    wall_counts,
    x_first,
    x_second,
    y_first,
    y_second,
    z_first,
    z_second,
    metric_table,
    metric_index,
):
    rows = lax.axis_size("row")
    cols = lax.axis_size("col")
    comps, slots, zloc, length = velocity.shape
    depth = slots * zloc
    field = velocity.reshape(comps * depth, length)
    group = min(depth, 32)
    wide = cols // quad

    def along(value, step):
        return lax.ppermute(value, "col", [(i, i ^ step) for i in range(cols)])

    def across(value, step):
        return lax.ppermute(value, "row", [(i, i ^ step) for i in range(rows)])

    gathered = [along(field, over(t)) for t in range(1, wide)]
    cells = metric_index.shape[0]
    z_matrix, mask, held, ends, others = call(
        functools.partial(span_matrix_kernel, rows, cols, zloc),
        [wall_counts, z_first, z_second, field],
        [SMEM] * 3 + [VMEM],
        [
            (quad * group, 2 * wide * group),
            (depth, length),
            field.shape,
            (2 * depth, cells),
            (rows // 2 * depth, cells),
        ],
        "span_matrix",
    )
    far = [across(held, step) for step in range(2, rows, 2)]
    parts = call(
        functools.partial(span_kernel, comps, wide),
        [z_matrix, field] + gathered,
        [VMEM] * (1 + wide),
        [field.shape] * quad,
        "span",
    )
    returned = [along(parts[t], t) for t in reversed(range(1, quad))]
    (y_matrix,) = call(
        functools.partial(wall_matrix_kernel, zloc),
        [ends, others, metric_table.reshape(1, -1), metric_index.reshape(1, -1), y_first, y_second, parts[0]],
        [VMEM] * 6 + [pl.ANY],
        [(2 * depth, rows * depth)],
        "wall_matrix",
    )
    total, away = call(
        functools.partial(wall_kernel, comps),
        [y_matrix, parts[0], field] + far,
        [VMEM] * (3 + len(far)),
        [field.shape] * 2,
        "wall",
    )
    near = across(away, 1)
    (x_part,) = call(
        functools.partial(stream_kernel, comps),
        [field, x_first.reshape(1, length), x_second.reshape(1, length), away],
        [VMEM] * 3 + [pl.ANY],
        [field.shape],
        "stream",
    )
    (summed,) = call(
        functools.partial(sum_kernel, comps),
        [mask, total, x_part] + returned,
        [VMEM] * (3 + len(returned)),
        [field.shape],
        "sum",
        cost=pl.CostEstimate(flops=1 << 30, bytes_accessed=1 << 22, transcendentals=0),
    )
    (result,) = call(finish_kernel, [summed, near], [VMEM] * 2, [field.shape], "finish")
    return result.reshape(velocity.shape)


def solution(mesh):
    in_specs = (P(None, "row", "col", None), P(), P(), P(), P(), P(), P(), P(), P(), P())
    out_specs = P(None, "row", "col", None)
    return jax.shard_map(local, mesh=mesh, in_specs=in_specs, out_specs=out_specs, check_vma=False)
```

```python
import functools
import math

import jax
import jax.numpy as jnp
from jax import lax
from jax.experimental import pallas as pl
from jax.experimental.pallas import tpu as pltpu
from jax.sharding import PartitionSpec as P

viscosity = 0.4
quad = 4

VMEM = pltpu.VMEM
SMEM = pltpu.SMEM


def halves(value):
    high = value.astype(jnp.bfloat16)
    low = (value - high.astype(jnp.float32)).astype(jnp.bfloat16)
    return high, low


def dot_split(left, right, transposed=False):
    dims = (((1,), (1 if transposed else 0,)), ((), ()))
    mul = functools.partial(lax.dot_general, dimension_numbers=dims, preferred_element_type=jnp.float32)
    lh, ll = halves(left)
    rh, rl = halves(right)
    both = mul(jnp.concatenate([lh, ll], axis=0), rh)
    count = left.shape[0]
    return both[:count] + (mul(lh, rl) + both[count:])


def over(t):
    return quad * t + 3 * (t != 0)


def span_kernel(comps, sources, matrix, *refs):
    fields, parts = refs[:sources], refs[sources:]
    depth, length = fields[0].shape[0] // comps, fields[0].shape[1]
    group = matrix.shape[0] // quad
    right = []
    for comp in range(comps):
        for at in range(0, depth, group):
            stack = [field[comp * depth + at : comp * depth + at + group] for field in fields]
            stack += [value * field[2 * depth + at : 2 * depth + at + group] for value, field in zip(stack, fields)]
            right.append(jnp.concatenate(stack, axis=0))
    result = dot_split(matrix[...], jnp.concatenate(right, axis=1))
    for t in range(quad):
        for i in range(len(right)):
            parts[t][i * group : (i + 1) * group] = result[
                t * group : (t + 1) * group, i * length : (i + 1) * length
            ]


def circulant_rows(row, length):
    return pltpu.roll(jnp.broadcast_to(row, (length, length)), 0, 1, stride=1, stride_axis=0)


def span_matrix_kernel(
    rows, cols, zloc, wall_counts, z_first, z_second, field, z_matrix, mask, held, ends, others
):
    held[...] = field[...]
    me = lax.axis_index("row")
    mask[...] = (lax.broadcasted_iota(jnp.int32, mask.shape, 0) // zloc < wall_counts[me]).astype(jnp.float32)
    depth = mask.shape[0]
    plane = lax.broadcasted_iota(jnp.int32, (depth, ends.shape[1]), 0) // zloc
    cell = lax.broadcasted_iota(jnp.int32, (depth, ends.shape[1]), 1)

    def spots(index):
        start = lax.fori_loop(0, rows, lambda i, acc: acc + jnp.where(i < index, wall_counts[i], 0), 0, unroll=True)
        return ((plane < wall_counts[index]) & (plane + start == cell)).astype(jnp.float32)

    for i in range(2):
        ends[i * depth : (i + 1) * depth] = spots(me ^ i)
    for i in range(rows // 2):
        others[i * depth : (i + 1) * depth] = spots(me ^ (2 * i))

    cells_z = cols * zloc
    shape = z_matrix.shape
    half = shape[1] // 2
    group = shape[0] // quad
    mine = lax.axis_index("col")
    r = lax.broadcasted_iota(jnp.int32, shape, 0)
    q = lax.broadcasted_iota(jnp.int32, shape, 1)
    q = jnp.where(q < half, q, q - half)
    out_cell = ((r // group) ^ mine) * zloc + r % zloc
    in_cell = (over(q // group) ^ mine) * zloc + q % zloc
    same = (r % group) // zloc == (q % group) // zloc
    gap = jnp.where(same, (in_cell - out_cell + cells_z) % cells_z, -1)
    kind = lax.broadcasted_iota(jnp.int32, (1, shape[1]), 1) < half

    def fill(k, total):
        value = jnp.where(kind, viscosity * z_second[k], -z_first[k])
        return jnp.where(gap == k, value, total)

    z_matrix[...] = lax.fori_loop(0, cells_z, fill, jnp.zeros(shape, jnp.float32), unroll=8)


def stream_kernel(comps, field, x_first, x_second, after, x_part):
    length = field.shape[1]
    depth = field.shape[0] // comps
    u = field[...]
    lead = u[:depth]
    left = jnp.concatenate(
        [u, jnp.concatenate([lead * u[c * depth : (c + 1) * depth] for c in range(comps)], axis=0)], axis=1
    )
    right = jnp.concatenate(
        [viscosity * circulant_rows(x_second[...], length), -circulant_rows(x_first[...], length)], axis=1
    )
    x_part[...] = dot_split(left, right, transposed=True)


def wall_matrix_kernel(zloc, ends, others, metric_table, metric_index, y_first, y_second, after, matrix):
    cells = y_first.shape[0]
    depth = matrix.shape[0] // 2
    plain = functools.partial(
        lax.dot_general, dimension_numbers=(((1,), (0,)), ((), ())), preferred_element_type=jnp.float32
    )
    turned = functools.partial(
        lax.dot_general, dimension_numbers=(((1,), (1,)), ((), ())), preferred_element_type=jnp.float32
    )
    levels = metric_table.shape[1]
    entry = (lax.broadcasted_iota(jnp.int32, (levels, cells), 0) == metric_index[...]).astype(jnp.float32)
    table = jnp.broadcast_to(metric_table[...], (8, levels))
    metric = plain(table, entry, precision=lax.Precision.HIGHEST)[:1]
    scale = jnp.sum(ends[...] * metric, axis=1, keepdims=True)
    pick = ends[...].astype(jnp.bfloat16)
    second = sum(plain(pick, part) for part in halves(viscosity * y_second[...]))
    first = -scale * sum(plain(pick, part) for part in halves(y_first[...]))
    other = others[...].astype(jnp.bfloat16)
    wide = sum(turned(part, other) for part in halves(jnp.concatenate([second, first], axis=0)))
    match = lax.broadcasted_iota(jnp.int32, wide.shape, 0) % zloc == lax.broadcasted_iota(jnp.int32, wide.shape, 1) % zloc
    wide = jnp.where(match, wide, 0.0)
    for b in range(others.shape[0] // depth):
        for k in range(2):
            matrix[:, (2 * b + k) * depth : (2 * b + k + 1) * depth] = wide[
                2 * k * depth : 2 * (k + 1) * depth, b * depth : (b + 1) * depth
            ]


def wall_kernel(comps, matrix, z_part, *refs):
    fields, (total, away) = refs[:-2], refs[-2:]
    depth = z_part.shape[0] // comps
    for comp in range(comps):
        at = slice(comp * depth, (comp + 1) * depth)
        stack = []
        for field in fields:
            stack += [field[at], field[depth : 2 * depth] * field[at]]
        result = dot_split(matrix[...], jnp.concatenate(stack, axis=0))
        total[at] = z_part[at] + result[:depth]
        away[at] = result[depth:]


def sum_kernel(comps, mask, *refs):
    parts, out = refs[:-1], refs[-1]
    depth = mask.shape[0]
    for comp in range(comps):
        at = slice(comp * depth, (comp + 1) * depth)
        out[at] = jnp.where(mask[...] > 0, sum(part[at] for part in parts[1:]) + parts[0][at], 0.0)


def finish_kernel(total, near, out):
    out[...] = total[...] + near[...]


def call(kernel, operands, spaces, results, name, scratch=(), cost=None):
    results = [jax.ShapeDtypeStruct(shape, jnp.float32) for shape in results]
    held = sum(4 * math.prod(array.shape) for array in list(operands) + results)
    return pl.pallas_call(
        kernel,
        out_shape=results,
        in_specs=[pl.BlockSpec(memory_space=space) for space in spaces],
        out_specs=[pl.BlockSpec(memory_space=VMEM)] * len(results),
        scratch_shapes=[pltpu.VMEM(shape, jnp.float32) for shape in scratch],
        compiler_params=pltpu.CompilerParams(vmem_limit_bytes=(4 << 20) + 3 * held),
        cost_estimate=cost,
        name=name,
    )(*operands)


def local(
    velocity,
    wall_counts,
    x_first,
    x_second,
    y_first,
    y_second,
    z_first,
    z_second,
    metric_table,
    metric_index,
):
    rows = lax.axis_size("row")
    cols = lax.axis_size("col")
    comps, slots, zloc, length = velocity.shape
    depth = slots * zloc
    field = velocity.reshape(comps * depth, length)
    group = min(depth, 32)
    wide = cols // quad

    def along(value, step):
        return lax.ppermute(value, "col", [(i, i ^ step) for i in range(cols)])

    def across(value, step):
        return lax.ppermute(value, "row", [(i, i ^ step) for i in range(rows)])

    gathered = [along(field, over(t)) for t in range(1, wide)]
    cells = metric_index.shape[0]
    z_matrix, mask, held, ends, others = call(
        functools.partial(span_matrix_kernel, rows, cols, zloc),
        [wall_counts, z_first, z_second, field],
        [SMEM] * 3 + [VMEM],
        [
            (quad * group, 2 * wide * group),
            (depth, length),
            field.shape,
            (2 * depth, cells),
            (rows // 2 * depth, cells),
        ],
        "span_matrix",
    )
    far = [across(held, step) for step in range(2, rows, 2)]
    parts = call(
        functools.partial(span_kernel, comps, wide),
        [z_matrix, field] + gathered,
        [VMEM] * (1 + wide),
        [field.shape] * quad,
        "span",
    )
    returned = [along(parts[t], t) for t in reversed(range(1, quad))]
    (y_matrix,) = call(
        functools.partial(wall_matrix_kernel, zloc),
        [ends, others, metric_table.reshape(1, -1), metric_index.reshape(1, -1), y_first, y_second, parts[0]],
        [VMEM] * 6 + [pl.ANY],
        [(2 * depth, rows * depth)],
        "wall_matrix",
    )
    total, away = call(
        functools.partial(wall_kernel, comps),
        [y_matrix, parts[0], field] + far,
        [VMEM] * (3 + len(far)),
        [field.shape] * 2,
        "wall",
    )
    near = across(away, 1)
    (x_part,) = call(
        functools.partial(stream_kernel, comps),
        [field, x_first.reshape(1, length), x_second.reshape(1, length), away],
        [VMEM] * 3 + [pl.ANY],
        [field.shape],
        "stream",
    )
    (summed,) = call(
        functools.partial(sum_kernel, comps),
        [mask, total, x_part] + returned,
        [VMEM] * (3 + len(returned)),
        [field.shape],
        "sum",
        cost=pl.CostEstimate(flops=1 << 30, bytes_accessed=1 << 22, transcendentals=0),
    )
    (result,) = call(finish_kernel, [summed, near], [VMEM] * 2, [field.shape], "finish")
    return result.reshape(velocity.shape)


def solution(mesh):
    in_specs = (P(None, "row", "col", None), P(), P(), P(), P(), P(), P(), P(), P(), P())
    out_specs = P(None, "row", "col", None)
    return jax.shard_map(local, mesh=mesh, in_specs=in_specs, out_specs=out_specs, check_vma=False)
```

```python
import functools
import math

import jax
import jax.numpy as jnp
from jax import lax
from jax.experimental import pallas as pl
from jax.experimental.pallas import tpu as pltpu
from jax.sharding import PartitionSpec as P

viscosity = 0.4
quad = 4

VMEM = pltpu.VMEM
SMEM = pltpu.SMEM


def halves(value):
    high = value.astype(jnp.bfloat16)
    low = (value - high.astype(jnp.float32)).astype(jnp.bfloat16)
    return high, low


def dot_split(left, right, transposed=False):
    dims = (((1,), (1 if transposed else 0,)), ((), ()))
    mul = functools.partial(lax.dot_general, dimension_numbers=dims, preferred_element_type=jnp.float32)
    lh, ll = halves(left)
    rh, rl = halves(right)
    both = mul(jnp.concatenate([lh, ll], axis=0), rh)
    count = left.shape[0]
    return both[:count] + (mul(lh, rl) + both[count:])


def over(t):
    return quad * t + 2 * (t != 0)


def quad_sums(comps, matrix, fields, chosen):
    depth, length = fields[0].shape[0] // comps, fields[0].shape[1]
    half = matrix.shape[1] // 2
    group = half // quad
    left = jnp.concatenate(
        [matrix[:, start + s * group : start + (s + 1) * group] for start in (0, half) for s in chosen], axis=1
    )
    right = []
    for comp in range(comps):
        for at in range(0, depth, group):
            stack = [field[comp * depth + at : comp * depth + at + group] for field in fields]
            stack += [value * field[2 * depth + at : 2 * depth + at + group] for value, field in zip(stack, fields)]
            right.append(jnp.concatenate(stack, axis=0))
    return dot_split(left, jnp.concatenate(right, axis=1))


def early_kernel(comps, chosen, count, matrix, *refs):
    fields, before, out = refs[:count], refs[count:-1], refs[-1]
    value = quad_sums(comps, matrix, fields, chosen)
    out[...] = value + before[0][...] if before else value


def span_kernel(comps, chosen, matrix, early, *refs):
    fields, parts = refs[: len(chosen)], refs[len(chosen) :]
    result = early[...] + quad_sums(comps, matrix, fields, chosen)
    rows, length = parts[0].shape
    count = len(parts)
    group = result.shape[0] // count
    for t in range(count):
        for i in range(rows // group):
            parts[t][i * group : (i + 1) * group] = result[
                t * group : (t + 1) * group, i * length : (i + 1) * length
            ]


def circulant_rows(row, length):
    return pltpu.roll(jnp.broadcast_to(row, (length, length)), 0, 1, stride=1, stride_axis=0)


def span_matrix_kernel(
    rows, cols, zloc, wall_counts, z_first, z_second, field, z_matrix, mask, held, ends, others
):
    held[...] = field[...]
    me = lax.axis_index("row")
    mask[...] = (lax.broadcasted_iota(jnp.int32, mask.shape, 0) // zloc < wall_counts[me]).astype(jnp.float32)
    depth = mask.shape[0]
    plane = lax.broadcasted_iota(jnp.int32, (depth, ends.shape[1]), 0) // zloc
    cell = lax.broadcasted_iota(jnp.int32, (depth, ends.shape[1]), 1)

    def spots(index):
        start = lax.fori_loop(0, rows, lambda i, acc: acc + jnp.where(i < index, wall_counts[i], 0), 0, unroll=True)
        return ((plane < wall_counts[index]) & (plane + start == cell)).astype(jnp.float32)

    for i in range(2):
        ends[i * depth : (i + 1) * depth] = spots(me ^ i)
    for i in range(rows // 2):
        others[i * depth : (i + 1) * depth] = spots(me ^ (2 * i))

    cells_z = cols * zloc
    shape = z_matrix.shape
    half = shape[1] // 2
    group = half // quad
    mine = lax.axis_index("col")
    r = lax.broadcasted_iota(jnp.int32, shape, 0)
    q = lax.broadcasted_iota(jnp.int32, shape, 1)
    q = jnp.where(q < half, q, q - half)
    out_cell = (over(r // group) ^ mine) * zloc + r % zloc
    in_cell = ((q // group) ^ mine) * zloc + q % zloc
    same = (r % group) // zloc == (q % group) // zloc
    gap = jnp.where(same, (in_cell - out_cell + cells_z) % cells_z, -1)
    kind = lax.broadcasted_iota(jnp.int32, (1, shape[1]), 1) < half

    def fill(k, total):
        value = jnp.where(kind, viscosity * z_second[k], -z_first[k])
        return jnp.where(gap == k, value, total)

    z_matrix[...] = lax.fori_loop(0, cells_z, fill, jnp.zeros(shape, jnp.float32), unroll=8)


def stream_kernel(comps, field, x_first, x_second, after, x_part):
    length = field.shape[1]
    depth = field.shape[0] // comps
    u = field[...]
    lead = u[:depth]
    left = jnp.concatenate(
        [u, jnp.concatenate([lead * u[c * depth : (c + 1) * depth] for c in range(comps)], axis=0)], axis=1
    )
    right = jnp.concatenate(
        [viscosity * circulant_rows(x_second[...], length), -circulant_rows(x_first[...], length)], axis=1
    )
    x_part[...] = dot_split(left, right, transposed=True)


def wall_matrix_kernel(zloc, ends, others, metric_table, metric_index, y_first, y_second, after, matrix):
    cells = y_first.shape[0]
    depth = matrix.shape[0] // 2
    plain = functools.partial(
        lax.dot_general, dimension_numbers=(((1,), (0,)), ((), ())), preferred_element_type=jnp.float32
    )
    turned = functools.partial(
        lax.dot_general, dimension_numbers=(((1,), (1,)), ((), ())), preferred_element_type=jnp.float32
    )
    levels = metric_table.shape[1]
    entry = (lax.broadcasted_iota(jnp.int32, (levels, cells), 0) == metric_index[...]).astype(jnp.float32)
    table = jnp.broadcast_to(metric_table[...], (8, levels))
    metric = plain(table, entry, precision=lax.Precision.HIGHEST)[:1]
    scale = jnp.sum(ends[...] * metric, axis=1, keepdims=True)
    pick = ends[...].astype(jnp.bfloat16)
    second = sum(plain(pick, part) for part in halves(viscosity * y_second[...]))
    first = -scale * sum(plain(pick, part) for part in halves(y_first[...]))
    other = others[...].astype(jnp.bfloat16)
    wide = sum(turned(part, other) for part in halves(jnp.concatenate([second, first], axis=0)))
    match = lax.broadcasted_iota(jnp.int32, wide.shape, 0) % zloc == lax.broadcasted_iota(jnp.int32, wide.shape, 1) % zloc
    wide = jnp.where(match, wide, 0.0)
    for b in range(others.shape[0] // depth):
        for k in range(2):
            matrix[:, (2 * b + k) * depth : (2 * b + k + 1) * depth] = wide[
                2 * k * depth : 2 * (k + 1) * depth, b * depth : (b + 1) * depth
            ]


def wall_kernel(comps, matrix, z_part, *refs):
    fields, (total, away) = refs[:-2], refs[-2:]
    depth = z_part.shape[0] // comps
    for comp in range(comps):
        at = slice(comp * depth, (comp + 1) * depth)
        stack = []
        for field in fields:
            stack += [field[at], field[depth : 2 * depth] * field[at]]
        result = dot_split(matrix[...], jnp.concatenate(stack, axis=0))
        total[at] = z_part[at] + result[:depth]
        away[at] = result[depth:]


def sum_kernel(comps, mask, *refs):
    parts, out = refs[:-1], refs[-1]
    depth = mask.shape[0]
    for comp in range(comps):
        at = slice(comp * depth, (comp + 1) * depth)
        out[at] = jnp.where(mask[...] > 0, sum(part[at] for part in parts[1:]) + parts[0][at], 0.0)


def finish_kernel(total, near, out):
    out[...] = total[...] + near[...]


def call(kernel, operands, spaces, results, name, scratch=(), cost=None):
    results = [jax.ShapeDtypeStruct(shape, jnp.float32) for shape in results]
    held = sum(4 * math.prod(array.shape) for array in list(operands) + results)
    return pl.pallas_call(
        kernel,
        out_shape=results,
        in_specs=[pl.BlockSpec(memory_space=space) for space in spaces],
        out_specs=[pl.BlockSpec(memory_space=VMEM)] * len(results),
        scratch_shapes=[pltpu.VMEM(shape, jnp.float32) for shape in scratch],
        compiler_params=pltpu.CompilerParams(vmem_limit_bytes=(4 << 20) + 3 * held),
        cost_estimate=cost,
        name=name,
    )(*operands)


def local(
    velocity,
    wall_counts,
    x_first,
    x_second,
    y_first,
    y_second,
    z_first,
    z_second,
    metric_table,
    metric_index,
):
    rows = lax.axis_size("row")
    cols = lax.axis_size("col")
    comps, slots, zloc, length = velocity.shape
    depth = slots * zloc
    field = velocity.reshape(comps * depth, length)
    group = min(depth, 32)
    wide = cols // quad

    def along(value, step):
        return lax.ppermute(value, "col", [(i, i ^ step) for i in range(cols)])

    def across(value, step):
        return lax.ppermute(value, "row", [(i, i ^ step) for i in range(rows)])

    gathered = [along(field, t) for t in range(1, quad)]
    cells = metric_index.shape[0]
    z_matrix, mask, held, ends, others = call(
        functools.partial(span_matrix_kernel, rows, cols, zloc),
        [wall_counts, z_first, z_second, field],
        [SMEM] * 3 + [VMEM],
        [
            (wide * group, 2 * quad * group),
            (depth, length),
            field.shape,
            (2 * depth, cells),
            (rows // 2 * depth, cells),
        ],
        "span_matrix",
    )
    far = [across(held, step) for step in range(2, rows, 2)]
    early_shape = (wide * group, comps * (depth // group) * length)
    early = []
    for chosen in ((0, 3), (2,)):
        fields = [field if s == 0 else gathered[s - 1] for s in chosen]
        early = list(call(
            functools.partial(early_kernel, comps, chosen, len(chosen)),
            [z_matrix] + fields + early,
            [VMEM] * (1 + len(chosen) + len(early)),
            [early_shape],
            "early",
        ))
    parts = call(
        functools.partial(span_kernel, comps, (1,)),
        [z_matrix] + early + [gathered[0]],
        [VMEM] * 3,
        [field.shape] * wide,
        "span",
    )
    returned = [along(parts[t], over(t)) for t in range(1, wide)]
    (y_matrix,) = call(
        functools.partial(wall_matrix_kernel, zloc),
        [ends, others, metric_table.reshape(1, -1), metric_index.reshape(1, -1), y_first, y_second, parts[0]],
        [VMEM] * 6 + [pl.ANY],
        [(2 * depth, rows * depth)],
        "wall_matrix",
    )
    total, away = call(
        functools.partial(wall_kernel, comps),
        [y_matrix, parts[0], field] + far,
        [VMEM] * (3 + len(far)),
        [field.shape] * 2,
        "wall",
    )
    near = across(away, 1)
    (x_part,) = call(
        functools.partial(stream_kernel, comps),
        [field, x_first.reshape(1, length), x_second.reshape(1, length), away],
        [VMEM] * 3 + [pl.ANY],
        [field.shape],
        "stream",
    )
    (summed,) = call(
        functools.partial(sum_kernel, comps),
        [mask, total, x_part] + returned,
        [VMEM] * (3 + len(returned)),
        [field.shape],
        "sum",
        cost=pl.CostEstimate(flops=1 << 30, bytes_accessed=1 << 22, transcendentals=0),
    )
    (result,) = call(finish_kernel, [summed, near], [VMEM] * 2, [field.shape], "finish")
    return result.reshape(velocity.shape)


def solution(mesh):
    in_specs = (P(None, "row", "col", None), P(), P(), P(), P(), P(), P(), P(), P(), P())
    out_specs = P(None, "row", "col", None)
    return jax.shard_map(local, mesh=mesh, in_specs=in_specs, out_specs=out_specs, check_vma=False)
```

```python
import functools
import math

import jax
import jax.numpy as jnp
from jax import lax
from jax.experimental import pallas as pl
from jax.experimental.pallas import tpu as pltpu
from jax.sharding import PartitionSpec as P

viscosity = 0.4
quad = 4

VMEM = pltpu.VMEM
SMEM = pltpu.SMEM


def halves(value):
    high = value.astype(jnp.bfloat16)
    low = (value - high.astype(jnp.float32)).astype(jnp.bfloat16)
    return high, low


def dot_split(left, right, transposed=False):
    dims = (((1,), (1 if transposed else 0,)), ((), ()))
    mul = functools.partial(lax.dot_general, dimension_numbers=dims, preferred_element_type=jnp.float32)
    lh, ll = halves(left)
    rh, rl = halves(right)
    both = mul(jnp.concatenate([lh, ll], axis=0), rh)
    count = left.shape[0]
    return both[:count] + (mul(lh, rl) + both[count:])


def over(t):
    return quad * t + 2 * (t != 0)


def span_kernel(comps, sources, matrix, *refs):
    fields, parts = refs[:sources], refs[sources:]
    depth, length = fields[0].shape[0] // comps, fields[0].shape[1]
    group = matrix.shape[0] // quad
    right = []
    for comp in range(comps):
        for at in range(0, depth, group):
            stack = [field[comp * depth + at : comp * depth + at + group] for field in fields]
            stack += [value * field[2 * depth + at : 2 * depth + at + group] for value, field in zip(stack, fields)]
            right.append(jnp.concatenate(stack, axis=0))
    result = dot_split(matrix[...], jnp.concatenate(right, axis=1))
    for t in range(quad):
        for i in range(len(right)):
            parts[t][i * group : (i + 1) * group] = result[
                t * group : (t + 1) * group, i * length : (i + 1) * length
            ]


def circulant_rows(row, length):
    return pltpu.roll(jnp.broadcast_to(row, (length, length)), 0, 1, stride=1, stride_axis=0)


def span_matrix_kernel(
    rows, cols, zloc, wall_counts, z_first, z_second, field, z_matrix, mask, held, ends, others
):
    held[...] = field[...]
    me = lax.axis_index("row")
    mask[...] = (lax.broadcasted_iota(jnp.int32, mask.shape, 0) // zloc < wall_counts[me]).astype(jnp.float32)
    depth = mask.shape[0]
    plane = lax.broadcasted_iota(jnp.int32, (depth, ends.shape[1]), 0) // zloc
    cell = lax.broadcasted_iota(jnp.int32, (depth, ends.shape[1]), 1)

    def spots(index):
        start = lax.fori_loop(0, rows, lambda i, acc: acc + jnp.where(i < index, wall_counts[i], 0), 0, unroll=True)
        return ((plane < wall_counts[index]) & (plane + start == cell)).astype(jnp.float32)

    for i in range(2):
        ends[i * depth : (i + 1) * depth] = spots(me ^ i)
    for i in range(rows // 2):
        others[i * depth : (i + 1) * depth] = spots(me ^ (2 * i))

    cells_z = cols * zloc
    shape = z_matrix.shape
    half = shape[1] // 2
    group = shape[0] // quad
    mine = lax.axis_index("col")
    r = lax.broadcasted_iota(jnp.int32, shape, 0)
    q = lax.broadcasted_iota(jnp.int32, shape, 1)
    q = jnp.where(q < half, q, q - half)
    out_cell = ((r // group) ^ mine) * zloc + r % zloc
    in_cell = (over(q // group) ^ mine) * zloc + q % zloc
    same = (r % group) // zloc == (q % group) // zloc
    gap = jnp.where(same, (in_cell - out_cell + cells_z) % cells_z, -1)
    kind = lax.broadcasted_iota(jnp.int32, (1, shape[1]), 1) < half

    def fill(k, total):
        value = jnp.where(kind, viscosity * z_second[k], -z_first[k])
        return jnp.where(gap == k, value, total)

    z_matrix[...] = lax.fori_loop(0, cells_z, fill, jnp.zeros(shape, jnp.float32), unroll=8)


def stream_kernel(comps, field, x_first, x_second, after, x_part):
    length = field.shape[1]
    depth = field.shape[0] // comps
    u = field[...]
    lead = u[:depth]
    left = jnp.concatenate(
        [u, jnp.concatenate([lead * u[c * depth : (c + 1) * depth] for c in range(comps)], axis=0)], axis=1
    )
    right = jnp.concatenate(
        [viscosity * circulant_rows(x_second[...], length), -circulant_rows(x_first[...], length)], axis=1
    )
    x_part[...] = dot_split(left, right, transposed=True)


def wall_matrix_kernel(zloc, ends, others, metric_table, metric_index, y_first, y_second, after, matrix):
    cells = y_first.shape[0]
    depth = matrix.shape[0] // 2
    plain = functools.partial(
        lax.dot_general, dimension_numbers=(((1,), (0,)), ((), ())), preferred_element_type=jnp.float32
    )
    turned = functools.partial(
        lax.dot_general, dimension_numbers=(((1,), (1,)), ((), ())), preferred_element_type=jnp.float32
    )
    levels = metric_table.shape[1]
    entry = (lax.broadcasted_iota(jnp.int32, (levels, cells), 0) == metric_index[...]).astype(jnp.float32)
    table = jnp.broadcast_to(metric_table[...], (8, levels))
    metric = plain(table, entry, precision=lax.Precision.HIGHEST)[:1]
    scale = jnp.sum(ends[...] * metric, axis=1, keepdims=True)
    pick = ends[...].astype(jnp.bfloat16)
    second = sum(plain(pick, part) for part in halves(viscosity * y_second[...]))
    first = -scale * sum(plain(pick, part) for part in halves(y_first[...]))
    other = others[...].astype(jnp.bfloat16)
    wide = sum(turned(part, other) for part in halves(jnp.concatenate([second, first], axis=0)))
    match = lax.broadcasted_iota(jnp.int32, wide.shape, 0) % zloc == lax.broadcasted_iota(jnp.int32, wide.shape, 1) % zloc
    wide = jnp.where(match, wide, 0.0)
    for b in range(others.shape[0] // depth):
        for k in range(2):
            matrix[:, (2 * b + k) * depth : (2 * b + k + 1) * depth] = wide[
                2 * k * depth : 2 * (k + 1) * depth, b * depth : (b + 1) * depth
            ]


def wall_kernel(comps, matrix, z_part, *refs):
    fields, (total, away) = refs[:-2], refs[-2:]
    depth = z_part.shape[0] // comps
    for comp in range(comps):
        at = slice(comp * depth, (comp + 1) * depth)
        stack = []
        for field in fields:
            stack += [field[at], field[depth : 2 * depth] * field[at]]
        result = dot_split(matrix[...], jnp.concatenate(stack, axis=0))
        total[at] = z_part[at] + result[:depth]
        away[at] = result[depth:]


def sum_kernel(comps, mask, *refs):
    parts, out = refs[:-1], refs[-1]
    depth = mask.shape[0]
    for comp in range(comps):
        at = slice(comp * depth, (comp + 1) * depth)
        out[at] = jnp.where(mask[...] > 0, sum(part[at] for part in parts[1:]) + parts[0][at], 0.0)


def finish_kernel(total, near, out):
    out[...] = total[...] + near[...]


def call(kernel, operands, spaces, results, name, scratch=(), cost=None):
    results = [jax.ShapeDtypeStruct(shape, jnp.float32) for shape in results]
    held = sum(4 * math.prod(array.shape) for array in list(operands) + results)
    return pl.pallas_call(
        kernel,
        out_shape=results,
        in_specs=[pl.BlockSpec(memory_space=space) for space in spaces],
        out_specs=[pl.BlockSpec(memory_space=VMEM)] * len(results),
        scratch_shapes=[pltpu.VMEM(shape, jnp.float32) for shape in scratch],
        compiler_params=pltpu.CompilerParams(vmem_limit_bytes=(4 << 20) + 3 * held),
        cost_estimate=cost,
        name=name,
    )(*operands)


def local(
    velocity,
    wall_counts,
    x_first,
    x_second,
    y_first,
    y_second,
    z_first,
    z_second,
    metric_table,
    metric_index,
):
    rows = lax.axis_size("row")
    cols = lax.axis_size("col")
    comps, slots, zloc, length = velocity.shape
    depth = slots * zloc
    field = velocity.reshape(comps * depth, length)
    group = min(depth, 32)
    wide = cols // quad

    def along(value, step):
        return lax.ppermute(value, "col", [(i, i ^ step) for i in range(cols)])

    def across(value, step):
        return lax.ppermute(value, "row", [(i, i ^ step) for i in range(rows)])

    gathered = [along(field, over(t)) for t in range(1, wide)]
    cells = metric_index.shape[0]
    z_matrix, mask, held, ends, others = call(
        functools.partial(span_matrix_kernel, rows, cols, zloc),
        [wall_counts, z_first, z_second, field],
        [SMEM] * 3 + [VMEM],
        [
            (quad * group, 2 * wide * group),
            (depth, length),
            field.shape,
            (2 * depth, cells),
            (rows // 2 * depth, cells),
        ],
        "span_matrix",
    )
    far = [across(held, step) for step in range(2, rows, 2)]
    parts = call(
        functools.partial(span_kernel, comps, wide),
        [z_matrix, field] + gathered,
        [VMEM] * (1 + wide),
        [field.shape] * quad,
        "span",
    )
    returned = [along(parts[t], t) for t in (3, 1, 2)]
    (y_matrix,) = call(
        functools.partial(wall_matrix_kernel, zloc),
        [ends, others, metric_table.reshape(1, -1), metric_index.reshape(1, -1), y_first, y_second, parts[0]],
        [VMEM] * 6 + [pl.ANY],
        [(2 * depth, rows * depth)],
        "wall_matrix",
    )
    total, away = call(
        functools.partial(wall_kernel, comps),
        [y_matrix, parts[0], field] + far,
        [VMEM] * (3 + len(far)),
        [field.shape] * 2,
        "wall",
    )
    near = across(away, 1)
    (x_part,) = call(
        functools.partial(stream_kernel, comps),
        [field, x_first.reshape(1, length), x_second.reshape(1, length), away],
        [VMEM] * 3 + [pl.ANY],
        [field.shape],
        "stream",
    )
    (summed,) = call(
        functools.partial(sum_kernel, comps),
        [mask, total, x_part] + returned,
        [VMEM] * (3 + len(returned)),
        [field.shape],
        "sum",
        cost=pl.CostEstimate(flops=1 << 30, bytes_accessed=1 << 22, transcendentals=0),
    )
    (result,) = call(finish_kernel, [summed, near], [VMEM] * 2, [field.shape], "finish")
    return result.reshape(velocity.shape)


def solution(mesh):
    in_specs = (P(None, "row", "col", None), P(), P(), P(), P(), P(), P(), P(), P(), P())
    out_specs = P(None, "row", "col", None)
    return jax.shard_map(local, mesh=mesh, in_specs=in_specs, out_specs=out_specs, check_vma=False)
```

```python
import functools
import math

import jax
import jax.numpy as jnp
from jax import lax
from jax.experimental import pallas as pl
from jax.experimental.pallas import tpu as pltpu
from jax.sharding import PartitionSpec as P

viscosity = 0.4
quad = 4

VMEM = pltpu.VMEM
SMEM = pltpu.SMEM


def halves(value):
    high = value.astype(jnp.bfloat16)
    low = (value - high.astype(jnp.float32)).astype(jnp.bfloat16)
    return high, low


def dot_split(left, right, transposed=False):
    dims = (((1,), (1 if transposed else 0,)), ((), ()))
    mul = functools.partial(lax.dot_general, dimension_numbers=dims, preferred_element_type=jnp.float32)
    lh, ll = halves(left)
    rh, rl = halves(right)
    both = mul(jnp.concatenate([lh, ll], axis=0), rh)
    count = left.shape[0]
    return both[:count] + (mul(lh, rl) + both[count:])


def over(t):
    return quad * t + 2 * (t != 0)


def reach(t, odd):
    return t if odd else (t + 1) % 3 + 1 if t else 0


def span_kernel(comps, sources, matrix, *refs):
    fields, parts = refs[:sources], refs[sources:]
    depth, length = fields[0].shape[0] // comps, fields[0].shape[1]
    group = matrix.shape[0] // quad
    right = []
    for comp in range(comps):
        for at in range(0, depth, group):
            stack = [field[comp * depth + at : comp * depth + at + group] for field in fields]
            stack += [value * field[2 * depth + at : 2 * depth + at + group] for value, field in zip(stack, fields)]
            right.append(jnp.concatenate(stack, axis=0))
    result = dot_split(matrix[...], jnp.concatenate(right, axis=1))
    for t in range(quad):
        for i in range(len(right)):
            parts[t][i * group : (i + 1) * group] = result[
                t * group : (t + 1) * group, i * length : (i + 1) * length
            ]


def circulant_rows(row, length):
    return pltpu.roll(jnp.broadcast_to(row, (length, length)), 0, 1, stride=1, stride_axis=0)


def span_matrix_kernel(
    rows, cols, zloc, wall_counts, z_first, z_second, field, z_matrix, mask, held, ends, others
):
    held[...] = field[...]
    me = lax.axis_index("row")
    mask[...] = (lax.broadcasted_iota(jnp.int32, mask.shape, 0) // zloc < wall_counts[me]).astype(jnp.float32)
    depth = mask.shape[0]
    plane = lax.broadcasted_iota(jnp.int32, (depth, ends.shape[1]), 0) // zloc
    cell = lax.broadcasted_iota(jnp.int32, (depth, ends.shape[1]), 1)

    def spots(index):
        start = lax.fori_loop(0, rows, lambda i, acc: acc + jnp.where(i < index, wall_counts[i], 0), 0, unroll=True)
        return ((plane < wall_counts[index]) & (plane + start == cell)).astype(jnp.float32)

    for i in range(2):
        ends[i * depth : (i + 1) * depth] = spots(me ^ i)
    for i in range(rows // 2):
        others[i * depth : (i + 1) * depth] = spots(me ^ (2 * i))

    cells_z = cols * zloc
    shape = z_matrix.shape
    half = shape[1] // 2
    group = shape[0] // quad
    mine = lax.axis_index("col")
    r = lax.broadcasted_iota(jnp.int32, shape, 0)
    q = lax.broadcasted_iota(jnp.int32, shape, 1)
    q = jnp.where(q < half, q, q - half)
    odd = lax.axis_index("row") % 2
    distance = jnp.zeros(shape, jnp.int32)
    for t in range(1, quad):
        distance = jnp.where(r // group == t, jnp.where(odd == 1, reach(t, 1), reach(t, 0)), distance)
    out_cell = (distance ^ mine) * zloc + r % zloc
    in_cell = (over(q // group) ^ mine) * zloc + q % zloc
    same = (r % group) // zloc == (q % group) // zloc
    gap = jnp.where(same, (in_cell - out_cell + cells_z) % cells_z, -1)
    kind = lax.broadcasted_iota(jnp.int32, (1, shape[1]), 1) < half

    def fill(k, total):
        value = jnp.where(kind, viscosity * z_second[k], -z_first[k])
        return jnp.where(gap == k, value, total)

    z_matrix[...] = lax.fori_loop(0, cells_z, fill, jnp.zeros(shape, jnp.float32), unroll=8)


def stream_kernel(comps, field, x_first, x_second, after, x_part):
    length = field.shape[1]
    depth = field.shape[0] // comps
    u = field[...]
    lead = u[:depth]
    left = jnp.concatenate(
        [u, jnp.concatenate([lead * u[c * depth : (c + 1) * depth] for c in range(comps)], axis=0)], axis=1
    )
    right = jnp.concatenate(
        [viscosity * circulant_rows(x_second[...], length), -circulant_rows(x_first[...], length)], axis=1
    )
    x_part[...] = dot_split(left, right, transposed=True)


def wall_matrix_kernel(zloc, ends, others, metric_table, metric_index, y_first, y_second, after, matrix):
    cells = y_first.shape[0]
    depth = matrix.shape[0] // 2
    plain = functools.partial(
        lax.dot_general, dimension_numbers=(((1,), (0,)), ((), ())), preferred_element_type=jnp.float32
    )
    turned = functools.partial(
        lax.dot_general, dimension_numbers=(((1,), (1,)), ((), ())), preferred_element_type=jnp.float32
    )
    levels = metric_table.shape[1]
    entry = (lax.broadcasted_iota(jnp.int32, (levels, cells), 0) == metric_index[...]).astype(jnp.float32)
    table = jnp.broadcast_to(metric_table[...], (8, levels))
    metric = plain(table, entry, precision=lax.Precision.HIGHEST)[:1]
    scale = jnp.sum(ends[...] * metric, axis=1, keepdims=True)
    pick = ends[...].astype(jnp.bfloat16)
    second = sum(plain(pick, part) for part in halves(viscosity * y_second[...]))
    first = -scale * sum(plain(pick, part) for part in halves(y_first[...]))
    other = others[...].astype(jnp.bfloat16)
    wide = sum(turned(part, other) for part in halves(jnp.concatenate([second, first], axis=0)))
    match = lax.broadcasted_iota(jnp.int32, wide.shape, 0) % zloc == lax.broadcasted_iota(jnp.int32, wide.shape, 1) % zloc
    wide = jnp.where(match, wide, 0.0)
    for b in range(others.shape[0] // depth):
        for k in range(2):
            matrix[:, (2 * b + k) * depth : (2 * b + k + 1) * depth] = wide[
                2 * k * depth : 2 * (k + 1) * depth, b * depth : (b + 1) * depth
            ]


def wall_kernel(comps, matrix, z_part, *refs):
    fields, (total, away) = refs[:-2], refs[-2:]
    depth = z_part.shape[0] // comps
    for comp in range(comps):
        at = slice(comp * depth, (comp + 1) * depth)
        stack = []
        for field in fields:
            stack += [field[at], field[depth : 2 * depth] * field[at]]
        result = dot_split(matrix[...], jnp.concatenate(stack, axis=0))
        total[at] = z_part[at] + result[:depth]
        away[at] = result[depth:]


def sum_kernel(comps, mask, *refs):
    parts, out = refs[:-1], refs[-1]
    depth = mask.shape[0]
    for comp in range(comps):
        at = slice(comp * depth, (comp + 1) * depth)
        out[at] = jnp.where(mask[...] > 0, sum(part[at] for part in parts[1:]) + parts[0][at], 0.0)


def finish_kernel(total, near, out):
    out[...] = total[...] + near[...]


def call(kernel, operands, spaces, results, name, scratch=(), cost=None):
    results = [jax.ShapeDtypeStruct(shape, jnp.float32) for shape in results]
    held = sum(4 * math.prod(array.shape) for array in list(operands) + results)
    return pl.pallas_call(
        kernel,
        out_shape=results,
        in_specs=[pl.BlockSpec(memory_space=space) for space in spaces],
        out_specs=[pl.BlockSpec(memory_space=VMEM)] * len(results),
        scratch_shapes=[pltpu.VMEM(shape, jnp.float32) for shape in scratch],
        compiler_params=pltpu.CompilerParams(vmem_limit_bytes=(4 << 20) + 3 * held),
        cost_estimate=cost,
        name=name,
    )(*operands)


def local(
    velocity,
    wall_counts,
    x_first,
    x_second,
    y_first,
    y_second,
    z_first,
    z_second,
    metric_table,
    metric_index,
):
    rows = lax.axis_size("row")
    cols = lax.axis_size("col")
    comps, slots, zloc, length = velocity.shape
    depth = slots * zloc
    field = velocity.reshape(comps * depth, length)
    group = min(depth, 32)
    wide = cols // quad

    def along(value, step):
        return lax.ppermute(value, "col", [(i, i ^ step) for i in range(cols)])

    def across(value, step):
        return lax.ppermute(value, "row", [(i, i ^ step) for i in range(rows)])

    gathered = [along(field, over(t)) for t in range(1, wide)]
    cells = metric_index.shape[0]
    z_matrix, mask, held, ends, others = call(
        functools.partial(span_matrix_kernel, rows, cols, zloc),
        [wall_counts, z_first, z_second, field],
        [SMEM] * 3 + [VMEM],
        [
            (quad * group, 2 * wide * group),
            (depth, length),
            field.shape,
            (2 * depth, cells),
            (rows // 2 * depth, cells),
        ],
        "span_matrix",
    )
    far = [across(held, step) for step in range(2, rows, 2)]
    parts = call(
        functools.partial(span_kernel, comps, wide),
        [z_matrix, field] + gathered,
        [VMEM] * (1 + wide),
        [field.shape] * quad,
        "span",
    )
    returned = [
        lax.ppermute(
            parts[t],
            ("row", "col"),
            [(i * cols + j, i * cols + (j ^ reach(t, i % 2))) for i in range(rows) for j in range(cols)],
        )
        for t in range(1, quad)
    ]
    (y_matrix,) = call(
        functools.partial(wall_matrix_kernel, zloc),
        [ends, others, metric_table.reshape(1, -1), metric_index.reshape(1, -1), y_first, y_second, parts[0]],
        [VMEM] * 6 + [pl.ANY],
        [(2 * depth, rows * depth)],
        "wall_matrix",
    )
    total, away = call(
        functools.partial(wall_kernel, comps),
        [y_matrix, parts[0], field] + far,
        [VMEM] * (3 + len(far)),
        [field.shape] * 2,
        "wall",
    )
    near = across(away, 1)
    (x_part,) = call(
        functools.partial(stream_kernel, comps),
        [field, x_first.reshape(1, length), x_second.reshape(1, length), away],
        [VMEM] * 3 + [pl.ANY],
        [field.shape],
        "stream",
    )
    (summed,) = call(
        functools.partial(sum_kernel, comps),
        [mask, total, x_part] + returned,
        [VMEM] * (3 + len(returned)),
        [field.shape],
        "sum",
        cost=pl.CostEstimate(flops=1 << 30, bytes_accessed=1 << 22, transcendentals=0),
    )
    (result,) = call(finish_kernel, [summed, near], [VMEM] * 2, [field.shape], "finish")
    return result.reshape(velocity.shape)


def solution(mesh):
    in_specs = (P(None, "row", "col", None), P(), P(), P(), P(), P(), P(), P(), P(), P())
    out_specs = P(None, "row", "col", None)
    return jax.shard_map(local, mesh=mesh, in_specs=in_specs, out_specs=out_specs, check_vma=False)
```

```python
import functools
import math

import jax
import jax.numpy as jnp
from jax import lax
from jax.experimental import pallas as pl
from jax.experimental.pallas import tpu as pltpu
from jax.sharding import PartitionSpec as P

viscosity = 0.4
quad = 4

VMEM = pltpu.VMEM
SMEM = pltpu.SMEM


def halves(value):
    high = value.astype(jnp.bfloat16)
    low = (value - high.astype(jnp.float32)).astype(jnp.bfloat16)
    return high, low


def dot_split(left, right, transposed=False):
    dims = (((1,), (1 if transposed else 0,)), ((), ()))
    mul = functools.partial(lax.dot_general, dimension_numbers=dims, preferred_element_type=jnp.float32)
    lh, ll = halves(left)
    rh, rl = halves(right)
    both = mul(jnp.concatenate([lh, ll], axis=0), rh)
    count = left.shape[0]
    return both[:count] + (mul(lh, rl) + both[count:])


def over(t):
    return quad * t + 2 * (t != 0)


def quad_step(s, odd):
    return (quad - s) % quad if odd else s


def quad_sums(comps, matrix, fields, chosen):
    depth, length = fields[0].shape[0] // comps, fields[0].shape[1]
    half = matrix.shape[1] // 2
    group = half // quad
    left = jnp.concatenate(
        [matrix[:, start + s * group : start + (s + 1) * group] for start in (0, half) for s in chosen], axis=1
    )
    right = []
    for comp in range(comps):
        for at in range(0, depth, group):
            stack = [field[comp * depth + at : comp * depth + at + group] for field in fields]
            stack += [value * field[2 * depth + at : 2 * depth + at + group] for value, field in zip(stack, fields)]
            right.append(jnp.concatenate(stack, axis=0))
    return dot_split(left, jnp.concatenate(right, axis=1))


def early_kernel(comps, chosen, matrix, *refs):
    refs[-1][...] = quad_sums(comps, matrix, refs[:-1], chosen)


def span_kernel(comps, chosen, matrix, early, *refs):
    fields, parts = refs[: len(chosen)], refs[len(chosen) :]
    result = early[...] + quad_sums(comps, matrix, fields, chosen)
    rows, length = parts[0].shape
    count = len(parts)
    group = result.shape[0] // count
    for t in range(count):
        for i in range(rows // group):
            parts[t][i * group : (i + 1) * group] = result[
                t * group : (t + 1) * group, i * length : (i + 1) * length
            ]


def circulant_rows(row, length):
    return pltpu.roll(jnp.broadcast_to(row, (length, length)), 0, 1, stride=1, stride_axis=0)


def span_matrix_kernel(
    rows, cols, zloc, wall_counts, z_first, z_second, field, z_matrix, mask, held, ends, others
):
    held[...] = field[...]
    me = lax.axis_index("row")
    mask[...] = (lax.broadcasted_iota(jnp.int32, mask.shape, 0) // zloc < wall_counts[me]).astype(jnp.float32)
    depth = mask.shape[0]
    plane = lax.broadcasted_iota(jnp.int32, (depth, ends.shape[1]), 0) // zloc
    cell = lax.broadcasted_iota(jnp.int32, (depth, ends.shape[1]), 1)

    def spots(index):
        start = lax.fori_loop(0, rows, lambda i, acc: acc + jnp.where(i < index, wall_counts[i], 0), 0, unroll=True)
        return ((plane < wall_counts[index]) & (plane + start == cell)).astype(jnp.float32)

    for i in range(2):
        ends[i * depth : (i + 1) * depth] = spots(me ^ i)
    for i in range(rows // 2):
        others[i * depth : (i + 1) * depth] = spots(me ^ (2 * i))

    cells_z = cols * zloc
    shape = z_matrix.shape
    half = shape[1] // 2
    group = half // quad
    mine = lax.axis_index("col")
    r = lax.broadcasted_iota(jnp.int32, shape, 0)
    q = lax.broadcasted_iota(jnp.int32, shape, 1)
    q = jnp.where(q < half, q, q - half)
    out_cell = (over(r // group) ^ mine) * zloc + r % zloc
    odd = lax.axis_index("row") % 2
    in_cell = (jnp.where(odd == 1, quad_step(q // group, 1), q // group) ^ mine) * zloc + q % zloc
    same = (r % group) // zloc == (q % group) // zloc
    gap = jnp.where(same, (in_cell - out_cell + cells_z) % cells_z, -1)
    kind = lax.broadcasted_iota(jnp.int32, (1, shape[1]), 1) < half

    def fill(k, total):
        value = jnp.where(kind, viscosity * z_second[k], -z_first[k])
        return jnp.where(gap == k, value, total)

    z_matrix[...] = lax.fori_loop(0, cells_z, fill, jnp.zeros(shape, jnp.float32), unroll=8)


def stream_kernel(comps, field, x_first, x_second, after, x_part):
    length = field.shape[1]
    depth = field.shape[0] // comps
    u = field[...]
    lead = u[:depth]
    left = jnp.concatenate(
        [u, jnp.concatenate([lead * u[c * depth : (c + 1) * depth] for c in range(comps)], axis=0)], axis=1
    )
    right = jnp.concatenate(
        [viscosity * circulant_rows(x_second[...], length), -circulant_rows(x_first[...], length)], axis=1
    )
    x_part[...] = dot_split(left, right, transposed=True)


def wall_matrix_kernel(zloc, ends, others, metric_table, metric_index, y_first, y_second, after, matrix):
    cells = y_first.shape[0]
    depth = matrix.shape[0] // 2
    plain = functools.partial(
        lax.dot_general, dimension_numbers=(((1,), (0,)), ((), ())), preferred_element_type=jnp.float32
    )
    turned = functools.partial(
        lax.dot_general, dimension_numbers=(((1,), (1,)), ((), ())), preferred_element_type=jnp.float32
    )
    levels = metric_table.shape[1]
    entry = (lax.broadcasted_iota(jnp.int32, (levels, cells), 0) == metric_index[...]).astype(jnp.float32)
    table = jnp.broadcast_to(metric_table[...], (8, levels))
    metric = plain(table, entry, precision=lax.Precision.HIGHEST)[:1]
    scale = jnp.sum(ends[...] * metric, axis=1, keepdims=True)
    pick = ends[...].astype(jnp.bfloat16)
    second = sum(plain(pick, part) for part in halves(viscosity * y_second[...]))
    first = -scale * sum(plain(pick, part) for part in halves(y_first[...]))
    other = others[...].astype(jnp.bfloat16)
    wide = sum(turned(part, other) for part in halves(jnp.concatenate([second, first], axis=0)))
    match = lax.broadcasted_iota(jnp.int32, wide.shape, 0) % zloc == lax.broadcasted_iota(jnp.int32, wide.shape, 1) % zloc
    wide = jnp.where(match, wide, 0.0)
    for b in range(others.shape[0] // depth):
        for k in range(2):
            matrix[:, (2 * b + k) * depth : (2 * b + k + 1) * depth] = wide[
                2 * k * depth : 2 * (k + 1) * depth, b * depth : (b + 1) * depth
            ]


def wall_kernel(comps, matrix, z_part, *refs):
    fields, (total, away) = refs[:-2], refs[-2:]
    depth = z_part.shape[0] // comps
    for comp in range(comps):
        at = slice(comp * depth, (comp + 1) * depth)
        stack = []
        for field in fields:
            stack += [field[at], field[depth : 2 * depth] * field[at]]
        result = dot_split(matrix[...], jnp.concatenate(stack, axis=0))
        total[at] = z_part[at] + result[:depth]
        away[at] = result[depth:]


def sum_kernel(comps, mask, *refs):
    parts, out = refs[:-1], refs[-1]
    depth = mask.shape[0]
    for comp in range(comps):
        at = slice(comp * depth, (comp + 1) * depth)
        out[at] = jnp.where(mask[...] > 0, sum(part[at] for part in parts[1:]) + parts[0][at], 0.0)


def finish_kernel(total, near, out):
    out[...] = total[...] + near[...]


def call(kernel, operands, spaces, results, name, scratch=(), cost=None):
    results = [jax.ShapeDtypeStruct(shape, jnp.float32) for shape in results]
    held = sum(4 * math.prod(array.shape) for array in list(operands) + results)
    return pl.pallas_call(
        kernel,
        out_shape=results,
        in_specs=[pl.BlockSpec(memory_space=space) for space in spaces],
        out_specs=[pl.BlockSpec(memory_space=VMEM)] * len(results),
        scratch_shapes=[pltpu.VMEM(shape, jnp.float32) for shape in scratch],
        compiler_params=pltpu.CompilerParams(vmem_limit_bytes=(4 << 20) + 3 * held),
        cost_estimate=cost,
        name=name,
    )(*operands)


def local(
    velocity,
    wall_counts,
    x_first,
    x_second,
    y_first,
    y_second,
    z_first,
    z_second,
    metric_table,
    metric_index,
):
    rows = lax.axis_size("row")
    cols = lax.axis_size("col")
    comps, slots, zloc, length = velocity.shape
    depth = slots * zloc
    field = velocity.reshape(comps * depth, length)
    group = min(depth, 32)
    wide = cols // quad

    def along(value, step):
        return lax.ppermute(value, "col", [(i, i ^ step) for i in range(cols)])

    def across(value, step):
        return lax.ppermute(value, "row", [(i, i ^ step) for i in range(rows)])

    gathered = [
        lax.ppermute(
            field,
            ("row", "col"),
            [(i * cols + j, i * cols + (j ^ quad_step(s, i % 2))) for i in range(rows) for j in range(cols)],
        )
        for s in range(1, quad)
    ]
    cells = metric_index.shape[0]
    z_matrix, mask, held, ends, others = call(
        functools.partial(span_matrix_kernel, rows, cols, zloc),
        [wall_counts, z_first, z_second, field],
        [SMEM] * 3 + [VMEM],
        [
            (wide * group, 2 * quad * group),
            (depth, length),
            field.shape,
            (2 * depth, cells),
            (rows // 2 * depth, cells),
        ],
        "span_matrix",
    )
    far = [across(held, step) for step in range(2, rows, 2)]
    (early,) = call(
        functools.partial(early_kernel, comps, (0, quad - 1)),
        [z_matrix, field, gathered[-1]],
        [VMEM] * 3,
        [(wide * group, comps * (depth // group) * length)],
        "early",
    )
    parts = call(
        functools.partial(span_kernel, comps, tuple(range(1, quad - 1))),
        [z_matrix, early] + gathered[:-1],
        [VMEM] * quad,
        [field.shape] * wide,
        "span",
    )
    returned = [along(parts[t], over(t)) for t in range(1, wide)]
    (y_matrix,) = call(
        functools.partial(wall_matrix_kernel, zloc),
        [ends, others, metric_table.reshape(1, -1), metric_index.reshape(1, -1), y_first, y_second, parts[0]],
        [VMEM] * 6 + [pl.ANY],
        [(2 * depth, rows * depth)],
        "wall_matrix",
    )
    total, away = call(
        functools.partial(wall_kernel, comps),
        [y_matrix, parts[0], field] + far,
        [VMEM] * (3 + len(far)),
        [field.shape] * 2,
        "wall",
    )
    near = across(away, 1)
    (x_part,) = call(
        functools.partial(stream_kernel, comps),
        [field, x_first.reshape(1, length), x_second.reshape(1, length), away],
        [VMEM] * 3 + [pl.ANY],
        [field.shape],
        "stream",
    )
    (summed,) = call(
        functools.partial(sum_kernel, comps),
        [mask, total, x_part] + returned,
        [VMEM] * (3 + len(returned)),
        [field.shape],
        "sum",
        cost=pl.CostEstimate(flops=1 << 30, bytes_accessed=1 << 22, transcendentals=0),
    )
    (result,) = call(finish_kernel, [summed, near], [VMEM] * 2, [field.shape], "finish")
    return result.reshape(velocity.shape)


def solution(mesh):
    in_specs = (P(None, "row", "col", None), P(), P(), P(), P(), P(), P(), P(), P(), P())
    out_specs = P(None, "row", "col", None)
    return jax.shard_map(local, mesh=mesh, in_specs=in_specs, out_specs=out_specs, check_vma=False)
```

```python
import functools
import math

import jax
import jax.numpy as jnp
from jax import lax
from jax.experimental import pallas as pl
from jax.experimental.pallas import tpu as pltpu
from jax.sharding import PartitionSpec as P

viscosity = 0.4
quad = 4

VMEM = pltpu.VMEM
SMEM = pltpu.SMEM


def halves(value):
    high = value.astype(jnp.bfloat16)
    low = (value - high.astype(jnp.float32)).astype(jnp.bfloat16)
    return high, low


def dot_split(left, right, transposed=False):
    dims = (((1,), (1 if transposed else 0,)), ((), ()))
    mul = functools.partial(lax.dot_general, dimension_numbers=dims, preferred_element_type=jnp.float32)
    lh, ll = halves(left)
    rh, rl = halves(right)
    both = mul(jnp.concatenate([lh, ll], axis=0), rh)
    count = left.shape[0]
    return both[:count] + (mul(lh, rl) + both[count:])


def over(t, odd):
    return quad * t + (0 if odd else 2 * (t != 0))


def quad_sums(comps, matrix, fields, chosen):
    depth, length = fields[0].shape[0] // comps, fields[0].shape[1]
    half = matrix.shape[1] // 2
    group = half // quad
    left = jnp.concatenate(
        [matrix[:, start + s * group : start + (s + 1) * group] for start in (0, half) for s in chosen], axis=1
    )
    right = []
    for comp in range(comps):
        for at in range(0, depth, group):
            stack = [field[comp * depth + at : comp * depth + at + group] for field in fields]
            stack += [value * field[2 * depth + at : 2 * depth + at + group] for value, field in zip(stack, fields)]
            right.append(jnp.concatenate(stack, axis=0))
    return dot_split(left, jnp.concatenate(right, axis=1))


def early_kernel(comps, chosen, matrix, *refs):
    refs[-1][...] = quad_sums(comps, matrix, refs[:-1], chosen)


def span_kernel(comps, chosen, matrix, early, *refs):
    fields, parts = refs[: len(chosen)], refs[len(chosen) :]
    result = early[...] + quad_sums(comps, matrix, fields, chosen)
    rows, length = parts[0].shape
    count = len(parts)
    group = result.shape[0] // count
    for t in range(count):
        for i in range(rows // group):
            parts[t][i * group : (i + 1) * group] = result[
                t * group : (t + 1) * group, i * length : (i + 1) * length
            ]


def circulant_rows(row, length):
    return pltpu.roll(jnp.broadcast_to(row, (length, length)), 0, 1, stride=1, stride_axis=0)


def span_matrix_kernel(
    rows, cols, zloc, wall_counts, z_first, z_second, field, z_matrix, mask, held, ends, others
):
    held[...] = field[...]
    me = lax.axis_index("row")
    mask[...] = (lax.broadcasted_iota(jnp.int32, mask.shape, 0) // zloc < wall_counts[me]).astype(jnp.float32)
    depth = mask.shape[0]
    plane = lax.broadcasted_iota(jnp.int32, (depth, ends.shape[1]), 0) // zloc
    cell = lax.broadcasted_iota(jnp.int32, (depth, ends.shape[1]), 1)

    def spots(index):
        start = lax.fori_loop(0, rows, lambda i, acc: acc + jnp.where(i < index, wall_counts[i], 0), 0, unroll=True)
        return ((plane < wall_counts[index]) & (plane + start == cell)).astype(jnp.float32)

    for i in range(2):
        ends[i * depth : (i + 1) * depth] = spots(me ^ i)
    for i in range(rows // 2):
        others[i * depth : (i + 1) * depth] = spots(me ^ (2 * i))

    cells_z = cols * zloc
    shape = z_matrix.shape
    half = shape[1] // 2
    group = half // quad
    mine = lax.axis_index("col")
    r = lax.broadcasted_iota(jnp.int32, shape, 0)
    q = lax.broadcasted_iota(jnp.int32, shape, 1)
    q = jnp.where(q < half, q, q - half)
    odd = lax.axis_index("row") % 2
    out_cell = (jnp.where(odd == 1, over(r // group, 1), over(r // group, 0)) ^ mine) * zloc + r % zloc
    in_cell = ((q // group) ^ mine) * zloc + q % zloc
    same = (r % group) // zloc == (q % group) // zloc
    gap = jnp.where(same, (in_cell - out_cell + cells_z) % cells_z, -1)
    kind = lax.broadcasted_iota(jnp.int32, (1, shape[1]), 1) < half

    def fill(k, total):
        value = jnp.where(kind, viscosity * z_second[k], -z_first[k])
        return jnp.where(gap == k, value, total)

    z_matrix[...] = lax.fori_loop(0, cells_z, fill, jnp.zeros(shape, jnp.float32), unroll=8)


def stream_kernel(comps, field, x_first, x_second, after, x_part):
    length = field.shape[1]
    depth = field.shape[0] // comps
    u = field[...]
    lead = u[:depth]
    left = jnp.concatenate(
        [u, jnp.concatenate([lead * u[c * depth : (c + 1) * depth] for c in range(comps)], axis=0)], axis=1
    )
    right = jnp.concatenate(
        [viscosity * circulant_rows(x_second[...], length), -circulant_rows(x_first[...], length)], axis=1
    )
    x_part[...] = dot_split(left, right, transposed=True)


def wall_matrix_kernel(zloc, ends, others, metric_table, metric_index, y_first, y_second, after, matrix):
    cells = y_first.shape[0]
    depth = matrix.shape[0] // 2
    plain = functools.partial(
        lax.dot_general, dimension_numbers=(((1,), (0,)), ((), ())), preferred_element_type=jnp.float32
    )
    turned = functools.partial(
        lax.dot_general, dimension_numbers=(((1,), (1,)), ((), ())), preferred_element_type=jnp.float32
    )
    levels = metric_table.shape[1]
    entry = (lax.broadcasted_iota(jnp.int32, (levels, cells), 0) == metric_index[...]).astype(jnp.float32)
    table = jnp.broadcast_to(metric_table[...], (8, levels))
    metric = plain(table, entry, precision=lax.Precision.HIGHEST)[:1]
    scale = jnp.sum(ends[...] * metric, axis=1, keepdims=True)
    pick = ends[...].astype(jnp.bfloat16)
    second = sum(plain(pick, part) for part in halves(viscosity * y_second[...]))
    first = -scale * sum(plain(pick, part) for part in halves(y_first[...]))
    other = others[...].astype(jnp.bfloat16)
    wide = sum(turned(part, other) for part in halves(jnp.concatenate([second, first], axis=0)))
    match = lax.broadcasted_iota(jnp.int32, wide.shape, 0) % zloc == lax.broadcasted_iota(jnp.int32, wide.shape, 1) % zloc
    wide = jnp.where(match, wide, 0.0)
    for b in range(others.shape[0] // depth):
        for k in range(2):
            matrix[:, (2 * b + k) * depth : (2 * b + k + 1) * depth] = wide[
                2 * k * depth : 2 * (k + 1) * depth, b * depth : (b + 1) * depth
            ]


def wall_kernel(comps, matrix, z_part, *refs):
    fields, (total, away) = refs[:-2], refs[-2:]
    depth = z_part.shape[0] // comps
    for comp in range(comps):
        at = slice(comp * depth, (comp + 1) * depth)
        stack = []
        for field in fields:
            stack += [field[at], field[depth : 2 * depth] * field[at]]
        result = dot_split(matrix[...], jnp.concatenate(stack, axis=0))
        total[at] = z_part[at] + result[:depth]
        away[at] = result[depth:]


def sum_kernel(comps, mask, *refs):
    parts, out = refs[:-1], refs[-1]
    depth = mask.shape[0]
    for comp in range(comps):
        at = slice(comp * depth, (comp + 1) * depth)
        out[at] = jnp.where(mask[...] > 0, sum(part[at] for part in parts[1:]) + parts[0][at], 0.0)


def finish_kernel(total, near, out):
    out[...] = total[...] + near[...]


def call(kernel, operands, spaces, results, name, scratch=(), cost=None):
    results = [jax.ShapeDtypeStruct(shape, jnp.float32) for shape in results]
    held = sum(4 * math.prod(array.shape) for array in list(operands) + results)
    return pl.pallas_call(
        kernel,
        out_shape=results,
        in_specs=[pl.BlockSpec(memory_space=space) for space in spaces],
        out_specs=[pl.BlockSpec(memory_space=VMEM)] * len(results),
        scratch_shapes=[pltpu.VMEM(shape, jnp.float32) for shape in scratch],
        compiler_params=pltpu.CompilerParams(vmem_limit_bytes=(4 << 20) + 3 * held),
        cost_estimate=cost,
        name=name,
    )(*operands)


def local(
    velocity,
    wall_counts,
    x_first,
    x_second,
    y_first,
    y_second,
    z_first,
    z_second,
    metric_table,
    metric_index,
):
    rows = lax.axis_size("row")
    cols = lax.axis_size("col")
    comps, slots, zloc, length = velocity.shape
    depth = slots * zloc
    field = velocity.reshape(comps * depth, length)
    group = min(depth, 32)
    wide = cols // quad

    def along(value, step):
        return lax.ppermute(value, "col", [(i, i ^ step) for i in range(cols)])

    def across(value, step):
        return lax.ppermute(value, "row", [(i, i ^ step) for i in range(rows)])

    gathered = [along(field, t) for t in range(1, quad)]
    cells = metric_index.shape[0]
    z_matrix, mask, held, ends, others = call(
        functools.partial(span_matrix_kernel, rows, cols, zloc),
        [wall_counts, z_first, z_second, field],
        [SMEM] * 3 + [VMEM],
        [
            (wide * group, 2 * quad * group),
            (depth, length),
            field.shape,
            (2 * depth, cells),
            (rows // 2 * depth, cells),
        ],
        "span_matrix",
    )
    far = [across(held, step) for step in range(2, rows, 2)]
    (early,) = call(
        functools.partial(early_kernel, comps, (0, quad - 1)),
        [z_matrix, field, gathered[-1]],
        [VMEM] * 3,
        [(wide * group, comps * (depth // group) * length)],
        "early",
    )
    parts = call(
        functools.partial(span_kernel, comps, tuple(range(1, quad - 1))),
        [z_matrix, early] + gathered[:-1],
        [VMEM] * quad,
        [field.shape] * wide,
        "span",
    )
    returned = [
        lax.ppermute(
            parts[t],
            ("row", "col"),
            [(i * cols + j, i * cols + (j ^ over(t, i % 2))) for i in range(rows) for j in range(cols)],
        )
        for t in range(1, wide)
    ]
    (y_matrix,) = call(
        functools.partial(wall_matrix_kernel, zloc),
        [ends, others, metric_table.reshape(1, -1), metric_index.reshape(1, -1), y_first, y_second, parts[0]],
        [VMEM] * 6 + [pl.ANY],
        [(2 * depth, rows * depth)],
        "wall_matrix",
    )
    total, away = call(
        functools.partial(wall_kernel, comps),
        [y_matrix, parts[0], field] + far,
        [VMEM] * (3 + len(far)),
        [field.shape] * 2,
        "wall",
    )
    near = across(away, 1)
    (x_part,) = call(
        functools.partial(stream_kernel, comps),
        [field, x_first.reshape(1, length), x_second.reshape(1, length), away],
        [VMEM] * 3 + [pl.ANY],
        [field.shape],
        "stream",
    )
    (summed,) = call(
        functools.partial(sum_kernel, comps),
        [mask, total, x_part] + returned,
        [VMEM] * (3 + len(returned)),
        [field.shape],
        "sum",
        cost=pl.CostEstimate(flops=1 << 30, bytes_accessed=1 << 22, transcendentals=0),
    )
    (result,) = call(finish_kernel, [summed, near], [VMEM] * 2, [field.shape], "finish")
    return result.reshape(velocity.shape)


def solution(mesh):
    in_specs = (P(None, "row", "col", None), P(), P(), P(), P(), P(), P(), P(), P(), P())
    out_specs = P(None, "row", "col", None)
    return jax.shard_map(local, mesh=mesh, in_specs=in_specs, out_specs=out_specs, check_vma=False)
```

```python
import functools
import math

import jax
import jax.numpy as jnp
from jax import lax
from jax.experimental import pallas as pl
from jax.experimental.pallas import tpu as pltpu
from jax.sharding import PartitionSpec as P

viscosity = 0.4
quad = 4

VMEM = pltpu.VMEM
SMEM = pltpu.SMEM


def halves(value):
    high = value.astype(jnp.bfloat16)
    low = (value - high.astype(jnp.float32)).astype(jnp.bfloat16)
    return high, low


def dot_split(left, right, transposed=False):
    dims = (((1,), (1 if transposed else 0,)), ((), ()))
    mul = functools.partial(lax.dot_general, dimension_numbers=dims, preferred_element_type=jnp.float32)
    lh, ll = halves(left)
    rh, rl = halves(right)
    both = mul(jnp.concatenate([lh, ll], axis=0), rh)
    count = left.shape[0]
    return both[:count] + (mul(lh, rl) + both[count:])


def over(t, odd):
    return quad * t + (0 if odd else 2 * (t != 0))


def quad_sums(comps, matrix, fields, chosen):
    depth, length = fields[0].shape[0] // comps, fields[0].shape[1]
    half = matrix.shape[1] // 2
    group = half // quad
    left = jnp.concatenate(
        [matrix[:, start + s * group : start + (s + 1) * group] for start in (0, half) for s in chosen], axis=1
    )
    right = []
    for comp in range(comps):
        for at in range(0, depth, group):
            stack = [field[comp * depth + at : comp * depth + at + group] for field in fields]
            stack += [value * field[2 * depth + at : 2 * depth + at + group] for value, field in zip(stack, fields)]
            right.append(jnp.concatenate(stack, axis=0))
    return dot_split(left, jnp.concatenate(right, axis=1))


def early_kernel(comps, chosen, matrix, *refs):
    refs[-1][...] = quad_sums(comps, matrix, refs[:-1], chosen)


def span_kernel(comps, chosen, matrix, early, *refs):
    fields, parts = refs[: len(chosen)], refs[len(chosen) :]
    result = early[...] + quad_sums(comps, matrix, fields, chosen)
    rows, length = parts[0].shape
    count = len(parts)
    group = result.shape[0] // count
    for t in range(count):
        for i in range(rows // group):
            parts[t][i * group : (i + 1) * group] = result[
                t * group : (t + 1) * group, i * length : (i + 1) * length
            ]


def circulant_rows(row, length):
    return pltpu.roll(jnp.broadcast_to(row, (length, length)), 0, 1, stride=1, stride_axis=0)


def span_matrix_kernel(
    rows, cols, zloc, wall_counts, z_first, z_second, field, z_matrix, mask, held, ends, others
):
    held[...] = field[...]
    me = lax.axis_index("row")
    mask[...] = (lax.broadcasted_iota(jnp.int32, mask.shape, 0) // zloc < wall_counts[me]).astype(jnp.float32)
    depth = mask.shape[0]
    plane = lax.broadcasted_iota(jnp.int32, (depth, ends.shape[1]), 0) // zloc
    cell = lax.broadcasted_iota(jnp.int32, (depth, ends.shape[1]), 1)

    def spots(index):
        start = lax.fori_loop(0, rows, lambda i, acc: acc + jnp.where(i < index, wall_counts[i], 0), 0, unroll=True)
        return ((plane < wall_counts[index]) & (plane + start == cell)).astype(jnp.float32)

    for i in range(2):
        ends[i * depth : (i + 1) * depth] = spots(me ^ i)
    for i in range(rows // 2):
        others[i * depth : (i + 1) * depth] = spots(me ^ (2 * i))

    cells_z = cols * zloc
    shape = z_matrix.shape
    half = shape[1] // 2
    group = half // quad
    mine = lax.axis_index("col")
    r = lax.broadcasted_iota(jnp.int32, shape, 0)
    q = lax.broadcasted_iota(jnp.int32, shape, 1)
    q = jnp.where(q < half, q, q - half)
    odd = lax.axis_index("row") % 2
    out_cell = (jnp.where(odd == 1, over(r // group, 1), over(r // group, 0)) ^ mine) * zloc + r % zloc
    in_cell = ((q // group) ^ mine) * zloc + q % zloc
    same = (r % group) // zloc == (q % group) // zloc
    gap = jnp.where(same, (in_cell - out_cell + cells_z) % cells_z, -1)
    kind = lax.broadcasted_iota(jnp.int32, (1, shape[1]), 1) < half

    def fill(k, total):
        value = jnp.where(kind, viscosity * z_second[k], -z_first[k])
        return jnp.where(gap == k, value, total)

    z_matrix[...] = lax.fori_loop(0, cells_z, fill, jnp.zeros(shape, jnp.float32), unroll=8)


def stream_kernel(comps, field, x_first, x_second, after, x_part):
    length = field.shape[1]
    depth = field.shape[0] // comps
    u = field[...]
    lead = u[:depth]
    left = jnp.concatenate(
        [u, jnp.concatenate([lead * u[c * depth : (c + 1) * depth] for c in range(comps)], axis=0)], axis=1
    )
    right = jnp.concatenate(
        [viscosity * circulant_rows(x_second[...], length), -circulant_rows(x_first[...], length)], axis=1
    )
    x_part[...] = dot_split(left, right, transposed=True)


def wall_matrix_kernel(zloc, ends, others, metric_table, metric_index, y_first, y_second, after, matrix):
    cells = y_first.shape[0]
    depth = matrix.shape[0] // 2
    plain = functools.partial(
        lax.dot_general, dimension_numbers=(((1,), (0,)), ((), ())), preferred_element_type=jnp.float32
    )
    turned = functools.partial(
        lax.dot_general, dimension_numbers=(((1,), (1,)), ((), ())), preferred_element_type=jnp.float32
    )
    levels = metric_table.shape[1]
    entry = (lax.broadcasted_iota(jnp.int32, (levels, cells), 0) == metric_index[...]).astype(jnp.float32)
    table = jnp.broadcast_to(metric_table[...], (8, levels))
    metric = plain(table, entry, precision=lax.Precision.HIGHEST)[:1]
    scale = jnp.sum(ends[...] * metric, axis=1, keepdims=True)
    pick = ends[...].astype(jnp.bfloat16)
    second = sum(plain(pick, part) for part in halves(viscosity * y_second[...]))
    first = -scale * sum(plain(pick, part) for part in halves(y_first[...]))
    other = others[...].astype(jnp.bfloat16)
    wide = sum(turned(part, other) for part in halves(jnp.concatenate([second, first], axis=0)))
    match = lax.broadcasted_iota(jnp.int32, wide.shape, 0) % zloc == lax.broadcasted_iota(jnp.int32, wide.shape, 1) % zloc
    wide = jnp.where(match, wide, 0.0)
    for b in range(others.shape[0] // depth):
        for k in range(2):
            matrix[:, (2 * b + k) * depth : (2 * b + k + 1) * depth] = wide[
                2 * k * depth : 2 * (k + 1) * depth, b * depth : (b + 1) * depth
            ]


def wall_kernel(comps, matrix, z_part, *refs):
    fields, (total, away) = refs[:-2], refs[-2:]
    depth = z_part.shape[0] // comps
    for comp in range(comps):
        at = slice(comp * depth, (comp + 1) * depth)
        stack = []
        for field in fields:
            stack += [field[at], field[depth : 2 * depth] * field[at]]
        result = dot_split(matrix[...], jnp.concatenate(stack, axis=0))
        total[at] = z_part[at] + result[:depth]
        away[at] = result[depth:]


def sum_kernel(comps, mask, *refs):
    parts, out = refs[:-1], refs[-1]
    depth = mask.shape[0]
    for comp in range(comps):
        at = slice(comp * depth, (comp + 1) * depth)
        out[at] = jnp.where(mask[...] > 0, sum(part[at] for part in parts[1:]) + parts[0][at], 0.0)


def finish_kernel(total, near, out):
    out[...] = total[...] + near[...]


def call(kernel, operands, spaces, results, name, scratch=(), cost=None):
    results = [jax.ShapeDtypeStruct(shape, jnp.float32) for shape in results]
    held = sum(4 * math.prod(array.shape) for array in list(operands) + results)
    return pl.pallas_call(
        kernel,
        out_shape=results,
        in_specs=[pl.BlockSpec(memory_space=space) for space in spaces],
        out_specs=[pl.BlockSpec(memory_space=VMEM)] * len(results),
        scratch_shapes=[pltpu.VMEM(shape, jnp.float32) for shape in scratch],
        compiler_params=pltpu.CompilerParams(vmem_limit_bytes=(4 << 20) + 3 * held),
        cost_estimate=cost,
        name=name,
    )(*operands)


def local(
    velocity,
    wall_counts,
    x_first,
    x_second,
    y_first,
    y_second,
    z_first,
    z_second,
    metric_table,
    metric_index,
):
    rows = lax.axis_size("row")
    cols = lax.axis_size("col")
    comps, slots, zloc, length = velocity.shape
    depth = slots * zloc
    field = velocity.reshape(comps * depth, length)
    group = min(depth, 16)
    wide = cols // quad

    def along(value, step):
        return lax.ppermute(value, "col", [(i, i ^ step) for i in range(cols)])

    def across(value, step):
        return lax.ppermute(value, "row", [(i, i ^ step) for i in range(rows)])

    gathered = [along(field, t) for t in range(1, quad)]
    cells = metric_index.shape[0]
    z_matrix, mask, held, ends, others = call(
        functools.partial(span_matrix_kernel, rows, cols, zloc),
        [wall_counts, z_first, z_second, field],
        [SMEM] * 3 + [VMEM],
        [
            (wide * group, 2 * quad * group),
            (depth, length),
            field.shape,
            (2 * depth, cells),
            (rows // 2 * depth, cells),
        ],
        "span_matrix",
    )
    far = [across(held, step) for step in range(2, rows, 2)]
    (early,) = call(
        functools.partial(early_kernel, comps, (0, quad - 1)),
        [z_matrix, field, gathered[-1]],
        [VMEM] * 3,
        [(wide * group, comps * (depth // group) * length)],
        "early",
    )
    parts = call(
        functools.partial(span_kernel, comps, tuple(range(1, quad - 1))),
        [z_matrix, early] + gathered[:-1],
        [VMEM] * quad,
        [field.shape] * wide,
        "span",
    )
    returned = [
        lax.ppermute(
            parts[t],
            ("row", "col"),
            [(i * cols + j, i * cols + (j ^ over(t, i % 2))) for i in range(rows) for j in range(cols)],
        )
        for t in range(1, wide)
    ]
    (y_matrix,) = call(
        functools.partial(wall_matrix_kernel, zloc),
        [ends, others, metric_table.reshape(1, -1), metric_index.reshape(1, -1), y_first, y_second, parts[0]],
        [VMEM] * 6 + [pl.ANY],
        [(2 * depth, rows * depth)],
        "wall_matrix",
    )
    total, away = call(
        functools.partial(wall_kernel, comps),
        [y_matrix, parts[0], field] + far,
        [VMEM] * (3 + len(far)),
        [field.shape] * 2,
        "wall",
    )
    near = across(away, 1)
    (x_part,) = call(
        functools.partial(stream_kernel, comps),
        [field, x_first.reshape(1, length), x_second.reshape(1, length), away],
        [VMEM] * 3 + [pl.ANY],
        [field.shape],
        "stream",
    )
    (summed,) = call(
        functools.partial(sum_kernel, comps),
        [mask, total, x_part] + returned,
        [VMEM] * (3 + len(returned)),
        [field.shape],
        "sum",
        cost=pl.CostEstimate(flops=1 << 30, bytes_accessed=1 << 22, transcendentals=0),
    )
    (result,) = call(finish_kernel, [summed, near], [VMEM] * 2, [field.shape], "finish")
    return result.reshape(velocity.shape)


def solution(mesh):
    in_specs = (P(None, "row", "col", None), P(), P(), P(), P(), P(), P(), P(), P(), P())
    out_specs = P(None, "row", "col", None)
    return jax.shard_map(local, mesh=mesh, in_specs=in_specs, out_specs=out_specs, check_vma=False)
```

```python
import functools
import math

import jax
import jax.numpy as jnp
from jax import lax
from jax.experimental import pallas as pl
from jax.experimental.pallas import tpu as pltpu
from jax.sharding import PartitionSpec as P

viscosity = 0.4
quad = 4

VMEM = pltpu.VMEM
SMEM = pltpu.SMEM


def halves(value):
    high = value.astype(jnp.bfloat16)
    low = (value - high.astype(jnp.float32)).astype(jnp.bfloat16)
    return high, low


def dot_split(left, right, transposed=False):
    dims = (((1,), (1 if transposed else 0,)), ((), ()))
    mul = functools.partial(lax.dot_general, dimension_numbers=dims, preferred_element_type=jnp.float32)
    lh, ll = halves(left)
    rh, rl = halves(right)
    both = mul(jnp.concatenate([lh, ll], axis=0), rh)
    count = left.shape[0]
    return both[:count] + (mul(lh, rl) + both[count:])


def over(t, odd):
    return quad * t + (0 if odd else 2 * (t != 0))


def quad_sums(comps, matrix, fields, chosen):
    depth, length = fields[0].shape[0] // comps, fields[0].shape[1]
    half = matrix.shape[1] // 2
    group = half // quad
    left = jnp.concatenate(
        [matrix[:, start + s * group : start + (s + 1) * group] for start in (0, half) for s in chosen], axis=1
    )
    right = []
    for comp in range(comps):
        for at in range(0, depth, group):
            stack = [field[comp * depth + at : comp * depth + at + group] for field in fields]
            stack += [value * field[2 * depth + at : 2 * depth + at + group] for value, field in zip(stack, fields)]
            right.append(jnp.concatenate(stack, axis=0))
    return dot_split(left, jnp.concatenate(right, axis=1))


def early_kernel(comps, chosen, matrix, *refs):
    refs[-1][...] = quad_sums(comps, matrix, refs[:-1], chosen)


def span_kernel(comps, chosen, matrix, early, *refs):
    fields, parts = refs[: len(chosen)], refs[len(chosen) :]
    result = early[...] + quad_sums(comps, matrix, fields, chosen)
    rows, length = parts[0].shape
    count = len(parts)
    group = result.shape[0] // count
    for t in range(count):
        for i in range(rows // group):
            parts[t][i * group : (i + 1) * group] = result[
                t * group : (t + 1) * group, i * length : (i + 1) * length
            ]


def circulant_rows(row, length):
    return pltpu.roll(jnp.broadcast_to(row, (length, length)), 0, 1, stride=1, stride_axis=0)


def span_matrix_kernel(
    rows, cols, zloc, wall_counts, z_first, z_second, field, z_matrix, mask, held, ends, others
):
    held[...] = field[...]
    me = lax.axis_index("row")
    mask[...] = (lax.broadcasted_iota(jnp.int32, mask.shape, 0) // zloc < wall_counts[me]).astype(jnp.float32)
    depth = mask.shape[0]
    plane = lax.broadcasted_iota(jnp.int32, (depth, ends.shape[1]), 0) // zloc
    cell = lax.broadcasted_iota(jnp.int32, (depth, ends.shape[1]), 1)

    def spots(index):
        start = lax.fori_loop(0, rows, lambda i, acc: acc + jnp.where(i < index, wall_counts[i], 0), 0, unroll=True)
        return ((plane < wall_counts[index]) & (plane + start == cell)).astype(jnp.float32)

    for i in range(2):
        ends[i * depth : (i + 1) * depth] = spots(me ^ i)
    for i in range(rows // 2):
        others[i * depth : (i + 1) * depth] = spots(me ^ (2 * i))

    cells_z = cols * zloc
    shape = z_matrix.shape
    half = shape[1] // 2
    group = half // quad
    mine = lax.axis_index("col")
    r = lax.broadcasted_iota(jnp.int32, shape, 0)
    q = lax.broadcasted_iota(jnp.int32, shape, 1)
    q = jnp.where(q < half, q, q - half)
    odd = lax.axis_index("row") % 2
    out_cell = (jnp.where(odd == 1, over(r // group, 1), over(r // group, 0)) ^ mine) * zloc + r % zloc
    in_cell = ((q // group) ^ mine) * zloc + q % zloc
    same = (r % group) // zloc == (q % group) // zloc
    gap = jnp.where(same, (in_cell - out_cell + cells_z) % cells_z, -1)
    kind = lax.broadcasted_iota(jnp.int32, (1, shape[1]), 1) < half

    def fill(k, total):
        value = jnp.where(kind, viscosity * z_second[k], -z_first[k])
        return jnp.where(gap == k, value, total)

    z_matrix[...] = lax.fori_loop(0, cells_z, fill, jnp.zeros(shape, jnp.float32), unroll=8)


def stream_kernel(comps, field, x_first, x_second, after, x_part):
    length = field.shape[1]
    depth = field.shape[0] // comps
    u = field[...]
    lead = u[:depth]
    left = jnp.concatenate(
        [u, jnp.concatenate([lead * u[c * depth : (c + 1) * depth] for c in range(comps)], axis=0)], axis=1
    )
    right = jnp.concatenate(
        [viscosity * circulant_rows(x_second[...], length), -circulant_rows(x_first[...], length)], axis=1
    )
    x_part[...] = dot_split(left, right, transposed=True)


def wall_matrix_kernel(zloc, ends, others, metric_table, metric_index, y_first, y_second, after, matrix):
    cells = y_first.shape[0]
    depth = matrix.shape[0] // 2
    plain = functools.partial(
        lax.dot_general, dimension_numbers=(((1,), (0,)), ((), ())), preferred_element_type=jnp.float32
    )
    turned = functools.partial(
        lax.dot_general, dimension_numbers=(((1,), (1,)), ((), ())), preferred_element_type=jnp.float32
    )
    levels = metric_table.shape[1]
    entry = (lax.broadcasted_iota(jnp.int32, (levels, cells), 0) == metric_index[...]).astype(jnp.float32)
    table = jnp.broadcast_to(metric_table[...], (8, levels))
    metric = plain(table, entry, precision=lax.Precision.HIGHEST)[:1]
    scale = jnp.sum(ends[...] * metric, axis=1, keepdims=True)
    pick = ends[...].astype(jnp.bfloat16)
    second = sum(plain(pick, part) for part in halves(viscosity * y_second[...]))
    first = -scale * sum(plain(pick, part) for part in halves(y_first[...]))
    other = others[...].astype(jnp.bfloat16)
    wide = sum(turned(part, other) for part in halves(jnp.concatenate([second, first], axis=0)))
    match = lax.broadcasted_iota(jnp.int32, wide.shape, 0) % zloc == lax.broadcasted_iota(jnp.int32, wide.shape, 1) % zloc
    wide = jnp.where(match, wide, 0.0)
    for b in range(others.shape[0] // depth):
        for k in range(2):
            matrix[:, (2 * b + k) * depth : (2 * b + k + 1) * depth] = wide[
                2 * k * depth : 2 * (k + 1) * depth, b * depth : (b + 1) * depth
            ]


def wall_kernel(comps, matrix, z_part, *refs):
    fields, (total, away) = refs[:-2], refs[-2:]
    depth = z_part.shape[0] // comps
    for comp in range(comps):
        at = slice(comp * depth, (comp + 1) * depth)
        stack = []
        for field in fields:
            stack += [field[at], field[depth : 2 * depth] * field[at]]
        result = dot_split(matrix[...], jnp.concatenate(stack, axis=0))
        total[at] = z_part[at] + result[:depth]
        away[at] = result[depth:]


def sum_kernel(comps, mask, *refs):
    parts, out = refs[:-1], refs[-1]
    depth = mask.shape[0]
    for comp in range(comps):
        at = slice(comp * depth, (comp + 1) * depth)
        out[at] = jnp.where(mask[...] > 0, sum(part[at] for part in parts[1:]) + parts[0][at], 0.0)


def finish_kernel(total, near, out):
    out[...] = total[...] + near[...]


def call(kernel, operands, spaces, results, name, scratch=(), cost=None):
    results = [jax.ShapeDtypeStruct(shape, jnp.float32) for shape in results]
    held = sum(4 * math.prod(array.shape) for array in list(operands) + results)
    return pl.pallas_call(
        kernel,
        out_shape=results,
        in_specs=[pl.BlockSpec(memory_space=space) for space in spaces],
        out_specs=[pl.BlockSpec(memory_space=VMEM)] * len(results),
        scratch_shapes=[pltpu.VMEM(shape, jnp.float32) for shape in scratch],
        compiler_params=pltpu.CompilerParams(vmem_limit_bytes=(4 << 20) + 3 * held),
        cost_estimate=cost,
        name=name,
    )(*operands)


def local(
    velocity,
    wall_counts,
    x_first,
    x_second,
    y_first,
    y_second,
    z_first,
    z_second,
    metric_table,
    metric_index,
):
    rows = lax.axis_size("row")
    cols = lax.axis_size("col")
    comps, slots, zloc, length = velocity.shape
    depth = slots * zloc
    field = velocity.reshape(comps * depth, length)
    group = min(depth, 8)
    wide = cols // quad

    def along(value, step):
        return lax.ppermute(value, "col", [(i, i ^ step) for i in range(cols)])

    def across(value, step):
        return lax.ppermute(value, "row", [(i, i ^ step) for i in range(rows)])

    gathered = [along(field, t) for t in range(1, quad)]
    cells = metric_index.shape[0]
    z_matrix, mask, held, ends, others = call(
        functools.partial(span_matrix_kernel, rows, cols, zloc),
        [wall_counts, z_first, z_second, field],
        [SMEM] * 3 + [VMEM],
        [
            (wide * group, 2 * quad * group),
            (depth, length),
            field.shape,
            (2 * depth, cells),
            (rows // 2 * depth, cells),
        ],
        "span_matrix",
    )
    far = [across(held, step) for step in range(2, rows, 2)]
    (early,) = call(
        functools.partial(early_kernel, comps, (0, quad - 1)),
        [z_matrix, field, gathered[-1]],
        [VMEM] * 3,
        [(wide * group, comps * (depth // group) * length)],
        "early",
    )
    parts = call(
        functools.partial(span_kernel, comps, tuple(range(1, quad - 1))),
        [z_matrix, early] + gathered[:-1],
        [VMEM] * quad,
        [field.shape] * wide,
        "span",
    )
    returned = [
        lax.ppermute(
            parts[t],
            ("row", "col"),
            [(i * cols + j, i * cols + (j ^ over(t, i % 2))) for i in range(rows) for j in range(cols)],
        )
        for t in range(1, wide)
    ]
    (y_matrix,) = call(
        functools.partial(wall_matrix_kernel, zloc),
        [ends, others, metric_table.reshape(1, -1), metric_index.reshape(1, -1), y_first, y_second, parts[0]],
        [VMEM] * 6 + [pl.ANY],
        [(2 * depth, rows * depth)],
        "wall_matrix",
    )
    total, away = call(
        functools.partial(wall_kernel, comps),
        [y_matrix, parts[0], field] + far,
        [VMEM] * (3 + len(far)),
        [field.shape] * 2,
        "wall",
    )
    near = across(away, 1)
    (x_part,) = call(
        functools.partial(stream_kernel, comps),
        [field, x_first.reshape(1, length), x_second.reshape(1, length), away],
        [VMEM] * 3 + [pl.ANY],
        [field.shape],
        "stream",
    )
    (summed,) = call(
        functools.partial(sum_kernel, comps),
        [mask, total, x_part] + returned,
        [VMEM] * (3 + len(returned)),
        [field.shape],
        "sum",
        cost=pl.CostEstimate(flops=1 << 30, bytes_accessed=1 << 22, transcendentals=0),
    )
    (result,) = call(finish_kernel, [summed, near], [VMEM] * 2, [field.shape], "finish")
    return result.reshape(velocity.shape)


def solution(mesh):
    in_specs = (P(None, "row", "col", None), P(), P(), P(), P(), P(), P(), P(), P(), P())
    out_specs = P(None, "row", "col", None)
    return jax.shard_map(local, mesh=mesh, in_specs=in_specs, out_specs=out_specs, check_vma=False)
```
